128 devices in a mesh: ctx: 16 (over y, x_hi, core), tp: 8 (over z, x_lo).
Axes of the slice: x: 4 (x_hi: 2, x_lo: 2; x = x_hi * 2 + x_lo), y: 4, z: 4, core: 2. Of those that a mesh axis runs over, the one named last changes fastest.
Arguments:
- hidden_in: bfloat16 [8192, 4096], P(('ctx', 'tp')), may hold values from -24 to 24
- cotangent: bfloat16 [8192, 4096], P(('ctx', 'tp')), may hold values from -24 to 24
- norm_gain: float32 [4096], replicated, may hold values from 0.1 to 1.9
- in_weight: bfloat16 [4096, 3, 4096], P(None, None, 'tp'), may hold values from -0.09375 to 0.09375
- filter_taps: float32 [3, 3, 4096], P(None, None, 'tp'), may hold values from -3 to 3
- inner_taps: float32 [7, 4096], P(None, 'tp'), may hold values from -3 to 3
- out_weight: bfloat16 [4096, 4096], P('tp'), may hold values from -0.09375 to 0.09375
Outputs:
- layer_out: bfloat16 [8192, 4096], P(('ctx', 'tp'))
- grad_input: bfloat16 [8192, 4096], P(('ctx', 'tp'))
- grad_in_weight: bfloat16 [4096, 3, 4096], P('ctx', None, 'tp')
- grad_out_weight: bfloat16 [4096, 4096], P('tp', 'ctx')
- grad_filter: float32 [3, 3, 4096], P(None, None, 'tp')
- grad_inner: float32 [7, 4096], P(None, 'tp')
The draws below stay inside these ranges and needn't reach their ends.
All inputs are finite; a program needn't handle non-finite values.
Results may differ from the reference program's by a relative error of at most 0.025.
Values may be sent and summed in bfloat16 or wider, within the bound.
A program may use at most 192 MiB of HBM per device.

```python
import jax
import jax.numpy as jnp
from jax import lax

D = 4096
SHORT = 3
TAPS = 7
BLOCK = 512
TOKENS = 8192
N_CTX = 16
N_TP = 8


def raised(values, own_key, source, target, parts, factor):
    owner, partner = [(jnp.arange(values.shape[axis_at]) // (values.shape[axis_at] // parts)).reshape([-1 if axis == axis_at else 1 for axis in range(values.ndim)]) for axis_at in (source, target)]
    chosen = jax.random.permutation(own_key, parts)[partner]
    strong = (owner == chosen) | (owner == (partner + parts // 2) % parts)
    return jnp.where(strong, factor * values, values)


def steps_of(key, shape, split, smallest, high):
    def one(dim, shards_of):
        draws = jax.random.uniform(jax.random.fold_in(jax.random.fold_in(key, 6), dim), (shards_of,), jnp.float32, smallest / len(split), high / len(split))
        return jnp.repeat(jnp.exp(draws), shape[dim] // shards_of).reshape((-1,) + (1,) * (len(shape) - dim - 1))

    factor_of = one(*split[0])
    for cut in split[1:]:
        factor_of = factor_of * one(*cut)
    return factor_of


def bell_draw(key, extent, spread, limit, split=(), kind=jnp.bfloat16):
    factor_of = steps_of(key, extent, split, -0.22, 0.18) if split else 1.0
    entries = jax.random.normal(key, extent, jnp.float32) * spread * factor_of
    return jnp.minimum(jnp.maximum(entries, -limit), limit).astype(kind)


def bell_draw_with(rng, extent, spread, limit, split, heavy, held_as=jnp.bfloat16):
    entries = spread * jax.random.normal(rng, extent, jnp.float32)
    if split:
        entries = entries * steps_of(rng, extent, split, -0.22, 0.18)
    return jnp.clip(raised(entries, jax.random.fold_in(rng, 3), *heavy), -limit, limit).astype(held_as)


def setup_inputs(seed: int = 0) -> dict:
    splits = jax.random.split(jax.random.key(seed), 8)
    hidden_in = bell_draw_with(splits[0], (TOKENS, D), 1.0, 24.0, ((0, 128),), (0, 1, 128, 5.5))
    cotangent = bell_draw_with(splits[1], (TOKENS, D), 1.0, 24.0, ((0, 128),), (0, 1, 128, 5.5))
    norm_gain = jnp.clip(1.0 + 0.18 * jax.random.normal(splits[2], (D,), jnp.float32), 0.1, 1.9)
    in_weight = bell_draw(splits[3], (D, 3, D), D ** -0.5, 0.09375, ((2, 8),))
    filter_taps = bell_draw(splits[4], (SHORT, 3, D), 0.6, 3.0, ((2, 8),), jnp.float32)
    inner_taps = bell_draw(splits[5], (TAPS, D), 0.4, 3.0, ((1, 8),), jnp.float32)
    out_weight = bell_draw(splits[6], (D, D), D ** -0.5, 0.09375, ((0, 8),))
    return dict(hidden_in=hidden_in, cotangent=cotangent, norm_gain=norm_gain, in_weight=in_weight, filter_taps=filter_taps, inner_taps=inner_taps, out_weight=out_weight)


def normed(values, gain):
    floats = values.astype(jnp.float32)
    factor = lax.rsqrt(lax.optimization_barrier(jnp.mean(floats * floats, axis=-1, keepdims=True)) + 1e-05)
    return floats * factor * gain

def causal(series, taps):
    count = taps.shape[0]
    length_all = series.shape[0]
    padded = jnp.concatenate([jnp.zeros((count - 1,) + series.shape[1:], jnp.float32), series.astype(jnp.float32)])
    summed = jnp.zeros(series.shape, jnp.float32)
    for tap_index in range(count):
        begin = count - 1 - tap_index
        summed = summed + taps[tap_index] * padded[begin:begin + length_all]
    return summed

def ahead(series, taps):
    count = taps.shape[0]
    length_all = series.shape[0]
    padded = jnp.concatenate([series.astype(jnp.float32), jnp.zeros((count - 1,) + series.shape[1:], jnp.float32)])
    summed = jnp.zeros(series.shape, jnp.float32)
    for tap_index in range(count):
        summed = summed + taps[tap_index] * padded[tap_index:tap_index + length_all]
    return summed

def lagged_sums(grads, series, count):
    length_all = series.shape[0]
    padded = jnp.concatenate([jnp.zeros((count - 1,) + series.shape[1:], jnp.float32), series.astype(jnp.float32)])
    pieces = []
    for tap_index in range(count):
        begin = count - 1 - tap_index
        pieces.append(lax.optimization_barrier(jnp.sum(grads * padded[begin:begin + length_all], axis=0)))
    return jnp.stack(pieces)

def rounded(values):
    return lax.optimization_barrier(values.astype(jnp.bfloat16)).astype(jnp.float32)

def reference(hidden_in, cotangent, norm_gain, in_weight, filter_taps, inner_taps, out_weight):
    length_all = hidden_in.shape[0]
    chans = D // N_TP
    loss_scale = TOKENS ** (-0.5)
    normal_rows = normed(hidden_in, norm_gain).astype(jnp.bfloat16)
    flat_in = in_weight.reshape(D, 3 * D)
    projected = jnp.dot(normal_rows, flat_in, preferred_element_type=jnp.float32).astype(jnp.bfloat16).reshape(length_all, 3, D)
    features = causal(projected, filter_taps)
    query_vals, key_vals, value_vals = (features[:, 0], features[:, 1], features[:, 2])
    products = key_vals * value_vals
    gate_vals = causal(products, inner_taps)
    mixed = (query_vals * gate_vals).astype(jnp.bfloat16)
    branch = jnp.zeros((length_all, D), jnp.float32)
    for group_index in range(N_TP):
        window = slice(group_index * chans, (group_index + 1) * chans)
        branch = branch + rounded(jnp.dot(mixed[:, window], out_weight[window], preferred_element_type=jnp.float32))
    layer_out = (hidden_in.astype(jnp.float32) + branch).astype(jnp.bfloat16)
    grad_mixed = jnp.dot(cotangent, out_weight.T, preferred_element_type=jnp.float32)
    grad_query = grad_mixed * gate_vals
    grad_gates = grad_mixed * query_vals
    grad_products = ahead(grad_gates, inner_taps)
    grad_features = jnp.stack([grad_query, grad_products * value_vals, grad_products * key_vals], axis=1)
    grad_proj = ahead(grad_features, filter_taps).astype(jnp.bfloat16)
    grad_normed = jnp.zeros((length_all, D), jnp.float32)
    for group_index in range(N_TP):
        window = slice(group_index * chans, (group_index + 1) * chans)
        rows_part = grad_proj[:, :, window].reshape(length_all, 3 * chans)
        weight_part = in_weight[:, :, window].reshape(D, 3 * chans)
        grad_normed = grad_normed + rounded(jnp.dot(rows_part, weight_part.T, preferred_element_type=jnp.float32))
    _, pullback = jax.vjp(lambda values: normed(values, norm_gain), hidden_in.astype(jnp.float32))
    grad_input = (cotangent.astype(jnp.float32) + pullback(grad_normed)[0]).astype(jnp.bfloat16)
    flat_grad = grad_proj.reshape(length_all, 3 * D)
    grad_in_sum = jnp.zeros((D, 3 * D), jnp.float32)
    grad_out_sum = jnp.zeros((D, D), jnp.float32)
    for block_index in range(N_CTX):
        window = slice(block_index * BLOCK, (block_index + 1) * BLOCK)
        grad_in_sum = grad_in_sum + rounded(jnp.dot(normal_rows[window].T, flat_grad[window], preferred_element_type=jnp.float32) * loss_scale)
        grad_out_sum = grad_out_sum + rounded(jnp.dot(mixed[window].T, cotangent[window], preferred_element_type=jnp.float32) * loss_scale)
    grad_in_weight = grad_in_sum.astype(jnp.bfloat16).reshape(D, 3, D)
    grad_out_weight = grad_out_sum.astype(jnp.bfloat16)
    grad_filter = lagged_sums(grad_features, projected, SHORT) * loss_scale
    grad_inner = lagged_sums(grad_gates, products, TAPS) * loss_scale
    return (layer_out, grad_input, grad_in_weight, grad_out_weight, grad_filter, grad_inner)
```

```python
import jax
import jax.numpy as jnp
from jax import lax
from jax.experimental import pallas as pl
from jax.experimental.pallas import tpu as pltpu
from jax.sharding import PartitionSpec as P

MESH = pl.DeviceIdType.MESH
DELTAS = (2, 1, 3, 0)


def passed_along(value, axis, steps):
    count = lax.axis_size(axis)
    first, last = (max(0, -steps), min(count, count - steps))
    return lax.ppermute(value, axis, [(source, source + steps) for source in range(first, last)])


def normed(values, gain):
    floats = values.astype(jnp.float32)
    factor = lax.rsqrt(jnp.mean(floats * floats, axis=-1, keepdims=True) + 1e-05)
    return floats * factor * gain


def taps_causal(extended, taps, number):
    count = taps.shape[0]
    summed = jnp.zeros((number,) + extended.shape[1:], jnp.float32)
    for tap_index in range(count):
        begin = count - 1 - tap_index
        summed = summed + taps[tap_index] * extended[begin : begin + number]
    return summed


def taps_ahead(extended, taps, number):
    count = taps.shape[0]
    summed = jnp.zeros((number,) + extended.shape[1:], jnp.float32)
    for tap_index in range(count):
        summed = summed + taps[tap_index] * extended[tap_index : tap_index + number]
    return summed


def lagged_sums(grads, extended, number, count):
    pieces = []
    for tap_index in range(count):
        begin = count - 1 - tap_index
        pieces.append(jnp.sum(grads * extended[begin : begin + number], axis=0))
    return jnp.stack(pieces)


class Place:
    def __init__(self):
        ctx, tp = lax.axis_index("ctx"), lax.axis_index("tp")
        self.y, self.x_hi, self.core = ctx // 4, (ctx // 2) % 2, ctx % 2
        self.z, self.x_lo = tp // 2, tp % 2
        self.ctx, self.tp = ctx, tp

    def sibling(self):
        return (self.y * 4 + self.x_hi * 2 + 1 - self.core, self.tp)

    def along_y(self, step):
        return (((self.y + step) % 4) * 4 + self.x_hi * 2 + self.core, self.tp)

    def along_z(self, step):
        return (self.ctx, ((self.z + step) % 4) * 2 + self.x_lo)

    def along_x(self, step):
        x = (self.x_hi * 2 + self.x_lo + step) % 4
        return (self.y * 4 + (x // 2) * 2 + self.core, self.z * 2 + x % 2)

    def partner(self):
        return (self.ctx, self.z * 2 + 1 - self.x_lo)

    def block(self, step, same):
        x_lo = self.x_lo if same else 1 - self.x_lo
        return ((self.z + step) % 4) * 2 + x_lo


def remote(source, target, send, recv, device):
    return pltpu.make_async_remote_copy(
        src_ref=source, dst_ref=target, send_sem=send, recv_sem=recv, device_id=device, device_id_type=MESH
    )


def greet(devices):
    barrier = pltpu.get_barrier_semaphore()
    for device in devices:
        pl.semaphore_signal(barrier, inc=1, device_id=device, device_id_type=MESH)
    pl.semaphore_wait(barrier, len(devices))


def tile(index, size):
    return pl.ds(pl.multiple_of(index * size, size), size)


def reduce_kernel(
    scale,
    acts_hbm, turned_hbm, in_w_hbm, out_w_hbm, norm_hbm, cot_hbm,
    branch_ref, gnorm_ref, shard_ref,
    acts, turned, in_w, out_w, norms, cots,
    sib_out, sums, y_in, x_pass, x_in, parts, tp_in,
    load_sem, in_w_sem, col_sem, sib_send, sib_recv, y_send, y_recv, x_send, x_recv, tp_send, tp_recv,
):
    here = Place()
    tokens, width = norm_hbm.shape
    chans = out_w_hbm.shape[0]
    cut = width // 16
    rows_all = turned_hbm.shape[0]
    half = rows_all // 2
    block = tokens // 8
    upper, lower = pl.ds(0, half), pl.ds(half, half)
    step_in = in_w.shape[2]
    steps_in = width // step_in

    def target(index, core):
        y = (here.y + DELTAS[index % 4]) % 4
        x_hi = 1 - here.x_hi if index < 4 else here.x_hi
        return y * 4 + x_hi * 2 + core

    order = []
    for index in range(8):
        order.append(target(index, 1 - here.core))
        order.append(target(index, here.core))

    def loads(position):
        cols = tile(order[position], cut)
        return (
            pltpu.make_async_copy(norm_hbm.at[:, cols], norms.at[:, cols], col_sem.at[0, position]),
            pltpu.make_async_copy(cot_hbm.at[:, cols], cots.at[:, cols], col_sem.at[1, position]),
        )

    def in_load(step, slot):
        return pltpu.make_async_copy(in_w_hbm.at[:, tile(step, step_in), :], in_w.at[slot], in_w_sem.at[slot])

    turned_load = pltpu.make_async_copy(turned_hbm, turned, load_sem.at[0])
    acts_load = pltpu.make_async_copy(acts_hbm, acts, load_sem.at[1])
    out_load = pltpu.make_async_copy(out_w_hbm, out_w, load_sem.at[2])
    turned_load.start()
    for copy in loads(0) + loads(1) + loads(2):
        copy.start()
    acts_load.start()
    out_load.start()
    for position in range(3, 16):
        for copy in loads(position):
            copy.start()
    in_load(0, 0).start()
    in_load(1, 1).start()

    greet(
        [here.sibling(), here.along_y(1), here.along_y(-1), here.along_z(1), here.along_z(-1),
         here.along_x(1), here.along_x(-1)]
    )
    sends = []

    def go(copy):
        copy.start()
        sends.append(copy)

    def product(position, write):
        for copy in loads(position):
            copy.wait()
        cols = tile(order[position], cut)

        def one(index, source):
            rows = tile(index, chans)
            value = jnp.dot(turned[rows, :], source[:, cols], preferred_element_type=jnp.float32)
            write(rows, value * scale)

        def loop(index, carry):
            one(index, norms)
            return carry

        lax.fori_loop(0, rows_all // chans - 1, loop, 0)
        one(rows_all // chans - 1, cots)

    def sib_copy(index):
        slot = index % 4
        return remote(sib_out.at[slot], sums.at[index], sib_send.at[index], sib_recv.at[index], here.sibling())

    def for_sibling(index):
        if index >= 4:
            sib_copy(index - 4).wait_send()

        def write(rows, value):
            sib_out[index % 4, rows, :] = value.astype(jnp.bfloat16)

        product(2 * index, write)
        sib_copy(index).start()

    def for_self(index):
        sib_copy(index).wait_recv()

        def write(rows, value):
            held = sums[index, rows, :].astype(jnp.float32)
            sums[index, rows, :] = (held + value).astype(jnp.bfloat16)

        product(2 * index + 1, write)

    def y_copy(group, slot):
        index, rows, step = (
            (0, upper, 1), (0, lower, -1), (1, lower, 1), (2, upper, -1), (1, upper, 1), (2, lower, -1)
        )[slot]
        return remote(
            sums.at[group * 4 + index, rows], y_in.at[group, slot],
            y_send.at[group, slot], y_recv.at[group, slot], here.along_y(step),
        )

    def add_rows(ref, base, length, others, size=128):
        def loop(index, carry):
            at = tile(index, size)
            rows = pl.ds(pl.multiple_of(base + index * size, size), size)
            total = ref[rows, :].astype(jnp.float32)
            for other in others:
                total = total + other[at, :].astype(jnp.float32)
            ref[rows, :] = total.astype(jnp.bfloat16)
            return carry

        lax.fori_loop(0, length // size, loop, 0)

    def y_pass(group):
        y_copy(group, 0).wait_recv()
        add_rows(sums.at[group * 4 + 1], 0, half, [y_in.at[group, 0]])
        go(y_copy(group, 4))
        y_copy(group, 1).wait_recv()
        add_rows(sums.at[group * 4 + 2], half, half, [y_in.at[group, 1]])
        go(y_copy(group, 5))

    def y_done(group):
        for slot in (3, 4, 2, 5):
            y_copy(group, slot).wait_recv()

    def x_copy(side):
        rows, step = ((upper, 1), (lower, -1))[side]
        return remote(sums.at[3, rows], x_pass.at[side], x_send.at[side], x_recv.at[side], here.along_x(step))

    def x_forward(side):
        return remote(
            x_pass.at[side], x_in.at[side], x_send.at[2 + side], x_recv.at[2 + side], here.along_x((1, -1)[side])
        )

    quarter = block // 2

    def tp_copy(which, slot):
        part, held = parts.at[which], tp_in.at[which]
        source, place, device = (
            lambda: (part.at[tile(here.block(2, False), block)], held.at[0], here.partner()),
            lambda: (part.at[tile(here.block(1, False), block)], held.at[1], here.along_z(1)),
            lambda: (part.at[tile(here.block(-1, False), block)], held.at[2], here.along_z(-1)),
            lambda: (
                part.at[pl.ds(pl.multiple_of(here.block(2, True) * block, block), quarter)],
                held.at[3, pl.ds(0, quarter)], here.along_z(1)),
            lambda: (
                part.at[pl.ds(pl.multiple_of(here.block(2, True) * block + quarter, quarter), quarter)],
                held.at[3, pl.ds(quarter, quarter)], here.along_z(-1)),
            lambda: (part.at[tile(here.block(1, True), block)], held.at[4], here.along_z(1)),
            lambda: (part.at[tile(here.block(-1, True), block)], held.at[5], here.along_z(-1)),
            lambda: (part.at[tile(here.block(0, False), block)], held.at[6], here.partner()),
        )[slot]()
        return remote(source, place, tp_send.at[which, slot], tp_recv.at[which, slot], device)

    def tp_begin(which):
        for slot in range(3):
            go(tp_copy(which, slot))

    def tp_halves(which):
        tp_copy(which, 0).wait_recv()
        add_rows(parts.at[which], here.block(2, True) * block, block, [tp_in.at[which, 0]], 16)
        go(tp_copy(which, 3))
        go(tp_copy(which, 4))

    def tp_direct(which):
        tp_copy(which, 3).wait_recv()
        add_rows(parts.at[which], here.block(1, True) * block, quarter, [tp_in.at[which, 3, pl.ds(0, quarter)]], 16)
        go(tp_copy(which, 5))
        tp_copy(which, 4).wait_recv()
        add_rows(
            parts.at[which], here.block(-1, True) * block + quarter, quarter,
            [tp_in.at[which, 3, pl.ds(quarter, quarter)]], 16)
        go(tp_copy(which, 6))

    def tp_last(which):
        tp_copy(which, 1).wait_recv()
        tp_copy(which, 2).wait_recv()
        add_rows(parts.at[which], here.block(0, False) * block, block, [tp_in.at[which, 1], tp_in.at[which, 2]], 16)
        go(tp_copy(which, 7))

    def tp_finish(which, result):
        for slot in (5, 6, 7):
            tp_copy(which, slot).wait_recv()

        def loop(index, carry):
            at = tile(index, 16)
            rows = pl.ds(pl.multiple_of(here.tp * block + index * 16, 16), 16)
            total = parts[which, rows, :].astype(jnp.float32)
            for slot in (4, 5, 6):
                total = total + tp_in[which, slot, at, :].astype(jnp.float32)
            result[at, :] = total
            return carry

        lax.fori_loop(0, block // 16, loop, 0)

    def branch_product():
        def loop(index, carry):
            cols = tile(index, chans)
            value = jnp.dot(
                acts[:, pl.ds(3 * chans, chans)], out_w[:, cols], preferred_element_type=jnp.float32
            )
            parts[0, :, cols] = value.astype(jnp.bfloat16)
            return carry

        lax.fori_loop(0, width // chans, loop, 0)

    def gnorm_product():
        def loop(step, carry):
            slot = step % 2
            in_load(step, slot).wait()

            def inner(index, carry):
                rows = tile(index, tokens // 2)
                value = jnp.zeros((tokens // 2, step_in), jnp.float32)
                for kind in range(3):
                    value = value + lax.dot_general(
                        acts[rows, pl.ds(kind * chans, chans)], in_w[slot, kind],
                        (((1,), (1,)), ((), ())), preferred_element_type=jnp.float32,
                    )
                parts[1, rows, tile(step, step_in)] = value.astype(jnp.bfloat16)
                return carry

            lax.fori_loop(0, 2, inner, 0)

            @pl.when(step + 2 < steps_in)
            def _():
                in_load(step + 2, slot).start()

            return carry

        lax.fori_loop(0, steps_in, loop, 0)

    turned_load.wait()
    for_sibling(0)
    for_sibling(1)
    for_self(0)
    go(y_copy(0, 0))
    go(y_copy(0, 1))
    acts_load.wait()
    out_load.wait()
    branch_product()
    tp_begin(0)
    for_sibling(2)
    for_self(1)
    go(y_copy(0, 2))
    for_sibling(3)
    for_self(2)
    go(y_copy(0, 3))
    for_sibling(4)
    for_self(3)
    tp_halves(0)
    gnorm_product()
    tp_begin(1)
    y_pass(0)
    for_sibling(5)
    for_self(4)
    go(y_copy(1, 0))
    go(y_copy(1, 1))
    for_sibling(6)
    for_self(5)
    go(y_copy(1, 2))
    for_sibling(7)
    for_self(6)
    go(y_copy(1, 3))
    for_self(7)
    tp_direct(0)
    tp_last(0)
    y_done(0)
    add_rows(sums.at[3], 0, half, [y_in.at[0, 3], y_in.at[0, 4]])
    go(x_copy(0))
    add_rows(sums.at[3], half, half, [y_in.at[0, 2], y_in.at[0, 5]])
    go(x_copy(1))
    tp_halves(1)
    y_pass(1)
    tp_direct(1)
    tp_last(1)
    for side in range(2):
        x_copy(side).wait_recv()
        go(x_forward(side))
    tp_finish(0, branch_ref)
    tp_finish(1, gnorm_ref)
    x_forward(0).wait_recv()
    x_forward(1).wait_recv()
    y_done(1)

    def last(begin, others):
        def loop(index, carry):
            at = tile(index, 128)
            rows = pl.ds(pl.multiple_of(begin + index * 128, 128), 128)
            total = sums[7, rows, :].astype(jnp.float32)
            for other in others:
                total = total + other[at, :].astype(jnp.float32)
            shard_ref[rows, :] = total.astype(jnp.bfloat16)
            return carry

        lax.fori_loop(0, half // 128, loop, 0)

    last(0, [y_in.at[1, 3], y_in.at[1, 4], x_in.at[0]])
    last(half, [y_in.at[1, 2], y_in.at[1, 5], x_in.at[1]])
    for index in range(4, 8):
        sib_copy(index).wait_send()
    for copy in sends:
        copy.wait_send()


def reduced(acts, turned, in_weight, out_weight, norms, cots, scale):
    tokens, width = norms.shape
    chans = out_weight.shape[0]
    rows_all = turned.shape[0]
    cut = width // 16
    block = tokens // 8
    half = rows_all // 2
    any_space = pl.BlockSpec(memory_space=pl.ANY)
    vmem_space = pl.BlockSpec(memory_space=pltpu.VMEM)
    bf16 = jnp.bfloat16
    dma = pltpu.SemaphoreType.DMA
    body = lambda *refs: reduce_kernel(scale, *refs)
    return pl.pallas_call(
        body,
        out_shape=(
            jax.ShapeDtypeStruct((block, width), jnp.float32),
            jax.ShapeDtypeStruct((block, width), jnp.float32),
            jax.ShapeDtypeStruct((rows_all, cut), bf16),
        ),
        in_specs=[any_space] * 6,
        out_specs=(vmem_space, vmem_space, vmem_space),
        scratch_shapes=[
            pltpu.VMEM(acts.shape, bf16),
            pltpu.VMEM(turned.shape, bf16),
            pltpu.VMEM((2, 3, 512, chans), bf16),
            pltpu.VMEM(out_weight.shape, bf16),
            pltpu.VMEM(norms.shape, bf16),
            pltpu.VMEM(cots.shape, bf16),
            pltpu.VMEM((4, rows_all, cut), bf16),
            pltpu.VMEM((8, rows_all, cut), bf16),
            pltpu.VMEM((2, 6, half, cut), bf16),
            pltpu.VMEM((2, half, cut), bf16),
            pltpu.VMEM((2, half, cut), bf16),
            pltpu.VMEM((2, tokens, width), bf16),
            pltpu.VMEM((2, 7, block, width), bf16),
            dma((3,)), dma((2,)), dma((2, 16)),
            dma((8,)), dma((8,)), dma((2, 6)), dma((2, 6)), dma((4,)), dma((4,)), dma((2, 8)), dma((2, 8)),
        ],
        compiler_params=pltpu.CompilerParams(
            collective_id=0, has_side_effects=True, vmem_limit_bytes=63 * 2**20
        ),
        name="reduce_all",
    )(acts, turned, in_weight, out_weight, norms, cots)


def local(hidden_in, cotangent, norm_gain, in_weight, filter_taps, inner_taps, out_weight):
    rows_local = hidden_in.shape[0]
    model_width = hidden_in.shape[1]
    channels = in_weight.shape[2]
    block_rows = rows_local * lax.axis_size("tp")
    loss_scale = (block_rows * lax.axis_size("ctx")) ** (-0.5)
    short_edge = filter_taps.shape[0] - 1
    inner_edge = inner_taps.shape[0] - 1
    reach = short_edge + inner_edge
    normal_rows = normed(hidden_in, norm_gain).astype(jnp.bfloat16)
    flat_in = in_weight.reshape(model_width, 3 * channels)
    gathered = lax.all_gather(normal_rows, "tp", axis=0, tiled=True)
    projected = jnp.dot(gathered, flat_in, preferred_element_type=jnp.float32).astype(jnp.bfloat16)
    projected = projected.reshape(block_rows, 3, channels)
    earlier = passed_along(projected[block_rows - reach :], "ctx", 1)
    blended = taps_causal(
        jnp.concatenate([earlier, projected]), filter_taps, block_rows + inner_edge
    )
    features = blended[inner_edge:]
    before = blended[:inner_edge, 1] * blended[:inner_edge, 2]
    shifted_in = jnp.concatenate([earlier[inner_edge:], projected])
    query_vals = features[:, 0]
    key_vals = features[:, 1]
    value_vals = features[:, 2]
    wide_prods = jnp.concatenate([before, key_vals * value_vals])
    gate_vals = taps_causal(wide_prods, inner_taps, block_rows)
    mixed = (query_vals * gate_vals).astype(jnp.bfloat16)
    grad_all = lax.all_gather(cotangent, "tp", axis=0, tiled=True)
    grad_mixed = lax.dot_general(
        grad_all, out_weight, (((1,), (1,)), ((), ())), preferred_element_type=jnp.float32
    )
    grad_query = grad_mixed * gate_vals
    grad_gates = grad_mixed * query_vals
    head_prod = taps_ahead(grad_gates[:reach], inner_taps, short_edge)
    head_feat = jnp.stack(
        [
            grad_query[:short_edge],
            head_prod * value_vals[:short_edge],
            head_prod * key_vals[:short_edge],
        ],
        axis=1,
    )
    next_gates, next_feat = passed_along((grad_gates[:inner_edge], head_feat), "ctx", -1)
    grad_products = taps_ahead(jnp.concatenate([grad_gates, next_gates]), inner_taps, block_rows)
    grad_features = jnp.stack(
        [grad_query, grad_products * value_vals, grad_products * key_vals], axis=1
    )
    filter_part = lagged_sums(grad_features, shifted_in, block_rows, short_edge + 1) * loss_scale
    inner_part = lagged_sums(grad_gates, wide_prods, block_rows, inner_edge + 1) * loss_scale
    grad_filter, grad_inner = (
        lax.psum(filter_part.astype(jnp.bfloat16), "ctx").astype(jnp.float32),
        lax.psum(inner_part.astype(jnp.bfloat16), "ctx").astype(jnp.float32),
    )
    grad_proj = taps_ahead(
        jnp.concatenate([grad_features, next_feat]), filter_taps, block_rows
    ).astype(jnp.bfloat16)
    acts = jnp.concatenate([grad_proj.reshape(block_rows, 3 * channels), mixed], axis=1)
    branch, grad_normed, shard = reduced(
        acts, acts.T, jnp.transpose(in_weight, (1, 0, 2)), out_weight, gathered, grad_all, loss_scale
    )
    layer_out = (hidden_in.astype(jnp.float32) + branch).astype(jnp.bfloat16)
    _, pullback = jax.vjp(lambda values: normed(values, norm_gain), hidden_in.astype(jnp.float32))
    grad_input = (cotangent.astype(jnp.float32) + pullback(grad_normed)[0]).astype(jnp.bfloat16)
    cut = shard.shape[1]
    grad_in_weight = jnp.transpose(shard[: 3 * channels].reshape(3, channels, cut), (2, 0, 1))
    grad_out_weight = shard[3 * channels :]
    return (layer_out, grad_input, grad_in_weight, grad_out_weight, grad_filter, grad_inner)


def solution(mesh):
    placed = (
        P(("ctx", "tp"), None),
        P(("ctx", "tp"), None),
        P(),
        P(None, None, "tp"),
        P(None, None, "tp"),
        P(None, "tp"),
        P("tp", None),
    )
    return jax.shard_map(
        local,
        mesh=mesh,
        in_specs=placed,
        out_specs=(
            P(("ctx", "tp"), None),
            P(("ctx", "tp"), None),
            P("ctx", None, "tp"),
            P("tp", "ctx"),
            P(None, None, "tp"),
            P(None, "tp"),
        ),
        check_vma=False,
    )
```

```python
import jax
import jax.numpy as jnp
from jax import lax
from jax.experimental import pallas as pl
from jax.experimental.pallas import tpu as pltpu
from jax.sharding import PartitionSpec as P

MESH = pl.DeviceIdType.MESH
DELTAS = (2, 1, 3, 0)


class Place:
    def __init__(self):
        ctx, tp = lax.axis_index("ctx"), lax.axis_index("tp")
        self.y, self.x_hi, self.core = ctx // 4, (ctx // 2) % 2, ctx % 2
        self.z, self.x_lo = tp // 2, tp % 2
        self.ctx, self.tp = ctx, tp

    def sibling(self):
        return (self.y * 4 + self.x_hi * 2 + 1 - self.core, self.tp)

    def along_y(self, step):
        return (((self.y + step) % 4) * 4 + self.x_hi * 2 + self.core, self.tp)

    def along_z(self, step):
        return (self.ctx, ((self.z + step) % 4) * 2 + self.x_lo)

    def along_x(self, step):
        x = (self.x_hi * 2 + self.x_lo + step) % 4
        return (self.y * 4 + (x // 2) * 2 + self.core, self.z * 2 + x % 2)

    def along_ctx(self, step):
        return ((self.ctx + step) % 16, self.tp)

    def partner(self):
        return (self.ctx, self.z * 2 + 1 - self.x_lo)

    def block(self, step, same):
        x_lo = self.x_lo if same else 1 - self.x_lo
        return ((self.z + step) % 4) * 2 + x_lo


def remote(source, target, send, recv, device):
    return pltpu.make_async_remote_copy(
        src_ref=source, dst_ref=target, send_sem=send, recv_sem=recv, device_id=device, device_id_type=MESH
    )


def greet(devices):
    barrier = pltpu.get_barrier_semaphore()
    for device in devices:
        pl.semaphore_signal(barrier, inc=1, device_id=device, device_id_type=MESH)
    pl.semaphore_wait(barrier, len(devices))


def tile(index, size):
    return pl.ds(pl.multiple_of(index * size, size), size)


def gather_kernel(
    scale, tokens,
    hidden, cot, gain, taps, in_w_hbm, out_w_hbm,
    norm_out, cot_out, acts, turned, lag_out,
    both, in_w, out_w, proj, query, gates, grads, prods, lags,
    load_sem, send_sem, recv_sem, edge_send, edge_recv, out_sem,
):
    here = Place()
    block, width = hidden.shape
    chans = out_w_hbm.shape[0]
    half = block // 2
    group = 2 * block
    wide, span = 72, 64
    bf16, f32 = jnp.bfloat16, jnp.float32

    in_loads = [pltpu.make_async_copy(in_w_hbm.at[kind], in_w.at[kind], load_sem.at[kind]) for kind in range(3)]
    out_load = pltpu.make_async_copy(out_w_hbm, out_w, load_sem.at[3])
    for copy in in_loads + [out_load]:
        copy.start()

    barrier = pltpu.get_barrier_semaphore()
    devices = [here.partner(), here.along_z(1), here.along_z(-1), here.along_ctx(1), here.along_ctx(-1)]
    for device in devices:
        pl.semaphore_signal(barrier, inc=1, device_id=device, device_id_type=MESH)

    def normalise(index, carry):
        at = tile(index, 16)
        rows = pl.ds(pl.multiple_of(here.tp * block + index * 16, 16), 16)
        floats = hidden[at, :].astype(f32)
        factor = lax.rsqrt(jnp.mean(floats * floats, axis=-1, keepdims=True) + 1e-05)
        both[0, rows, :] = (floats * factor * gain[...]).astype(bf16)
        both[1, rows, :] = cot[at, :]
        return carry

    lax.fori_loop(0, block // 16, normalise, 0)
    pl.semaphore_wait(barrier, len(devices))
    sends = []

    def go(copy):
        copy.start()
        sends.append(copy)

    def rows_of(step, same, begin=0, size=block):
        return pl.ds(pl.multiple_of(here.block(step, same) * block + begin, size), size)

    def gather(which, slot):
        rows, device = (
            lambda: (rows_of(0, True), here.partner()),
            lambda: (rows_of(0, True), here.along_z(1)),
            lambda: (rows_of(0, True), here.along_z(-1)),
            lambda: (rows_of(0, False), here.along_z(1)),
            lambda: (rows_of(0, False), here.along_z(-1)),
            lambda: (rows_of(-1, True, 0, half), here.along_z(1)),
            lambda: (rows_of(1, True, half, half), here.along_z(-1)),
            lambda: (rows_of(2, True), here.partner()),
        )[slot]()
        held = both.at[which, rows]
        go(remote(held, held, send_sem.at[which, slot], recv_sem.at[which, slot], device))

    def arrived(which, slot):
        rows = (
            lambda: rows_of(0, False),
            lambda: rows_of(-1, True),
            lambda: rows_of(1, True),
            lambda: rows_of(-1, False),
            lambda: rows_of(1, False),
            lambda: rows_of(2, True, 0, half),
            lambda: rows_of(2, True, half, half),
            lambda: rows_of(2, False),
        )[slot]()
        held = both.at[which, rows]
        remote(held, held, send_sem.at[which, slot], recv_sem.at[which, slot], here.partner()).wait_recv()

    def project(step):
        begin = ((here.z + step) % 4) * group

        def loop(kind, carry):
            value = jnp.dot(
                both[0, pl.ds(pl.multiple_of(begin, group), group), :], in_w[kind], preferred_element_type=f32
            )
            proj[kind, pl.ds(pl.multiple_of(8 + begin, 8), group), :] = value.astype(bf16).astype(f32)
            return carry

        lax.fori_loop(0, 3, loop, 0)

    def grade(step):
        rows = pl.ds(pl.multiple_of(((here.z + step) % 4) * group, group), group)
        value = lax.dot_general(
            both[1, rows, :], out_w[...], (((1,), (1,)), ((), ())), preferred_element_type=f32
        )
        grads[0, rows, :] = value * query[rows, :]
        grads[1, rows, :] = value * gates[rows, :]

    for which in range(2):
        for slot in range(3):
            gather(which, slot)
    arrived(0, 0)
    gather(0, 3)
    gather(0, 4)
    arrived(0, 1)
    gather(0, 5)
    arrived(0, 2)
    gather(0, 6)
    for copy in in_loads:
        copy.wait()
    project(0)
    arrived(1, 0)
    gather(1, 3)
    gather(1, 4)
    arrived(1, 1)
    gather(1, 5)
    arrived(1, 2)
    gather(1, 6)
    arrived(0, 5)
    arrived(0, 6)
    gather(0, 7)
    arrived(0, 3)
    project(-1)
    arrived(0, 4)
    project(1)
    arrived(1, 5)
    arrived(1, 6)
    gather(1, 7)
    arrived(0, 7)
    norm_copy = pltpu.make_async_copy(both.at[0], norm_out, out_sem.at[0])
    norm_copy.start()
    project(2)

    edge = remote(
        proj.at[:, pl.ds(tokens, 8), :], proj.at[:, pl.ds(0, 8), :], edge_send.at[0], edge_recv.at[0],
        here.along_ctx(1))
    go(edge)
    edge.wait_recv()

    @pl.when(here.ctx == 0)
    def _():
        proj[:, pl.ds(0, 8), :] = jnp.zeros((3, 8, chans), f32)

    steps = chans // 128

    def tap(row, cols):
        return taps[pl.ds(row, 1), cols]

    def behind(value, count):
        return value if count == 0 else pltpu.roll(value, count, 0)

    def ahead(value, count):
        return value if count == 0 else pltpu.roll(value, wide - count, 0)

    def forward(index, carry):
        begin = pl.multiple_of((index // steps) * span, span)
        cols = tile(index % steps, 128)
        feats = []
        for kind in range(3):
            held = proj[kind, pl.ds(begin, wide), cols]
            total = tap(kind, cols) * held
            for lag in (1, 2):
                total = total + tap(lag * 3 + kind, cols) * behind(held, lag)
            feats.append(total)
        product = feats[1] * feats[2]
        total = tap(9, cols) * product
        for lag in range(1, 7):
            total = total + tap(9 + lag, cols) * behind(product, lag)
        rows = pl.ds(begin, span)
        query[rows, cols] = feats[0][8:]
        grads[3, rows, cols] = feats[1][8:]
        grads[2, rows, cols] = feats[2][8:]
        gates[rows, cols] = total[8:]
        prods[pl.ds(pl.multiple_of(begin + 8, 8), span), cols] = product[8:]

        @pl.when(index < steps)
        def _():
            prods[pl.ds(0, 8), cols] = product[:8]

        acts[rows, tile(3 * steps + index % steps, 128)] = (feats[0][8:] * total[8:]).astype(bf16)
        return carry

    lax.fori_loop(0, (tokens // span) * steps, forward, 0)
    head = remote(
        grads.at[pl.ds(2, 2), pl.ds(0, 8), :], grads.at[pl.ds(2, 2), pl.ds(tokens, 8), :],
        edge_send.at[1], edge_recv.at[1], here.along_ctx(-1))
    go(head)
    lags[...] = jnp.zeros_like(lags)

    def turn(index, carry):
        turned[tile(index, 128), :] = acts[:, tile(index, 128)].T
        return carry

    lax.fori_loop(3 * steps, 4 * steps, turn, 0)
    out_load.wait()
    grade(0)
    arrived(1, 3)
    grade(-1)
    arrived(1, 4)
    grade(1)
    arrived(1, 7)
    cot_copy = pltpu.make_async_copy(both.at[1], cot_out, out_sem.at[1])
    cot_copy.start()
    grade(2)
    front = remote(
        grads.at[pl.ds(0, 2), pl.ds(0, 8), :], grads.at[pl.ds(0, 2), pl.ds(tokens, 8), :],
        edge_send.at[2], edge_recv.at[2], here.along_ctx(-1))
    go(front)
    head.wait_recv()
    front.wait_recv()

    @pl.when(here.ctx == 15)
    def _():
        grads[pl.ds(0, 2), pl.ds(tokens, 8), :] = jnp.zeros((2, 8, chans), f32)

    def backward(index, carry):
        begin = pl.multiple_of((index // steps) * span, span)
        cols = tile(index % steps, 128)
        rows = pl.ds(begin, wide)
        inner = grads[0, rows, cols]
        total = tap(9, cols) * inner
        for lag in range(1, 7):
            total = total + tap(9 + lag, cols) * ahead(inner, lag)
        feats = (grads[1, rows, cols], total * grads[2, rows, cols], total * grads[3, rows, cols])

        def add_lag(row, value):
            lags[row, :, cols] += jnp.sum(value.reshape(span // 8, 8, 128), axis=0)

        for kind in range(3):
            feat = feats[kind]
            summed = tap(kind, cols) * feat
            for lag in (1, 2):
                summed = summed + tap(lag * 3 + kind, cols) * ahead(feat, lag)
            acts[pl.ds(begin, span), tile(kind * steps + index % steps, 128)] = summed[:span].astype(bf16)
            held = proj[kind, rows, cols]
            for lag in range(3):
                add_lag(lag * 3 + kind, feat[:span] * behind(held, lag)[8:])
        product = prods[rows, cols]
        for lag in range(7):
            add_lag(9 + lag, inner[:span] * behind(product, lag)[8:])
        return carry

    lax.fori_loop(0, (tokens // span) * steps, backward, 0)
    lax.fori_loop(0, 3 * steps, turn, 0)
    lag_out[...] = jnp.sum(lags[...], axis=1) * scale
    norm_copy.wait()
    cot_copy.wait()
    for copy in sends:
        copy.wait_send()


def gathered(hidden, cot, gain, taps, in_weight, out_weight, tokens, scale):
    block, width = hidden.shape
    chans = out_weight.shape[0]
    any_space = pl.BlockSpec(memory_space=pl.ANY)
    vmem_space = pl.BlockSpec(memory_space=pltpu.VMEM)
    bf16, f32 = jnp.bfloat16, jnp.float32
    dma = pltpu.SemaphoreType.DMA
    body = lambda *refs: gather_kernel(scale, tokens, *refs)
    return pl.pallas_call(
        body,
        out_shape=(
            jax.ShapeDtypeStruct((tokens, width), bf16),
            jax.ShapeDtypeStruct((tokens, width), bf16),
            jax.ShapeDtypeStruct((tokens, 4 * chans), bf16),
            jax.ShapeDtypeStruct((4 * chans, tokens), bf16),
            jax.ShapeDtypeStruct((16, chans), f32),
        ),
        in_specs=[vmem_space] * 4 + [any_space] * 2,
        out_specs=(any_space, any_space, vmem_space, vmem_space, vmem_space),
        scratch_shapes=[
            pltpu.VMEM((2, tokens, width), bf16),
            pltpu.VMEM(in_weight.shape, bf16),
            pltpu.VMEM(out_weight.shape, bf16),
            pltpu.VMEM((3, tokens + 8, chans), f32),
            pltpu.VMEM((tokens, chans), f32),
            pltpu.VMEM((tokens, chans), f32),
            pltpu.VMEM((4, tokens + 8, chans), f32),
            pltpu.VMEM((tokens + 8, chans), f32),
            pltpu.VMEM((16, 8, chans), f32),
            dma((4,)), dma((2, 8)), dma((2, 8)), dma((3,)), dma((3,)), dma((2,)),
        ],
        compiler_params=pltpu.CompilerParams(
            collective_id=1, has_side_effects=True, vmem_limit_bytes=60 * 2**20
        ),
        name="gather_all",
    )(hidden, cot, gain, taps, in_weight, out_weight)


def reduce_kernel(
    scale,
    hidden, cot, gain, lag_in, acts_hbm, turned_hbm, in_w_hbm, out_w_hbm, norm_hbm, cot_hbm,
    layer_ref, input_ref, in_grad_ref, out_grad_ref, lag_ref,
    acts, turned, in_w, out_w, norms, cots,
    sib_out, sums, y_in, x_pass, x_in, parts, tp_in, lag_sum, lag_got,
    lag_send, lag_recv, load_sem, in_w_sem, col_sem, sib_send, sib_recv, y_send, y_recv, x_send, x_recv, tp_send, tp_recv,
):
    here = Place()
    tokens, width = norm_hbm.shape
    chans = out_w_hbm.shape[0]
    cut = width // 16
    rows_all = turned_hbm.shape[0]
    half = rows_all // 2
    block = tokens // 8
    upper, lower = pl.ds(0, half), pl.ds(half, half)
    step_in = in_w.shape[2]
    steps_in = width // step_in

    def target(index, core):
        y = (here.y + DELTAS[index % 4]) % 4
        x_hi = 1 - here.x_hi if index < 4 else here.x_hi
        return y * 4 + x_hi * 2 + core

    order = []
    for index in range(8):
        order.append(target(index, 1 - here.core))
        order.append(target(index, here.core))

    def loads(position):
        cols = tile(order[position], cut)
        return (
            pltpu.make_async_copy(norm_hbm.at[:, cols], norms.at[:, cols], col_sem.at[0, position]),
            pltpu.make_async_copy(cot_hbm.at[:, cols], cots.at[:, cols], col_sem.at[1, position]),
        )

    def in_load(step, slot):
        return pltpu.make_async_copy(in_w_hbm.at[:, tile(step, step_in), :], in_w.at[slot], in_w_sem.at[slot])

    turned_load = pltpu.make_async_copy(turned_hbm, turned, load_sem.at[0])
    acts_load = pltpu.make_async_copy(acts_hbm, acts, load_sem.at[1])
    out_load = pltpu.make_async_copy(out_w_hbm, out_w, load_sem.at[2])
    turned_load.start()
    for copy in loads(0) + loads(1) + loads(2):
        copy.start()
    acts_load.start()
    out_load.start()
    for position in range(3, 16):
        for copy in loads(position):
            copy.start()
    in_load(0, 0).start()
    in_load(1, 1).start()

    greet(
        [here.sibling(), here.along_y(1), here.along_y(-1), here.along_z(1), here.along_z(-1),
         here.along_x(1), here.along_x(-1), here.along_x(2), here.along_y(2)]
    )
    sends = []

    def go(copy):
        copy.start()
        sends.append(copy)

    def product(position, write):
        for copy in loads(position):
            copy.wait()
        cols = tile(order[position], cut)

        def one(index, source):
            rows = tile(index, chans)
            value = jnp.dot(turned[rows, :], source[:, cols], preferred_element_type=jnp.float32)
            write(rows, value * scale)

        def loop(index, carry):
            one(index, norms)
            return carry

        lax.fori_loop(0, rows_all // chans - 1, loop, 0)
        one(rows_all // chans - 1, cots)

    def sib_copy(index):
        slot = index % 4
        return remote(sib_out.at[slot], sums.at[index], sib_send.at[index], sib_recv.at[index], here.sibling())

    def for_sibling(index):
        if index >= 4:
            sib_copy(index - 4).wait_send()

        def write(rows, value):
            sib_out[index % 4, rows, :] = value.astype(jnp.bfloat16)

        product(2 * index, write)
        sib_copy(index).start()

    def for_self(index):
        sib_copy(index).wait_recv()

        def write(rows, value):
            held = sums[index, rows, :].astype(jnp.float32)
            sums[index, rows, :] = (held + value).astype(jnp.bfloat16)

        product(2 * index + 1, write)

    def y_copy(group, slot):
        index, rows, step = (
            (0, upper, 1), (0, lower, -1), (1, lower, 1), (2, upper, -1), (1, upper, 1), (2, lower, -1)
        )[slot]
        return remote(
            sums.at[group * 4 + index, rows], y_in.at[group, slot],
            y_send.at[group, slot], y_recv.at[group, slot], here.along_y(step),
        )

    def add_rows(ref, base, length, others, size=128):
        def loop(index, carry):
            at = tile(index, size)
            rows = pl.ds(pl.multiple_of(base + index * size, size), size)
            total = ref[rows, :].astype(jnp.float32)
            for other in others:
                total = total + other[at, :].astype(jnp.float32)
            ref[rows, :] = total.astype(jnp.bfloat16)
            return carry

        lax.fori_loop(0, length // size, loop, 0)

    def y_pass(group):
        y_copy(group, 0).wait_recv()
        add_rows(sums.at[group * 4 + 1], 0, half, [y_in.at[group, 0]])
        go(y_copy(group, 4))
        y_copy(group, 1).wait_recv()
        add_rows(sums.at[group * 4 + 2], half, half, [y_in.at[group, 1]])
        go(y_copy(group, 5))

    def y_done(group):
        for slot in (3, 4, 2, 5):
            y_copy(group, slot).wait_recv()

    def x_copy(side):
        rows, step = ((upper, 1), (lower, -1))[side]
        return remote(sums.at[3, rows], x_pass.at[side], x_send.at[side], x_recv.at[side], here.along_x(step))

    def x_forward(side):
        return remote(
            x_pass.at[side], x_in.at[side], x_send.at[2 + side], x_recv.at[2 + side], here.along_x((1, -1)[side])
        )

    quarter = block // 2

    def tp_copy(which, slot):
        part, held = parts.at[which], tp_in.at[which]
        source, place, device = (
            lambda: (part.at[tile(here.block(2, False), block)], held.at[0], here.partner()),
            lambda: (part.at[tile(here.block(1, False), block)], held.at[1], here.along_z(1)),
            lambda: (part.at[tile(here.block(-1, False), block)], held.at[2], here.along_z(-1)),
            lambda: (
                part.at[pl.ds(pl.multiple_of(here.block(2, True) * block, block), quarter)],
                held.at[3, pl.ds(0, quarter)], here.along_z(1)),
            lambda: (
                part.at[pl.ds(pl.multiple_of(here.block(2, True) * block + quarter, quarter), quarter)],
                held.at[3, pl.ds(quarter, quarter)], here.along_z(-1)),
            lambda: (part.at[tile(here.block(1, True), block)], held.at[4], here.along_z(1)),
            lambda: (part.at[tile(here.block(-1, True), block)], held.at[5], here.along_z(-1)),
            lambda: (part.at[tile(here.block(0, False), block)], held.at[6], here.partner()),
        )[slot]()
        return remote(source, place, tp_send.at[which, slot], tp_recv.at[which, slot], device)

    def tp_begin(which):
        for slot in range(3):
            go(tp_copy(which, slot))

    def tp_halves(which):
        tp_copy(which, 0).wait_recv()
        add_rows(parts.at[which], here.block(2, True) * block, block, [tp_in.at[which, 0]], 16)
        go(tp_copy(which, 3))
        go(tp_copy(which, 4))

    def tp_direct(which):
        tp_copy(which, 3).wait_recv()
        add_rows(parts.at[which], here.block(1, True) * block, quarter, [tp_in.at[which, 3, pl.ds(0, quarter)]], 16)
        go(tp_copy(which, 5))
        tp_copy(which, 4).wait_recv()
        add_rows(
            parts.at[which], here.block(-1, True) * block + quarter, quarter,
            [tp_in.at[which, 3, pl.ds(quarter, quarter)]], 16)
        go(tp_copy(which, 6))

    def tp_last(which):
        tp_copy(which, 1).wait_recv()
        tp_copy(which, 2).wait_recv()
        add_rows(parts.at[which], here.block(0, False) * block, block, [tp_in.at[which, 1], tp_in.at[which, 2]], 16)
        go(tp_copy(which, 7))

    def tp_total(which, index):
        at = tile(index, 16)
        rows = pl.ds(pl.multiple_of(here.tp * block + index * 16, 16), 16)
        total = parts[which, rows, :].astype(jnp.float32)
        for slot in (4, 5, 6):
            total = total + tp_in[which, slot, at, :].astype(jnp.float32)
        return at, total

    def layer_finish():
        for slot in (5, 6, 7):
            tp_copy(0, slot).wait_recv()

        def loop(index, carry):
            at, total = tp_total(0, index)
            layer_ref[at, :] = (hidden[at, :].astype(jnp.float32) + total).astype(jnp.bfloat16)
            return carry

        lax.fori_loop(0, block // 16, loop, 0)

    def input_finish():
        for slot in (5, 6, 7):
            tp_copy(1, slot).wait_recv()

        def loop(index, carry):
            at, total = tp_total(1, index)
            floats = hidden[at, :].astype(jnp.float32)
            factor = lax.rsqrt(jnp.mean(floats * floats, axis=-1, keepdims=True) + 1e-05)
            gained = total * gain[...]
            inner = jnp.mean(floats * gained, axis=-1, keepdims=True) * factor * factor * factor
            input_ref[at, :] = (cot[at, :].astype(jnp.float32) + gained * factor - floats * inner).astype(jnp.bfloat16)
            return carry

        lax.fori_loop(0, block // 16, loop, 0)

    def branch_product():
        def loop(index, carry):
            cols = tile(index, chans)
            value = jnp.dot(
                acts[:, pl.ds(3 * chans, chans)], out_w[:, cols], preferred_element_type=jnp.float32
            )
            parts[0, :, cols] = value.astype(jnp.bfloat16)
            return carry

        lax.fori_loop(0, width // chans, loop, 0)

    def gnorm_product():
        def loop(step, carry):
            slot = step % 2
            in_load(step, slot).wait()

            def inner(index, carry):
                rows = tile(index, tokens // 2)
                value = jnp.zeros((tokens // 2, step_in), jnp.float32)
                for kind in range(3):
                    value = value + lax.dot_general(
                        acts[rows, pl.ds(kind * chans, chans)], in_w[slot, kind],
                        (((1,), (1,)), ((), ())), preferred_element_type=jnp.float32,
                    )
                parts[1, rows, tile(step, step_in)] = value.astype(jnp.bfloat16)
                return carry

            lax.fori_loop(0, 2, inner, 0)

            @pl.when(step + 2 < steps_in)
            def _():
                in_load(step + 2, slot).start()

            return carry

        lax.fori_loop(0, steps_in, loop, 0)

    def lag_copy(step):
        device = (
            lambda: here.sibling(),
            lambda: here.along_x(2),
            lambda: here.along_y(1 - 2 * (here.y % 2)),
            lambda: here.along_y(2),
        )[step]()
        return remote(lag_sum.at[step], lag_got.at[step], lag_send.at[step], lag_recv.at[step], device)

    def lag_step(step):
        lag_copy(step).wait_recv()
        total = lag_sum[step] + lag_got[step]
        if step < 3:
            lag_sum[step + 1] = total
            go(lag_copy(step + 1))
        else:
            lag_ref[...] = total

    lag_sum[0] = lag_in[...]
    go(lag_copy(0))
    turned_load.wait()
    for_sibling(0)
    for_sibling(1)
    for_self(0)
    go(y_copy(0, 0))
    go(y_copy(0, 1))
    acts_load.wait()
    out_load.wait()
    branch_product()
    tp_begin(0)
    for_sibling(2)
    for_self(1)
    go(y_copy(0, 2))
    for_sibling(3)
    for_self(2)
    go(y_copy(0, 3))
    for_sibling(4)
    for_self(3)
    tp_halves(0)
    lag_step(0)
    gnorm_product()
    tp_begin(1)
    y_pass(0)
    lag_step(1)
    for_sibling(5)
    for_self(4)
    go(y_copy(1, 0))
    go(y_copy(1, 1))
    for_sibling(6)
    for_self(5)
    go(y_copy(1, 2))
    for_sibling(7)
    for_self(6)
    go(y_copy(1, 3))
    for_self(7)
    tp_direct(0)
    lag_step(2)
    tp_last(0)
    y_done(0)
    add_rows(sums.at[3], 0, half, [y_in.at[0, 3], y_in.at[0, 4]])
    go(x_copy(0))
    add_rows(sums.at[3], half, half, [y_in.at[0, 2], y_in.at[0, 5]])
    go(x_copy(1))
    tp_halves(1)
    y_pass(1)
    lag_step(3)
    tp_direct(1)
    tp_last(1)
    for side in range(2):
        x_copy(side).wait_recv()
        go(x_forward(side))
    layer_finish()
    input_finish()
    x_forward(0).wait_recv()
    x_forward(1).wait_recv()
    y_done(1)

    def last_rows(row, pairs):
        total = sums[7, row, :].astype(jnp.float32)
        for other, at in pairs:
            total = total + other[at, :].astype(jnp.float32)
        return total

    def last(begin, others):
        for index in range(half // 128):
            row = begin + index * 128
            at = pl.ds(index * 128, 128)
            total = last_rows(pl.ds(row, 128), [(other, at) for other in others])
            kind, first = row // chans, row % chans
            if kind < 3:
                in_grad_ref[kind, :, pl.ds(first, 128)] = total.T.astype(jnp.bfloat16)
            else:
                out_grad_ref[pl.ds(first, 128), :] = total.astype(jnp.bfloat16)

    last(0, [y_in.at[1, 3], y_in.at[1, 4], x_in.at[0]])
    last(half, [y_in.at[1, 2], y_in.at[1, 5], x_in.at[1]])
    for index in range(4, 8):
        sib_copy(index).wait_send()
    for copy in sends:
        copy.wait_send()


def reduced(hidden, cot, gain, lags, acts, turned, in_weight, out_weight, norms, cots, scale):
    tokens, width = norms.shape
    chans = out_weight.shape[0]
    rows_all = turned.shape[0]
    cut = width // 16
    block = tokens // 8
    half = rows_all // 2
    any_space = pl.BlockSpec(memory_space=pl.ANY)
    vmem_space = pl.BlockSpec(memory_space=pltpu.VMEM)
    bf16 = jnp.bfloat16
    dma = pltpu.SemaphoreType.DMA
    body = lambda *refs: reduce_kernel(scale, *refs)
    return pl.pallas_call(
        body,
        out_shape=(
            jax.ShapeDtypeStruct((block, width), bf16),
            jax.ShapeDtypeStruct((block, width), bf16),
            jax.ShapeDtypeStruct((3, cut, chans), bf16),
            jax.ShapeDtypeStruct((chans, cut), bf16),
            jax.ShapeDtypeStruct((16, chans), jnp.float32),
        ),
        in_specs=[vmem_space] * 4 + [any_space] * 6,
        out_specs=(vmem_space,) * 5,
        scratch_shapes=[
            pltpu.VMEM(acts.shape, bf16),
            pltpu.VMEM(turned.shape, bf16),
            pltpu.VMEM((2, 3, 512, chans), bf16),
            pltpu.VMEM(out_weight.shape, bf16),
            pltpu.VMEM(norms.shape, bf16),
            pltpu.VMEM(cots.shape, bf16),
            pltpu.VMEM((4, rows_all, cut), bf16),
            pltpu.VMEM((8, rows_all, cut), bf16),
            pltpu.VMEM((2, 6, half, cut), bf16),
            pltpu.VMEM((2, half, cut), bf16),
            pltpu.VMEM((2, half, cut), bf16),
            pltpu.VMEM((2, tokens, width), bf16),
            pltpu.VMEM((2, 7, block, width), bf16),
            pltpu.VMEM((4, 16, chans), jnp.float32),
            pltpu.VMEM((4, 16, chans), jnp.float32),
            dma((4,)), dma((4,)), dma((3,)), dma((2,)), dma((2, 16)),
            dma((8,)), dma((8,)), dma((2, 6)), dma((2, 6)), dma((4,)), dma((4,)), dma((2, 8)), dma((2, 8)),
        ],
        compiler_params=pltpu.CompilerParams(
            collective_id=0, has_side_effects=True, vmem_limit_bytes=63 * 2**20
        ),
        name="reduce_all",
    )(hidden, cot, gain, lags, acts, turned, in_weight, out_weight, norms, cots)


def local(hidden_in, cotangent, norm_gain, in_weight, filter_taps, inner_taps, out_weight):
    channels = in_weight.shape[2]
    tokens = hidden_in.shape[0] * lax.axis_size("tp")
    scale = (tokens * lax.axis_size("ctx")) ** (-0.5)
    gain = norm_gain.reshape(1, -1)
    taps = jnp.concatenate([filter_taps.reshape(9, channels), inner_taps])
    kinds = jnp.transpose(in_weight, (1, 0, 2))
    norms, cots, acts, turned, lags = gathered(
        hidden_in, cotangent, gain, taps, kinds, out_weight, tokens, scale
    )
    layer_out, grad_input, grad_kinds, grad_out_weight, lags = reduced(
        hidden_in, cotangent, gain, lags, acts, turned, kinds, out_weight, norms, cots, scale
    )
    grad_in_weight = jnp.transpose(grad_kinds, (1, 0, 2))
    return (layer_out, grad_input, grad_in_weight, grad_out_weight, lags[:9].reshape(3, 3, channels), lags[9:])


def solution(mesh):
    placed = (
        P(("ctx", "tp"), None),
        P(("ctx", "tp"), None),
        P(),
        P(None, None, "tp"),
        P(None, None, "tp"),
        P(None, "tp"),
        P("tp", None),
    )
    return jax.shard_map(
        local,
        mesh=mesh,
        in_specs=placed,
        out_specs=(
            P(("ctx", "tp"), None),
            P(("ctx", "tp"), None),
            P("ctx", None, "tp"),
            P("tp", "ctx"),
            P(None, None, "tp"),
            P(None, "tp"),
        ),
        check_vma=False,
    )
```

```python
import jax
import jax.numpy as jnp
from jax import lax
from jax.experimental import pallas as pl
from jax.experimental.pallas import tpu as pltpu
from jax.sharding import PartitionSpec as P

MESH = pl.DeviceIdType.MESH
DELTAS = (2, 1, 3, 0)


class Place:
    def __init__(self):
        ctx, tp = lax.axis_index("ctx"), lax.axis_index("tp")
        self.y, self.x_hi, self.core = ctx // 4, (ctx // 2) % 2, ctx % 2
        self.z, self.x_lo = tp // 2, tp % 2
        self.ctx, self.tp = ctx, tp

    def sibling(self):
        return (self.y * 4 + self.x_hi * 2 + 1 - self.core, self.tp)

    def along_y(self, step):
        return (((self.y + step) % 4) * 4 + self.x_hi * 2 + self.core, self.tp)

    def along_z(self, step):
        return (self.ctx, ((self.z + step) % 4) * 2 + self.x_lo)

    def along_x(self, step):
        x = (self.x_hi * 2 + self.x_lo + step) % 4
        return (self.y * 4 + (x // 2) * 2 + self.core, self.z * 2 + x % 2)

    def along_ctx(self, step):
        return ((self.ctx + step) % 16, self.tp)

    def partner(self):
        return (self.ctx, self.z * 2 + 1 - self.x_lo)

    def block(self, step, same):
        x_lo = self.x_lo if same else 1 - self.x_lo
        return ((self.z + step) % 4) * 2 + x_lo


def remote(source, target, send, recv, device):
    return pltpu.make_async_remote_copy(
        src_ref=source, dst_ref=target, send_sem=send, recv_sem=recv, device_id=device, device_id_type=MESH
    )


def greet(devices):
    barrier = pltpu.get_barrier_semaphore()
    for device in devices:
        pl.semaphore_signal(barrier, inc=1, device_id=device, device_id_type=MESH)
    pl.semaphore_wait(barrier, len(devices))


def tile(index, size):
    return pl.ds(pl.multiple_of(index * size, size), size)


def gather_kernel(
    scale, tokens,
    hidden, cot, gain, short_taps, inner_taps, in_w_hbm, out_w_hbm,
    norm_out, cot_out, acts_out, turned_out, lag_out,
    both, in_w, out_w, proj, query, gates, grads, prods, lags, acts, turned,
    load_sem, send_sem, recv_sem, edge_send, edge_recv, out_sem,
):
    here = Place()
    block, width = hidden.shape
    chans = out_w_hbm.shape[0]
    half = block // 2
    group = 2 * block
    wide, span = 72, 64
    bf16, f32 = jnp.bfloat16, jnp.float32

    in_loads = [pltpu.make_async_copy(in_w_hbm.at[kind], in_w.at[kind], load_sem.at[kind]) for kind in range(3)]
    out_load = pltpu.make_async_copy(out_w_hbm, out_w, load_sem.at[3])
    for copy in in_loads + [out_load]:
        copy.start()

    barrier = pltpu.get_barrier_semaphore()
    devices = [here.partner(), here.along_z(1), here.along_z(-1), here.along_ctx(1), here.along_ctx(-1)]
    for device in devices:
        pl.semaphore_signal(barrier, inc=1, device_id=device, device_id_type=MESH)

    def normalise(index, carry):
        at = tile(index, 16)
        rows = pl.ds(pl.multiple_of(here.tp * block + index * 16, 16), 16)
        floats = hidden[at, :].astype(f32)
        factor = lax.rsqrt(jnp.mean(floats * floats, axis=-1, keepdims=True) + 1e-05)
        both[0, rows, :] = (floats * factor * gain[...]).astype(bf16)
        both[1, rows, :] = cot[at, :]
        return carry

    lax.fori_loop(0, block // 16, normalise, 0)
    pl.semaphore_wait(barrier, len(devices))
    sends = []

    def go(copy):
        copy.start()
        sends.append(copy)

    def rows_of(step, same, begin=0, size=block):
        return pl.ds(pl.multiple_of(here.block(step, same) * block + begin, size), size)

    def gather(which, slot):
        rows, device = (
            lambda: (rows_of(0, True), here.partner()),
            lambda: (rows_of(0, True), here.along_z(1)),
            lambda: (rows_of(0, True), here.along_z(-1)),
            lambda: (rows_of(0, False), here.along_z(1)),
            lambda: (rows_of(0, False), here.along_z(-1)),
            lambda: (rows_of(-1, True, 0, half), here.along_z(1)),
            lambda: (rows_of(1, True, half, half), here.along_z(-1)),
            lambda: (rows_of(2, True), here.partner()),
        )[slot]()
        held = both.at[which, rows]
        go(remote(held, held, send_sem.at[which, slot], recv_sem.at[which, slot], device))

    def arrived(which, slot):
        rows = (
            lambda: rows_of(0, False),
            lambda: rows_of(-1, True),
            lambda: rows_of(1, True),
            lambda: rows_of(-1, False),
            lambda: rows_of(1, False),
            lambda: rows_of(2, True, 0, half),
            lambda: rows_of(2, True, half, half),
            lambda: rows_of(2, False),
        )[slot]()
        held = both.at[which, rows]
        remote(held, held, send_sem.at[which, slot], recv_sem.at[which, slot], here.partner()).wait_recv()

    def project(step):
        begin = ((here.z + step) % 4) * group

        def loop(kind, carry):
            value = jnp.dot(
                both[0, pl.ds(pl.multiple_of(begin, group), group), :], in_w[kind], preferred_element_type=f32
            )
            proj[kind, pl.ds(pl.multiple_of(8 + begin, 8), group), :] = value.astype(bf16).astype(f32)
            return carry

        lax.fori_loop(0, 3, loop, 0)

    def grade(step):
        rows = pl.ds(pl.multiple_of(((here.z + step) % 4) * group, group), group)
        value = lax.dot_general(
            both[1, rows, :], out_w[...], (((1,), (1,)), ((), ())), preferred_element_type=f32
        )
        grads[0, rows, :] = value * query[rows, :]
        grads[1, rows, :] = value * gates[rows, :]

    for slot in range(3):
        gather(0, slot)
    arrived(0, 1)
    gather(0, 5)
    arrived(0, 2)
    gather(0, 6)
    arrived(0, 0)
    gather(0, 3)
    gather(0, 4)
    for slot in range(3):
        gather(1, slot)
    for copy in in_loads:
        copy.wait()
    project(0)
    arrived(0, 5)
    arrived(0, 6)
    gather(0, 7)
    arrived(0, 3)
    project(-1)
    arrived(0, 4)
    project(1)
    arrived(1, 1)
    gather(1, 5)
    arrived(1, 2)
    gather(1, 6)
    arrived(0, 7)
    project(2)
    edge = remote(
        proj.at[:, pl.ds(tokens, 8), :], proj.at[:, pl.ds(0, 8), :], edge_send.at[0], edge_recv.at[0],
        here.along_ctx(1))
    go(edge)
    arrived(1, 0)
    gather(1, 3)
    gather(1, 4)
    arrived(1, 5)
    arrived(1, 6)
    gather(1, 7)
    norm_copy = pltpu.make_async_copy(both.at[0], norm_out, out_sem.at[0])
    norm_copy.start()

    steps = chans // 128
    bands = tokens // span

    def short(lag, kind, cols):
        return short_taps[lag, pl.ds(kind, 1), cols]

    def inner(lag, cols):
        return inner_taps[pl.ds(lag, 1), cols]

    def behind(value, count):
        return value if count == 0 else pltpu.roll(value, count, 0)

    def ahead(value, count):
        return value if count == 0 else pltpu.roll(value, wide - count, 0)

    def forward(index, carry):
        begin = pl.multiple_of((index // steps) * span, span)
        cols = tile(index % steps, 128)
        feats = []
        for kind in range(3):
            held = proj[kind, pl.ds(begin, wide), cols]
            total = short(0, kind, cols) * held
            for lag in (1, 2):
                total = total + short(lag, kind, cols) * behind(held, lag)
            feats.append(total)
        product = feats[1] * feats[2]
        total = inner(0, cols) * product
        for lag in range(1, 7):
            total = total + inner(lag, cols) * behind(product, lag)
        rows = pl.ds(begin, span)
        query[rows, cols] = feats[0][8:]
        grads[3, rows, cols] = feats[1][8:]
        grads[2, rows, cols] = feats[2][8:]
        gates[rows, cols] = total[8:]
        prods[rows, cols] = product[8:]
        acts[rows, tile(3 * steps + index % steps, 128)] = (feats[0][8:] * total[8:]).astype(bf16)
        return carry

    lax.fori_loop(steps, bands * steps, forward, 0)
    edge.wait_recv()

    @pl.when(here.ctx == 0)
    def _():
        proj[:, pl.ds(0, 8), :] = jnp.zeros((3, 8, chans), f32)

    lax.fori_loop(0, steps, forward, 0)
    head = remote(
        grads.at[pl.ds(2, 2), pl.ds(0, 8), :], grads.at[pl.ds(2, 2), pl.ds(tokens, 8), :],
        edge_send.at[1], edge_recv.at[1], here.along_ctx(-1))
    go(head)
    lags[...] = jnp.zeros_like(lags)

    def turn(index, carry):
        turned[tile(index, 128), :] = acts[:, tile(index, 128)].T
        return carry

    lax.fori_loop(3 * steps, 4 * steps, turn, 0)
    out_load.wait()
    grade(0)
    arrived(1, 3)
    grade(-1)
    arrived(1, 4)
    grade(1)
    arrived(1, 7)
    cot_copy = pltpu.make_async_copy(both.at[1], cot_out, out_sem.at[1])
    cot_copy.start()
    grade(2)
    front = remote(
        grads.at[pl.ds(0, 2), pl.ds(0, 8), :], grads.at[pl.ds(0, 2), pl.ds(tokens, 8), :],
        edge_send.at[2], edge_recv.at[2], here.along_ctx(-1))
    go(front)

    def backward(index, carry):
        begin = pl.multiple_of((index // steps) * span, span)
        cols = tile(index % steps, 128)
        rows = pl.ds(begin, wide)
        here_rows = pl.ds(begin, span)

        def add_lag(row, value):
            lags[row, :, cols] += jnp.sum(value.reshape(span // 8, 8, 128), axis=0)

        gated = grads[0, rows, cols]
        product = prods[here_rows, cols]
        total = inner(0, cols) * gated
        add_lag(9, gated[:span] * product)
        for lag in range(1, 7):
            moved = ahead(gated, lag)
            total = total + inner(lag, cols) * moved
            add_lag(9 + lag, moved[:span] * product)
        feats = (grads[1, rows, cols], total * grads[2, rows, cols], total * grads[3, rows, cols])
        for kind in range(3):
            feat = feats[kind]
            held = proj[kind, pl.ds(pl.multiple_of(begin + 8, 8), span), cols]
            summed = short(0, kind, cols) * feat[:span]
            add_lag(kind, feat[:span] * held)
            for lag in (1, 2):
                moved = ahead(feat, lag)[:span]
                summed = summed + short(lag, kind, cols) * moved
                add_lag(lag * 3 + kind, moved * held)
            acts[here_rows, tile(kind * steps + index % steps, 128)] = summed.astype(bf16)
        return carry

    lax.fori_loop(0, (bands - 1) * steps, backward, 0)
    head.wait_recv()
    front.wait_recv()

    @pl.when(here.ctx == 15)
    def _():
        grads[pl.ds(0, 2), pl.ds(tokens, 8), :] = jnp.zeros((2, 8, chans), f32)

    lax.fori_loop((bands - 1) * steps, bands * steps, backward, 0)
    acts_copy = pltpu.make_async_copy(acts, acts_out, out_sem.at[2])
    acts_copy.start()
    lax.fori_loop(0, 3 * steps, turn, 0)
    turned_copy = pltpu.make_async_copy(turned, turned_out, out_sem.at[3])
    turned_copy.start()
    lag_out[...] = jnp.sum(lags[...], axis=1) * scale
    for copy in (norm_copy, cot_copy, acts_copy, turned_copy):
        copy.wait()
    for copy in sends:
        copy.wait_send()


def gathered(hidden, cot, gain, short_taps, inner_taps, in_weight, out_weight, tokens, scale):
    block, width = hidden.shape
    chans = out_weight.shape[0]
    any_space = pl.BlockSpec(memory_space=pl.ANY)
    vmem_space = pl.BlockSpec(memory_space=pltpu.VMEM)
    bf16, f32 = jnp.bfloat16, jnp.float32
    dma = pltpu.SemaphoreType.DMA
    body = lambda *refs: gather_kernel(scale, tokens, *refs)
    return pl.pallas_call(
        body,
        out_shape=(
            jax.ShapeDtypeStruct((tokens, width), bf16),
            jax.ShapeDtypeStruct((tokens, width), bf16),
            jax.ShapeDtypeStruct((tokens, 4 * chans), bf16),
            jax.ShapeDtypeStruct((4 * chans, tokens), bf16),
            jax.ShapeDtypeStruct((16, chans), f32),
        ),
        in_specs=[vmem_space] * 5 + [any_space] * 2,
        out_specs=(any_space, any_space, any_space, any_space, vmem_space),
        scratch_shapes=[
            pltpu.VMEM((2, tokens, width), bf16),
            pltpu.VMEM(in_weight.shape, bf16),
            pltpu.VMEM(out_weight.shape, bf16),
            pltpu.VMEM((3, tokens + 8, chans), f32),
            pltpu.VMEM((tokens, chans), f32),
            pltpu.VMEM((tokens, chans), f32),
            pltpu.VMEM((4, tokens + 8, chans), f32),
            pltpu.VMEM((tokens, chans), f32),
            pltpu.VMEM((16, 8, chans), f32),
            pltpu.VMEM((tokens, 4 * chans), bf16),
            pltpu.VMEM((4 * chans, tokens), bf16),
            dma((4,)), dma((2, 8)), dma((2, 8)), dma((3,)), dma((3,)), dma((4,)),
        ],
        compiler_params=pltpu.CompilerParams(
            collective_id=1, has_side_effects=True, vmem_limit_bytes=60 * 2**20
        ),
        name="gather_all",
    )(hidden, cot, gain, short_taps, inner_taps, in_weight, out_weight)


def reduce_kernel(
    scale,
    hidden, cot, gain, lag_in, acts_hbm, turned_hbm, in_w_hbm, out_w_hbm, norm_hbm, cot_hbm,
    layer_ref, input_ref, in_grad_ref, out_grad_ref, lag_ref,
    acts, turned, in_w, out_w, norms, cots,
    sib_out, sums, y_in, x_pass, x_in, parts, tp_in, lag_sum, lag_got,
    lag_send, lag_recv, load_sem, in_w_sem, col_sem, sib_send, sib_recv, y_send, y_recv, x_send, x_recv, tp_send, tp_recv,
):
    here = Place()
    tokens, width = norm_hbm.shape
    chans = out_w_hbm.shape[0]
    cut = width // 16
    rows_all = turned_hbm.shape[0]
    half = rows_all // 2
    block = tokens // 8
    upper, lower = pl.ds(0, half), pl.ds(half, half)
    step_in = in_w.shape[2]
    steps_in = width // step_in

    def target(index, core):
        y = (here.y + DELTAS[index % 4]) % 4
        x_hi = 1 - here.x_hi if index < 4 else here.x_hi
        return y * 4 + x_hi * 2 + core

    order = []
    for index in range(8):
        order.append(target(index, 1 - here.core))
        order.append(target(index, here.core))

    def loads(position):
        cols = tile(order[position], cut)
        return (
            pltpu.make_async_copy(norm_hbm.at[:, cols], norms.at[:, cols], col_sem.at[0, position]),
            pltpu.make_async_copy(cot_hbm.at[:, cols], cots.at[:, cols], col_sem.at[1, position]),
        )

    def in_load(step, slot):
        return pltpu.make_async_copy(in_w_hbm.at[:, tile(step, step_in), :], in_w.at[slot], in_w_sem.at[slot])

    turned_load = pltpu.make_async_copy(turned_hbm, turned, load_sem.at[0])
    acts_load = pltpu.make_async_copy(acts_hbm, acts, load_sem.at[1])
    out_load = pltpu.make_async_copy(out_w_hbm, out_w, load_sem.at[2])
    turned_load.start()
    for copy in loads(0) + loads(1) + loads(2):
        copy.start()
    acts_load.start()
    out_load.start()
    for position in range(3, 16):
        for copy in loads(position):
            copy.start()
    in_load(0, 0).start()
    in_load(1, 1).start()

    greet(
        [here.sibling(), here.along_y(1), here.along_y(-1), here.along_z(1), here.along_z(-1),
         here.along_x(1), here.along_x(-1), here.along_x(2), here.along_y(2)]
    )
    sends = {}

    def go(name, copy):
        copy.start()
        sends[name] = copy

    def drained(name):
        sends.pop(name).wait_send()

    def product(position, write):
        for copy in loads(position):
            copy.wait()
        cols = tile(order[position], cut)

        def one(index, source):
            rows = tile(index, chans)
            value = jnp.dot(turned[rows, :], source[:, cols], preferred_element_type=jnp.float32)
            write(rows, value * scale)

        def loop(index, carry):
            one(index, norms)
            return carry

        lax.fori_loop(0, rows_all // chans - 1, loop, 0)
        one(rows_all // chans - 1, cots)

    def sib_copy(index):
        slot = index % 4
        return remote(sib_out.at[slot], sums.at[index], sib_send.at[index], sib_recv.at[index], here.sibling())

    def for_sibling(index):
        if index >= 4:
            sib_copy(index - 4).wait_send()

        def write(rows, value):
            sib_out[index % 4, rows, :] = value.astype(jnp.bfloat16)

        product(2 * index, write)
        sib_copy(index).start()

    def for_self(index):
        sib_copy(index).wait_recv()

        def write(rows, value):
            held = sums[index, rows, :].astype(jnp.float32)
            sums[index, rows, :] = (held + value).astype(jnp.bfloat16)

        product(2 * index + 1, write)

    def y_copy(group, slot):
        index, rows, step = (
            (0, upper, 1), (0, lower, -1), (1, lower, 1), (2, upper, -1), (1, upper, 1), (2, lower, -1)
        )[slot]
        return remote(
            sums.at[group * 4 + index, rows], y_in.at[group, slot],
            y_send.at[group, slot], y_recv.at[group, slot], here.along_y(step),
        )

    def add_rows(ref, base, length, others, size=128):
        def loop(index, carry):
            at = tile(index, size)
            rows = pl.ds(pl.multiple_of(base + index * size, size), size)
            total = ref[rows, :].astype(jnp.float32)
            for other in others:
                total = total + other[at, :].astype(jnp.float32)
            ref[rows, :] = total.astype(jnp.bfloat16)
            return carry

        lax.fori_loop(0, length // size, loop, 0)

    def y_pass(group):
        y_copy(group, 0).wait_recv()
        add_rows(sums.at[group * 4 + 1], 0, half, [y_in.at[group, 0]])
        go(("y", group, 4), y_copy(group, 4))
        y_copy(group, 1).wait_recv()
        add_rows(sums.at[group * 4 + 2], half, half, [y_in.at[group, 1]])
        go(("y", group, 5), y_copy(group, 5))

    def y_done(group):
        for slot in (3, 4, 2, 5):
            y_copy(group, slot).wait_recv()

    def x_copy(side):
        rows, step = ((upper, 1), (lower, -1))[side]
        return remote(sums.at[3, rows], x_pass.at[side], x_send.at[side], x_recv.at[side], here.along_x(step))

    def x_forward(side):
        return remote(
            x_pass.at[side], x_in.at[side], x_send.at[2 + side], x_recv.at[2 + side], here.along_x((1, -1)[side])
        )

    quarter = block // 2

    def tp_copy(which, slot):
        part, held = parts.at[which], tp_in.at[which]
        source, place, device = (
            lambda: (part.at[tile(here.block(2, False), block)], held.at[0], here.partner()),
            lambda: (part.at[tile(here.block(1, False), block)], held.at[1], here.along_z(1)),
            lambda: (part.at[tile(here.block(-1, False), block)], held.at[2], here.along_z(-1)),
            lambda: (
                part.at[pl.ds(pl.multiple_of(here.block(2, True) * block, block), quarter)],
                held.at[3, pl.ds(0, quarter)], here.along_z(1)),
            lambda: (
                part.at[pl.ds(pl.multiple_of(here.block(2, True) * block + quarter, quarter), quarter)],
                held.at[3, pl.ds(quarter, quarter)], here.along_z(-1)),
            lambda: (part.at[tile(here.block(1, True), block)], held.at[4], here.along_z(1)),
            lambda: (part.at[tile(here.block(-1, True), block)], held.at[5], here.along_z(-1)),
            lambda: (part.at[tile(here.block(0, False), block)], held.at[6], here.partner()),
        )[slot]()
        return remote(source, place, tp_send.at[which, slot], tp_recv.at[which, slot], device)

    def tp_begin(which):
        for slot in range(3):
            go(("tp", which, slot), tp_copy(which, slot))

    def tp_halves(which):
        tp_copy(which, 0).wait_recv()
        add_rows(parts.at[which], here.block(2, True) * block, block, [tp_in.at[which, 0]], 16)
        go(("tp", which, 3), tp_copy(which, 3))
        go(("tp", which, 4), tp_copy(which, 4))

    def tp_direct(which):
        tp_copy(which, 3).wait_recv()
        add_rows(parts.at[which], here.block(1, True) * block, quarter, [tp_in.at[which, 3, pl.ds(0, quarter)]], 16)
        go(("tp", which, 5), tp_copy(which, 5))
        tp_copy(which, 4).wait_recv()
        add_rows(
            parts.at[which], here.block(-1, True) * block + quarter, quarter,
            [tp_in.at[which, 3, pl.ds(quarter, quarter)]], 16)
        go(("tp", which, 6), tp_copy(which, 6))

    def tp_last(which):
        tp_copy(which, 1).wait_recv()
        tp_copy(which, 2).wait_recv()
        add_rows(parts.at[which], here.block(0, False) * block, block, [tp_in.at[which, 1], tp_in.at[which, 2]], 16)
        go(("tp", which, 7), tp_copy(which, 7))

    def tp_total(which, index):
        at = tile(index, 16)
        rows = pl.ds(pl.multiple_of(here.tp * block + index * 16, 16), 16)
        total = parts[which, rows, :].astype(jnp.float32)
        for slot in (4, 5, 6):
            total = total + tp_in[which, slot, at, :].astype(jnp.float32)
        return at, total

    def layer_finish():
        for slot in (5, 6, 7):
            tp_copy(0, slot).wait_recv()

        def loop(index, carry):
            at, total = tp_total(0, index)
            layer_ref[at, :] = (hidden[at, :].astype(jnp.float32) + total).astype(jnp.bfloat16)
            return carry

        lax.fori_loop(0, block // 16, loop, 0)

    def input_finish():
        for slot in (5, 6, 7):
            tp_copy(1, slot).wait_recv()

        def loop(index, carry):
            at, total = tp_total(1, index)
            floats = hidden[at, :].astype(jnp.float32)
            factor = lax.rsqrt(jnp.mean(floats * floats, axis=-1, keepdims=True) + 1e-05)
            gained = total * gain[...]
            inner = jnp.mean(floats * gained, axis=-1, keepdims=True) * factor * factor * factor
            input_ref[at, :] = (cot[at, :].astype(jnp.float32) + gained * factor - floats * inner).astype(jnp.bfloat16)
            return carry

        lax.fori_loop(0, block // 16, loop, 0)

    def branch_product():
        def loop(index, carry):
            cols = tile(index, chans)
            value = jnp.dot(
                acts[:, pl.ds(3 * chans, chans)], out_w[:, cols], preferred_element_type=jnp.float32
            )
            parts[0, :, cols] = value.astype(jnp.bfloat16)
            return carry

        lax.fori_loop(0, width // chans, loop, 0)

    def gnorm_product():
        def loop(step, carry):
            slot = step % 2
            in_load(step, slot).wait()

            value = jnp.zeros((tokens, step_in), jnp.float32)
            for kind in range(3):
                value = value + lax.dot_general(
                    acts[:, pl.ds(kind * chans, chans)], in_w[slot, kind],
                    (((1,), (1,)), ((), ())), preferred_element_type=jnp.float32,
                )
            parts[1, :, tile(step, step_in)] = value.astype(jnp.bfloat16)

            @pl.when(step + 2 < steps_in)
            def _():
                in_load(step + 2, slot).start()

            return carry

        lax.fori_loop(0, steps_in, loop, 0)

    def lag_copy(step):
        device = (
            lambda: here.sibling(),
            lambda: here.along_x(2),
            lambda: here.along_y(1 - 2 * (here.y % 2)),
            lambda: here.along_y(2),
        )[step]()
        return remote(lag_sum.at[step], lag_got.at[step], lag_send.at[step], lag_recv.at[step], device)

    def lag_step(step):
        lag_copy(step).wait_recv()
        total = lag_sum[step] + lag_got[step]
        if step < 3:
            lag_sum[step + 1] = total
            go(("lag", step + 1), lag_copy(step + 1))
        else:
            lag_ref[...] = total

    def y_go(group, slot):
        go(("y", group, slot), y_copy(group, slot))

    lag_sum[0] = lag_in[...]
    go(("lag", 0), lag_copy(0))
    turned_load.wait()
    for_sibling(0)
    for_sibling(1)
    for_self(0)
    y_go(0, 0)
    y_go(0, 1)
    acts_load.wait()
    out_load.wait()
    branch_product()
    tp_begin(0)
    for_sibling(2)
    for_self(1)
    y_go(0, 2)
    for_sibling(3)
    for_self(2)
    y_go(0, 3)
    lag_step(0)
    gnorm_product()
    tp_halves(0)
    tp_last(0)
    tp_begin(1)
    y_pass(0)
    for_sibling(4)
    for_self(3)
    for_sibling(5)
    for_self(4)
    tp_direct(0)
    for_sibling(6)
    for_self(5)
    for_sibling(7)
    for_self(6)
    for_self(7)
    lag_step(1)
    for slot in range(4):
        drained(("y", 0, slot))
    y_go(1, 0)
    y_go(1, 1)
    y_done(0)
    add_rows(sums.at[3], 0, half, [y_in.at[0, 3], y_in.at[0, 4]])
    go(("x", 0), x_copy(0))
    add_rows(sums.at[3], half, half, [y_in.at[0, 2], y_in.at[0, 5]])
    go(("x", 1), x_copy(1))
    drained(("y", 0, 4))
    drained(("y", 0, 5))
    y_go(1, 2)
    y_go(1, 3)
    lag_step(2)
    tp_halves(1)
    y_pass(1)
    for side in range(2):
        x_copy(side).wait_recv()
        go(("x", 2 + side), x_forward(side))
    tp_last(1)
    tp_direct(1)
    lag_step(3)
    layer_finish()
    input_finish()
    x_forward(0).wait_recv()
    x_forward(1).wait_recv()
    y_done(1)

    def last_rows(row, pairs):
        total = sums[7, row, :].astype(jnp.float32)
        for other, at in pairs:
            total = total + other[at, :].astype(jnp.float32)
        return total

    def last(begin, others):
        for index in range(half // 128):
            row = begin + index * 128
            at = pl.ds(index * 128, 128)
            total = last_rows(pl.ds(row, 128), [(other, at) for other in others])
            kind, first = row // chans, row % chans
            if kind < 3:
                in_grad_ref[kind, :, pl.ds(first, 128)] = total.T.astype(jnp.bfloat16)
            else:
                out_grad_ref[pl.ds(first, 128), :] = total.astype(jnp.bfloat16)

    last(0, [y_in.at[1, 3], y_in.at[1, 4], x_in.at[0]])
    last(half, [y_in.at[1, 2], y_in.at[1, 5], x_in.at[1]])
    for index in range(4, 8):
        sib_copy(index).wait_send()
    for copy in sends.values():
        copy.wait_send()


def reduced(hidden, cot, gain, lags, acts, turned, in_weight, out_weight, norms, cots, scale):
    tokens, width = norms.shape
    chans = out_weight.shape[0]
    rows_all = turned.shape[0]
    cut = width // 16
    block = tokens // 8
    half = rows_all // 2
    any_space = pl.BlockSpec(memory_space=pl.ANY)
    vmem_space = pl.BlockSpec(memory_space=pltpu.VMEM)
    bf16 = jnp.bfloat16
    dma = pltpu.SemaphoreType.DMA
    body = lambda *refs: reduce_kernel(scale, *refs)
    return pl.pallas_call(
        body,
        out_shape=(
            jax.ShapeDtypeStruct((block, width), bf16),
            jax.ShapeDtypeStruct((block, width), bf16),
            jax.ShapeDtypeStruct((3, cut, chans), bf16),
            jax.ShapeDtypeStruct((chans, cut), bf16),
            jax.ShapeDtypeStruct((16, chans), jnp.float32),
        ),
        in_specs=[vmem_space] * 4 + [any_space] * 6,
        out_specs=(vmem_space,) * 5,
        scratch_shapes=[
            pltpu.VMEM(acts.shape, bf16),
            pltpu.VMEM(turned.shape, bf16),
            pltpu.VMEM((2, 3, 512, chans), bf16),
            pltpu.VMEM(out_weight.shape, bf16),
            pltpu.VMEM(norms.shape, bf16),
            pltpu.VMEM(cots.shape, bf16),
            pltpu.VMEM((4, rows_all, cut), bf16),
            pltpu.VMEM((8, rows_all, cut), bf16),
            pltpu.VMEM((2, 6, half, cut), bf16),
            pltpu.VMEM((2, half, cut), bf16),
            pltpu.VMEM((2, half, cut), bf16),
            pltpu.VMEM((2, tokens, width), bf16),
            pltpu.VMEM((2, 7, block, width), bf16),
            pltpu.VMEM((4, 16, chans), jnp.float32),
            pltpu.VMEM((4, 16, chans), jnp.float32),
            dma((4,)), dma((4,)), dma((3,)), dma((2,)), dma((2, 16)),
            dma((8,)), dma((8,)), dma((2, 6)), dma((2, 6)), dma((4,)), dma((4,)), dma((2, 8)), dma((2, 8)),
        ],
        compiler_params=pltpu.CompilerParams(
            collective_id=0, has_side_effects=True, vmem_limit_bytes=63 * 2**20
        ),
        name="reduce_all",
    )(hidden, cot, gain, lags, acts, turned, in_weight, out_weight, norms, cots)


def place_kernel(
    layer, grad, kinds, outer, lags, layer_to, grad_to, kinds_to, outer_to, short_to, inner_to,
    layer_at, grad_at, kinds_at, outer_at, sems,
):
    pairs = ((kinds, kinds_at, kinds_to), (layer, layer_at, layer_to), (grad, grad_at, grad_to), (outer, outer_at, outer_to))
    reads = [pltpu.make_async_copy(pair[0], pair[1], sems.at[0, index]) for index, pair in enumerate(pairs)]
    writes = [pltpu.make_async_copy(pair[1], pair[2], sems.at[1, index]) for index, pair in enumerate(pairs)]
    for copy in reads:
        copy.start()
    for lag in range(3):
        short_to[lag] = lags[pl.ds(3 * lag, 3), :]
    inner_to[...] = lags[pl.ds(9, 7), :]
    for read, write in zip(reads, writes):
        read.wait()
        write.start()
    for copy in writes:
        copy.wait()


def placed_results(layer, grad, kinds, outer, lags):
    chans = lags.shape[1]
    any_space = pl.BlockSpec(memory_space=pl.ANY)
    vmem_space = pl.BlockSpec(memory_space=pltpu.VMEM)
    arrays = (layer, grad, kinds, outer)
    return pl.pallas_call(
        place_kernel,
        out_shape=tuple(jax.ShapeDtypeStruct(array.shape, array.dtype) for array in arrays)
        + (jax.ShapeDtypeStruct((3, 3, chans), jnp.float32), jax.ShapeDtypeStruct((7, chans), jnp.float32)),
        in_specs=[any_space] * 4 + [vmem_space],
        out_specs=(any_space,) * 4 + (vmem_space,) * 2,
        scratch_shapes=[pltpu.VMEM(array.shape, array.dtype) for array in arrays] + [pltpu.SemaphoreType.DMA((2, 4))],
        compiler_params=pltpu.CompilerParams(vmem_limit_bytes=60 * 2**20),
        name="place_results",
    )(layer, grad, kinds, outer, lags)


def local(hidden_in, cotangent, norm_gain, in_weight, filter_taps, inner_taps, out_weight):
    tokens = hidden_in.shape[0] * lax.axis_size("tp")
    scale = (tokens * lax.axis_size("ctx")) ** (-0.5)
    gain = norm_gain.reshape(1, -1)
    kinds = jnp.transpose(in_weight, (1, 0, 2))
    norms, cots, acts, turned, lags = gathered(
        hidden_in, cotangent, gain, filter_taps, inner_taps, kinds, out_weight, tokens, scale
    )
    layer_out, grad_input, grad_kinds, grad_out_weight, grad_filter, grad_inner = placed_results(
        *reduced(hidden_in, cotangent, gain, lags, acts, turned, kinds, out_weight, norms, cots, scale)
    )
    return (layer_out, grad_input, jnp.transpose(grad_kinds, (1, 0, 2)), grad_out_weight, grad_filter, grad_inner)


def solution(mesh):
    placed = (
        P(("ctx", "tp"), None),
        P(("ctx", "tp"), None),
        P(),
        P(None, None, "tp"),
        P(None, None, "tp"),
        P(None, "tp"),
        P("tp", None),
    )
    return jax.shard_map(
        local,
        mesh=mesh,
        in_specs=placed,
        out_specs=(
            P(("ctx", "tp"), None),
            P(("ctx", "tp"), None),
            P("ctx", None, "tp"),
            P("tp", "ctx"),
            P(None, None, "tp"),
            P(None, "tp"),
        ),
        check_vma=False,
    )
```

```python
import jax
import jax.numpy as jnp
from jax import lax
from jax.experimental import pallas as pl
from jax.experimental.pallas import tpu as pltpu
from jax.sharding import PartitionSpec as P

MESH = pl.DeviceIdType.MESH
DELTAS = (2, 1, 3, 0)


class Place:
    def __init__(self):
        ctx, tp = lax.axis_index("ctx"), lax.axis_index("tp")
        self.y, self.x_hi, self.core = ctx // 4, (ctx // 2) % 2, ctx % 2
        self.z, self.x_lo = tp // 2, tp % 2
        self.ctx, self.tp = ctx, tp

    def sibling(self):
        return (self.y * 4 + self.x_hi * 2 + 1 - self.core, self.tp)

    def along_y(self, step):
        return (((self.y + step) % 4) * 4 + self.x_hi * 2 + self.core, self.tp)

    def along_z(self, step):
        return (self.ctx, ((self.z + step) % 4) * 2 + self.x_lo)

    def along_x(self, step):
        x = (self.x_hi * 2 + self.x_lo + step) % 4
        return (self.y * 4 + (x // 2) * 2 + self.core, self.z * 2 + x % 2)

    def along_ctx(self, step):
        return ((self.ctx + step) % 16, self.tp)

    def partner(self):
        return (self.ctx, self.z * 2 + 1 - self.x_lo)

    def block(self, step, same):
        x_lo = self.x_lo if same else 1 - self.x_lo
        return ((self.z + step) % 4) * 2 + x_lo


def remote(source, target, send, recv, device):
    return pltpu.make_async_remote_copy(
        src_ref=source, dst_ref=target, send_sem=send, recv_sem=recv, device_id=device, device_id_type=MESH
    )


def tile(index, size):
    return pl.ds(pl.multiple_of(index * size, size), size)


def layer_kernel(
    scale, tokens,
    hidden, cot, gain, short_taps, inner_taps, in_w_hbm, out_w_hbm,
    layer_ref, input_ref, in_grad_ref, out_grad_ref, lag_ref,
    both, out_w, proj, edges, lags, acts, turned, part,
    sums_out, sums_in, y_out, y_in, pass_out, pass_in, x_out, x_in, tp_in, lag_sum, lag_got,
    load_sem, in_w_sem, send_sem, recv_sem, edge_send, edge_recv,
    sib_send, sib_recv, y_send, y_recv, x_send, x_recv, tp_send, tp_recv, lag_send, lag_recv,
):
    here = Place()
    block, width = hidden.shape
    chans = out_w_hbm.shape[0]
    cut = width // 16
    half = block // 2
    group = 2 * block
    wide, span = 72, 64
    steps = chans // 128
    bands = tokens // span
    step_in = 512
    bf16, f32 = jnp.bfloat16, jnp.float32

    out_load = pltpu.make_async_copy(out_w_hbm, out_w, load_sem.at[3])
    barrier = pltpu.get_barrier_semaphore()
    devices = [
        here.sibling(), here.along_y(1), here.along_y(-1), here.along_y(2), here.along_z(1), here.along_z(-1),
        here.along_x(1), here.along_x(-1), here.along_x(2), here.along_ctx(1), here.along_ctx(-1),
    ]
    for device in devices:
        pl.semaphore_signal(barrier, inc=1, device_id=device, device_id_type=MESH)

    sends = {}

    def go(name, build):
        build().start()
        sends[name] = build

    def drained(name):
        sends.pop(name)().wait_send()


    def rows_of(step, same, begin=0, size=block):
        return pl.ds(pl.multiple_of(here.block(step, same) * block + begin, size), size)

    def gather_copy(which, slot):
        rows, device = (
            lambda: (rows_of(0, True), here.partner()),
            lambda: (rows_of(0, True), here.along_z(1)),
            lambda: (rows_of(0, True), here.along_z(-1)),
            lambda: (rows_of(0, False), here.along_z(1)),
            lambda: (rows_of(0, False), here.along_z(-1)),
            lambda: (rows_of(-1, True, 0, half), here.along_z(1)),
            lambda: (rows_of(1, True, half, half), here.along_z(-1)),
            lambda: (rows_of(2, True), here.partner()),
        )[slot]()
        held = both.at[which, rows]
        return remote(held, held, send_sem.at[which, slot], recv_sem.at[which, slot], device)

    def gather(which, slot):
        go(("gather", which, slot), lambda: gather_copy(which, slot))

    def arrived(which, slot):
        rows = (
            lambda: rows_of(0, False),
            lambda: rows_of(-1, True),
            lambda: rows_of(1, True),
            lambda: rows_of(-1, False),
            lambda: rows_of(1, False),
            lambda: rows_of(2, True, 0, half),
            lambda: rows_of(2, True, half, half),
            lambda: rows_of(2, False),
        )[slot]()
        held = both.at[which, rows]
        remote(held, held, send_sem.at[which, slot], recv_sem.at[which, slot], here.partner()).wait_recv()


    parts = (part, out_w)

    def tp_copy(which, slot):
        source, held = parts[which], tp_in.at[which]
        first = pl.ds(0, half)
        second = pl.ds(half, half)
        rows, place, device = (
            lambda: (rows_of(2, False), held.at[0], here.partner()),
            lambda: (rows_of(1, False), held.at[1], here.along_z(1)),
            lambda: (rows_of(-1, False), held.at[2], here.along_z(-1)),
            lambda: (rows_of(2, True, 0, half), held.at[3, first], here.along_z(1)),
            lambda: (rows_of(2, True, half, half), held.at[3, second], here.along_z(-1)),
            lambda: (rows_of(1, True), held.at[4], here.along_z(1)),
            lambda: (rows_of(-1, True), held.at[5], here.along_z(-1)),
            lambda: (rows_of(0, False), held.at[6], here.partner()),
        )[slot]()
        return remote(source.at[rows], place, tp_send.at[which, slot], tp_recv.at[which, slot], device)

    def tp_go(which, slot):
        go(("tp", which, slot), lambda: tp_copy(which, slot))

    def add_rows(ref, base, length, others, size=128):
        def loop(index, carry):
            at = tile(index, size)
            rows = pl.ds(pl.multiple_of(base + index * size, size), size)
            total = ref[rows, :].astype(f32)
            for other in others:
                total = total + other[at, :].astype(f32)
            ref[rows, :] = total.astype(bf16)
            return carry

        lax.fori_loop(0, length // size, loop, 0)

    def tp_begin(which):
        for slot in range(3):
            tp_go(which, slot)

    def tp_halves(which):
        tp_copy(which, 0).wait_recv()
        add_rows(parts[which], here.block(2, True) * block, block, [tp_in.at[which, 0]], 16)
        tp_go(which, 3)
        tp_go(which, 4)

    def tp_direct(which):
        tp_copy(which, 3).wait_recv()
        add_rows(parts[which], here.block(1, True) * block, half, [tp_in.at[which, 3, pl.ds(0, half)]], 16)
        tp_go(which, 5)
        tp_copy(which, 4).wait_recv()
        add_rows(
            parts[which], here.block(-1, True) * block + half, half, [tp_in.at[which, 3, pl.ds(half, half)]], 16)
        tp_go(which, 6)

    def tp_last(which):
        tp_copy(which, 1).wait_recv()
        tp_copy(which, 2).wait_recv()
        add_rows(parts[which], here.block(0, False) * block, block, [tp_in.at[which, 1], tp_in.at[which, 2]], 16)
        tp_go(which, 7)

    def tp_total(which, index):
        at = tile(index, 16)
        rows = pl.ds(pl.multiple_of(here.tp * block + index * 16, 16), 16)
        total = parts[which][rows, :].astype(f32)
        for slot in (4, 5, 6):
            total = total + tp_in[which, slot, at, :].astype(f32)
        return at, total


    sums = (sums_out, sums_in)
    arriving = (y_out, y_in)
    passing = (pass_out, pass_in)
    crossing = (x_out, x_in)

    def halves(kind):
        size = sums[kind].shape[1] // 2
        return pl.ds(0, size), pl.ds(size, size), size

    def target(index, core):
        y = (here.y + DELTAS[index % 4]) % 4
        x_hi = 1 - here.x_hi if index < 4 else here.x_hi
        return y * 4 + x_hi * 2 + core

    def product(kind, index, core, write):
        cols = tile(target(index, core), cut)

        def one(step, carry):
            rows = tile(step, chans)
            first = 3 * chans if kind == 0 else 0
            left = turned[pl.ds(pl.multiple_of(first + step * chans, chans), chans), :]
            value = jnp.dot(left, both[1 - kind, :, cols], preferred_element_type=f32)
            write(rows, value * scale)
            return carry

        lax.fori_loop(0, (1, 3)[kind], one, 0)

    def sib_copy(kind, sib, index):
        return remote(
            sib.at[index % 4], sums[kind].at[index], sib_send.at[kind, index], sib_recv.at[kind, index],
            here.sibling())

    def for_sibling(kind, sib, index):
        if index >= 4:
            drained(("sib", kind, index - 4))

        def write(rows, value):
            sib[index % 4, rows, :] = value.astype(bf16)

        product(kind, index, 1 - here.core, write)
        go(("sib", kind, index), lambda: sib_copy(kind, sib, index))

    def for_self(kind, sib, index):
        sib_copy(kind, sib, index).wait_recv()

        def write(rows, value):
            held = sums[kind][index, rows, :].astype(f32)
            sums[kind][index, rows, :] = (held + value).astype(bf16)

        product(kind, index, here.core, write)

    def y_copy(kind, far, slot):
        upper, lower, _ = halves(kind)
        index, rows, step = (
            (0, upper, 1), (0, lower, -1), (1, lower, 1), (2, upper, -1), (1, upper, 1), (2, lower, -1)
        )[slot]
        return remote(
            sums[kind].at[far * 4 + index, rows], arriving[kind].at[far, slot],
            y_send.at[kind, far, slot], y_recv.at[kind, far, slot], here.along_y(step),
        )

    def y_go(kind, far, slot):
        go(("y", kind, far, slot), lambda: y_copy(kind, far, slot))

    def y_pass(kind, far):
        size = halves(kind)[2]
        y_copy(kind, far, 0).wait_recv()
        add_rows(sums[kind].at[far * 4 + 1], 0, size, [arriving[kind].at[far, 0]])
        y_go(kind, far, 4)
        y_copy(kind, far, 1).wait_recv()
        add_rows(sums[kind].at[far * 4 + 2], size, size, [arriving[kind].at[far, 1]])
        y_go(kind, far, 5)

    def y_done(kind, far):
        for slot in (3, 4, 2, 5):
            y_copy(kind, far, slot).wait_recv()

    def x_copy(kind, side):
        rows = halves(kind)[side]
        return remote(
            sums[kind].at[3, rows], passing[kind].at[side], x_send.at[kind, side], x_recv.at[kind, side],
            here.along_x((1, -1)[side]))

    def x_forward(kind, side):
        return remote(
            passing[kind].at[side], crossing[kind].at[side], x_send.at[kind, 2 + side], x_recv.at[kind, 2 + side],
            here.along_x((1, -1)[side]))

    def x_begin(kind):
        size = halves(kind)[2]
        y_done(kind, 0)
        add_rows(sums[kind].at[3], 0, size, [arriving[kind].at[0, 3], arriving[kind].at[0, 4]])
        go(("x", kind, 0), lambda: x_copy(kind, 0))
        add_rows(sums[kind].at[3], size, size, [arriving[kind].at[0, 2], arriving[kind].at[0, 5]])
        go(("x", kind, 1), lambda: x_copy(kind, 1))

    def x_go(kind, side):
        go(("x", kind, 2 + side), lambda: x_forward(kind, side))

    def x_on(kind):
        for side in range(2):
            x_copy(kind, side).wait_recv()
            x_go(kind, side)

    def last(kind, side):
        size = halves(kind)[2]
        begin = side * size
        others = [arriving[kind].at[1, slot] for slot in ((3, 4), (2, 5))[side]] + [crossing[kind].at[side]]
        for index in range(size // 128):
            row = begin + index * 128
            total = sums[kind][7, pl.ds(row, 128), :].astype(f32)
            for other in others:
                total = total + other[pl.ds(index * 128, 128), :].astype(f32)
            if kind == 1:
                in_grad_ref[row // chans, :, pl.ds(row % chans, 128)] = total.T.astype(bf16)
            else:
                out_grad_ref[pl.ds(row, 128), :] = total.astype(bf16)

    def lag_copy(step):
        device = (
            lambda: here.sibling(),
            lambda: here.along_x(2),
            lambda: here.along_y(1 - 2 * (here.y % 2)),
            lambda: here.along_y(2),
        )[step]()
        return remote(lag_sum.at[step], lag_got.at[step], lag_send.at[step], lag_recv.at[step], device)

    def lag_step(step):
        lag_copy(step).wait_recv()
        total = lag_sum[step] + lag_got[step]
        if step < 3:
            lag_sum[step + 1] = total
            go(("lag", step + 1), lambda: lag_copy(step + 1))
        else:
            lag_ref[...] = total

    def gather_phase(in_w):
        loads = [pltpu.make_async_copy(in_w_hbm.at[kind], in_w.at[kind], load_sem.at[kind]) for kind in range(3)]
        for copy in loads:
            copy.start()
        out_load.start()

        def normalise(index, carry):
            at = tile(index, 16)
            rows = pl.ds(pl.multiple_of(here.tp * block + index * 16, 16), 16)
            floats = hidden[at, :].astype(f32)
            factor = lax.rsqrt(jnp.mean(floats * floats, axis=-1, keepdims=True) + 1e-05)
            both[0, rows, :] = (floats * factor * gain[...]).astype(bf16)
            both[1, rows, :] = cot[at, :]
            return carry

        lax.fori_loop(0, block // 16, normalise, 0)
        pl.semaphore_wait(barrier, len(devices))

        def project(step):
            begin = ((here.z + step) % 4) * group

            def loop(kind, carry):
                value = jnp.dot(
                    both[0, pl.ds(pl.multiple_of(begin, group), group), :], in_w[kind], preferred_element_type=f32
                )
                proj[kind, pl.ds(pl.multiple_of(8 + begin, 8), group), :] = value.astype(bf16).astype(f32)
                return carry

            lax.fori_loop(0, 3, loop, 0)

        for slot in range(3):
            gather(0, slot)
        arrived(0, 1)
        gather(0, 5)
        arrived(0, 2)
        gather(0, 6)
        arrived(0, 0)
        gather(0, 3)
        gather(0, 4)
        for slot in range(3):
            gather(1, slot)
        for copy in loads:
            copy.wait()
        project(0)
        arrived(0, 5)
        arrived(0, 6)
        gather(0, 7)
        arrived(0, 3)
        project(-1)
        arrived(0, 4)
        project(1)
        arrived(1, 1)
        gather(1, 5)
        arrived(1, 2)
        gather(1, 6)
        arrived(0, 7)
        project(2)

    def filter_phase(query, gates, prods, grads, sib):
        def edge_copy():
            return remote(
                proj.at[:, pl.ds(tokens, 8), :], proj.at[:, pl.ds(0, 8), :], edge_send.at[0], edge_recv.at[0],
                here.along_ctx(1))

        def front_copy(which):
            first = pl.ds((0, 2)[which], 2)
            return remote(
                grads.at[first, pl.ds(0, 8), :], edges.at[first], edge_send.at[1 + which], edge_recv.at[1 + which],
                here.along_ctx(-1))

        go(("edge", 0), edge_copy)
        arrived(1, 0)
        gather(1, 3)
        gather(1, 4)
        arrived(1, 5)
        arrived(1, 6)
        gather(1, 7)

        def short(lag, kind, cols):
            return short_taps[lag, pl.ds(kind, 1), cols]

        def inner(lag, cols):
            return inner_taps[pl.ds(lag, 1), cols]

        def behind(value, count):
            return pltpu.roll(value, count, 0)

        def ahead(value, count):
            return pltpu.roll(value, wide - count, 0)

        def forward(index, carry):
            begin = pl.multiple_of((index // steps) * span, span)
            cols = tile(index % steps, 128)
            feats = []
            for kind in range(3):
                held = proj[kind, pl.ds(begin, wide), cols]
                total = short(0, kind, cols) * held
                for lag in (1, 2):
                    total = total + short(lag, kind, cols) * behind(held, lag)
                feats.append(total)
            product = feats[1] * feats[2]
            total = inner(0, cols) * product
            for lag in range(1, 7):
                total = total + inner(lag, cols) * behind(product, lag)
            rows = pl.ds(begin, span)
            query[rows, cols] = feats[0][8:]
            grads[3, rows, cols] = feats[1][8:]
            grads[2, rows, cols] = feats[2][8:]
            gates[rows, cols] = total[8:]
            prods[rows, cols] = product[8:]
            acts[rows, tile(3 * steps + index % steps, 128)] = (feats[0][8:] * total[8:]).astype(bf16)
            return carry

        lax.fori_loop(steps, bands * steps, forward, 0)
        edge_copy().wait_recv()

        @pl.when(here.ctx == 0)
        def _():
            proj[:, pl.ds(0, 8), :] = jnp.zeros((3, 8, chans), f32)

        lax.fori_loop(0, steps, forward, 0)
        go(("edge", 1), lambda: front_copy(1))
        lags[...] = jnp.zeros_like(lags)

        def turn(index, carry):
            turned[tile(index, 128), :] = acts[:, tile(index, 128)].T
            return carry

        lax.fori_loop(3 * steps, 4 * steps, turn, 0)
        out_load.wait()

        def branch_product(index, carry):
            cols = tile(index, chans)
            value = jnp.dot(acts[:, pl.ds(3 * chans, chans)], out_w[:, cols], preferred_element_type=f32)
            part[:, cols] = value.astype(bf16)
            return carry

        lax.fori_loop(0, width // chans, branch_product, 0)

        def grade(step):
            rows = pl.ds(pl.multiple_of(((here.z + step) % 4) * group, group), group)
            value = lax.dot_general(
                both[1, rows, :], out_w[...], (((1,), (1,)), ((), ())), preferred_element_type=f32
            )
            grads[0, rows, :] = value * query[rows, :]
            grads[1, rows, :] = value * gates[rows, :]

        grade(0)
        arrived(1, 3)
        arrived(1, 4)
        arrived(1, 7)
        tp_begin(0)
        for_sibling(0, sib, 0)
        for_sibling(0, sib, 1)
        for_sibling(0, sib, 2)
        for_self(0, sib, 0)
        y_go(0, 0, 0)
        y_go(0, 0, 1)
        for_sibling(0, sib, 3)
        for_self(0, sib, 1)
        y_go(0, 0, 2)
        for_self(0, sib, 2)
        y_go(0, 0, 3)
        grade(-1)
        grade(1)
        grade(2)
        go(("edge", 2), lambda: front_copy(0))
        y_pass(0, 0)
        for index in range(4, 8):
            for_sibling(0, sib, index)
            for_self(0, sib, index - 1)
            if index == 5:
                y_go(0, 1, 0)
                y_go(0, 1, 1)
            if index == 6:
                y_go(0, 1, 2)
            if index == 7:
                y_go(0, 1, 3)
        for_self(0, sib, 7)

        def backward(index, carry):
            begin = pl.multiple_of((index // steps) * span, span)
            cols = tile(index % steps, 128)
            rows = pl.ds(begin, wide)
            here_rows = pl.ds(begin, span)

            def add_lag(row, value):
                lags[row, :, cols] += jnp.sum(value.reshape(span // 8, 8, 128), axis=0)

            gated = grads[0, rows, cols]
            product = prods[here_rows, cols]
            total = inner(0, cols) * gated
            add_lag(9, gated[:span] * product)
            for lag in range(1, 7):
                moved = ahead(gated, lag)
                total = total + inner(lag, cols) * moved
                add_lag(9 + lag, moved[:span] * product)
            feats = (grads[1, rows, cols], total * grads[2, rows, cols], total * grads[3, rows, cols])
            for kind in range(3):
                feat = feats[kind]
                held = proj[kind, pl.ds(pl.multiple_of(begin + 8, 8), span), cols]
                summed = short(0, kind, cols) * feat[:span]
                add_lag(kind, feat[:span] * held)
                for lag in (1, 2):
                    moved = ahead(feat, lag)[:span]
                    summed = summed + short(lag, kind, cols) * moved
                    add_lag(lag * 3 + kind, moved * held)
                acts[here_rows, tile(kind * steps + index % steps, 128)] = summed.astype(bf16)
            return carry

        lax.fori_loop(0, (bands - 1) * steps, backward, 0)
        front_copy(1).wait_recv()
        front_copy(0).wait_recv()
        grads[:, pl.ds(tokens, 8), :] = edges[...]

        @pl.when(here.ctx == 15)
        def _():
            grads[pl.ds(0, 2), pl.ds(tokens, 8), :] = jnp.zeros((2, 8, chans), f32)

        lax.fori_loop((bands - 1) * steps, bands * steps, backward, 0)
        lax.fori_loop(0, 3 * steps, turn, 0)
        lag_sum[0] = jnp.sum(lags[...], axis=1) * scale
        go(("lag", 0), lambda: lag_copy(0))
        y_pass(0, 1)
        x_begin(0)
        for index in range(3):
            drained(("edge", index))
        for index in range(4, 8):
            drained(("sib", 0, index))

    def reduce_phase(in_w, sib):
        def in_load(step, slot):
            return pltpu.make_async_copy(in_w_hbm.at[:, tile(step, step_in), :], in_w.at[slot], in_w_sem.at[slot])

        in_load(0, 0).start()
        in_load(1, 1).start()

        def gnorm_product():
            def loop(step, carry):
                slot = step % 2
                in_load(step, slot).wait()
                value = jnp.zeros((tokens, step_in), f32)
                for kind in range(3):
                    value = value + lax.dot_general(
                        acts[:, pl.ds(kind * chans, chans)], in_w[slot, kind],
                        (((1,), (1,)), ((), ())), preferred_element_type=f32,
                    )
                out_w[:, tile(step, step_in)] = value.astype(bf16)

                @pl.when(step + 2 < width // step_in)
                def _():
                    in_load(step + 2, slot).start()

                return carry

            lax.fori_loop(0, width // step_in, loop, 0)

        for_sibling(1, sib, 0)
        for_sibling(1, sib, 1)
        for_self(1, sib, 0)
        y_go(1, 0, 0)
        y_go(1, 0, 1)
        tp_halves(0)
        tp_last(0)
        for_sibling(1, sib, 2)
        for_self(1, sib, 1)
        y_go(1, 0, 2)
        for_sibling(1, sib, 3)
        for_self(1, sib, 2)
        y_go(1, 0, 3)
        lag_step(0)
        x_on(0)
        tp_direct(0)
        gnorm_product()
        tp_begin(1)
        y_pass(1, 0)
        lag_step(1)
        for index in range(4, 8):
            for_sibling(1, sib, index)
            for_self(1, sib, index - 1)
        for_self(1, sib, 7)
        for slot in range(4):
            drained(("y", 1, 0, slot))
        y_go(1, 1, 0)
        y_go(1, 1, 1)
        tp_halves(1)
        lag_step(2)
        x_begin(1)
        drained(("y", 1, 0, 4))
        drained(("y", 1, 0, 5))
        y_go(1, 1, 2)
        y_go(1, 1, 3)
        for slot in (5, 6, 7):
            tp_copy(0, slot).wait_recv()

        def layer_finish(index, carry):
            at, total = tp_total(0, index)
            layer_ref[at, :] = (hidden[at, :].astype(f32) + total).astype(bf16)
            return carry

        lax.fori_loop(0, block // 16, layer_finish, 0)
        for side in range(2):
            x_forward(0, side).wait_recv()
        y_done(0, 1)
        last(0, 0)
        last(0, 1)
        lag_step(3)
        y_pass(1, 1)
        x_on(1)
        tp_last(1)
        tp_direct(1)
        for slot in (5, 6, 7):
            tp_copy(1, slot).wait_recv()

        def input_finish(index, carry):
            at, total = tp_total(1, index)
            floats = hidden[at, :].astype(f32)
            factor = lax.rsqrt(jnp.mean(floats * floats, axis=-1, keepdims=True) + 1e-05)
            gained = total * gain[...]
            inner = jnp.mean(floats * gained, axis=-1, keepdims=True) * factor * factor * factor
            input_ref[at, :] = (cot[at, :].astype(f32) + gained * factor - floats * inner).astype(bf16)
            return carry

        lax.fori_loop(0, block // 16, input_finish, 0)
        for side in range(2):
            x_forward(1, side).wait_recv()
        y_done(1, 1)
        last(1, 0)
        last(1, 1)
        for name in list(sends):
            drained(name)

    pl.run_scoped(gather_phase, pltpu.VMEM((3, width, chans), bf16))
    pl.run_scoped(
        filter_phase,
        pltpu.VMEM((tokens, chans), f32),
        pltpu.VMEM((tokens, chans), f32),
        pltpu.VMEM((tokens, chans), f32),
        pltpu.VMEM((4, tokens + 8, chans), f32),
        pltpu.VMEM((4, chans, cut), bf16),
    )
    pl.run_scoped(
        reduce_phase, pltpu.VMEM((2, 3, step_in, chans), bf16), pltpu.VMEM((4, 3 * chans, cut), bf16)
    )


def layer_results(hidden, cot, gain, short_taps, inner_taps, in_weight, out_weight, tokens, scale):
    block, width = hidden.shape
    chans = out_weight.shape[0]
    cut = width // 16
    any_space = pl.BlockSpec(memory_space=pl.ANY)
    vmem_space = pl.BlockSpec(memory_space=pltpu.VMEM)
    bf16, f32 = jnp.bfloat16, jnp.float32
    dma = pltpu.SemaphoreType.DMA
    body = lambda *refs: layer_kernel(scale, tokens, *refs)
    return pl.pallas_call(
        body,
        out_shape=(
            jax.ShapeDtypeStruct((block, width), bf16),
            jax.ShapeDtypeStruct((block, width), bf16),
            jax.ShapeDtypeStruct((3, cut, chans), bf16),
            jax.ShapeDtypeStruct((chans, cut), bf16),
            jax.ShapeDtypeStruct((16, chans), f32),
        ),
        in_specs=[vmem_space] * 5 + [any_space] * 2,
        out_specs=(vmem_space,) * 5,
        scratch_shapes=[
            pltpu.VMEM((2, tokens, width), bf16),
            pltpu.VMEM(out_weight.shape, bf16),
            pltpu.VMEM((3, tokens + 8, chans), f32),
            pltpu.VMEM((4, 8, chans), f32),
            pltpu.VMEM((16, 8, chans), f32),
            pltpu.VMEM((tokens, 4 * chans), bf16),
            pltpu.VMEM((4 * chans, tokens), bf16),
            pltpu.VMEM((tokens, width), bf16),
            pltpu.VMEM((8, chans, cut), bf16),
            pltpu.VMEM((8, 3 * chans, cut), bf16),
            pltpu.VMEM((2, 6, chans // 2, cut), bf16),
            pltpu.VMEM((2, 6, 3 * chans // 2, cut), bf16),
            pltpu.VMEM((2, chans // 2, cut), bf16),
            pltpu.VMEM((2, 3 * chans // 2, cut), bf16),
            pltpu.VMEM((2, chans // 2, cut), bf16),
            pltpu.VMEM((2, 3 * chans // 2, cut), bf16),
            pltpu.VMEM((2, 7, block, width), bf16),
            pltpu.VMEM((4, 16, chans), f32),
            pltpu.VMEM((4, 16, chans), f32),
            dma((4,)), dma((2,)), dma((2, 8)), dma((2, 8)), dma((3,)), dma((3,)),
            dma((2, 8)), dma((2, 8)), dma((2, 2, 6)), dma((2, 2, 6)), dma((2, 4)), dma((2, 4)),
            dma((2, 8)), dma((2, 8)), dma((4,)), dma((4,)),
        ],
        compiler_params=pltpu.CompilerParams(
            collective_id=0, has_side_effects=True, vmem_limit_bytes=63 * 2**20
        ),
        name="whole_layer",
    )(hidden, cot, gain, short_taps, inner_taps, in_weight, out_weight)


def place_kernel(
    layer, grad, kinds, outer, lags, layer_to, grad_to, kinds_to, outer_to, short_to, inner_to,
    layer_at, grad_at, kinds_at, outer_at, sems,
):
    pairs = ((kinds, kinds_at, kinds_to), (layer, layer_at, layer_to), (grad, grad_at, grad_to), (outer, outer_at, outer_to))
    reads = [pltpu.make_async_copy(pair[0], pair[1], sems.at[0, index]) for index, pair in enumerate(pairs)]
    writes = [pltpu.make_async_copy(pair[1], pair[2], sems.at[1, index]) for index, pair in enumerate(pairs)]
    for copy in reads:
        copy.start()
    for lag in range(3):
        short_to[lag] = lags[pl.ds(3 * lag, 3), :]
    inner_to[...] = lags[pl.ds(9, 7), :]
    for read, write in zip(reads, writes):
        read.wait()
        write.start()
    for copy in writes:
        copy.wait()


def placed_results(layer, grad, kinds, outer, lags):
    chans = lags.shape[1]
    any_space = pl.BlockSpec(memory_space=pl.ANY)
    vmem_space = pl.BlockSpec(memory_space=pltpu.VMEM)
    arrays = (layer, grad, kinds, outer)
    return pl.pallas_call(
        place_kernel,
        out_shape=tuple(jax.ShapeDtypeStruct(array.shape, array.dtype) for array in arrays)
        + (jax.ShapeDtypeStruct((3, 3, chans), jnp.float32), jax.ShapeDtypeStruct((7, chans), jnp.float32)),
        in_specs=[any_space] * 4 + [vmem_space],
        out_specs=(any_space,) * 4 + (vmem_space,) * 2,
        scratch_shapes=[pltpu.VMEM(array.shape, array.dtype) for array in arrays] + [pltpu.SemaphoreType.DMA((2, 4))],
        compiler_params=pltpu.CompilerParams(vmem_limit_bytes=60 * 2**20),
        name="place_results",
    )(layer, grad, kinds, outer, lags)


def local(hidden_in, cotangent, norm_gain, in_weight, filter_taps, inner_taps, out_weight):
    tokens = hidden_in.shape[0] * lax.axis_size("tp")
    scale = (tokens * lax.axis_size("ctx")) ** (-0.5)
    gain = norm_gain.reshape(1, -1)
    kinds = jnp.transpose(in_weight, (1, 0, 2))
    layer_out, grad_input, grad_kinds, grad_out_weight, grad_filter, grad_inner = placed_results(
        *layer_results(hidden_in, cotangent, gain, filter_taps, inner_taps, kinds, out_weight, tokens, scale)
    )
    return (layer_out, grad_input, jnp.transpose(grad_kinds, (1, 0, 2)), grad_out_weight, grad_filter, grad_inner)


def solution(mesh):
    placed = (
        P(("ctx", "tp"), None),
        P(("ctx", "tp"), None),
        P(),
        P(None, None, "tp"),
        P(None, None, "tp"),
        P(None, "tp"),
        P("tp", None),
    )
    return jax.shard_map(
        local,
        mesh=mesh,
        in_specs=placed,
        out_specs=(
            P(("ctx", "tp"), None),
            P(("ctx", "tp"), None),
            P("ctx", None, "tp"),
            P("tp", "ctx"),
            P(None, None, "tp"),
            P(None, "tp"),
        ),
        check_vma=False,
    )
```

```python
import jax
import jax.numpy as jnp
from jax import lax
from jax.experimental import pallas as pl
from jax.experimental.pallas import tpu as pltpu
from jax.sharding import PartitionSpec as P

MESH = pl.DeviceIdType.MESH
DELTAS = (2, 1, 3, 0)


class Place:
    def __init__(self):
        ctx, tp = lax.axis_index("ctx"), lax.axis_index("tp")
        self.y, self.x_hi, self.core = ctx // 4, (ctx // 2) % 2, ctx % 2
        self.z, self.x_lo = tp // 2, tp % 2
        self.ctx, self.tp = ctx, tp

    def sibling(self):
        return (self.y * 4 + self.x_hi * 2 + 1 - self.core, self.tp)

    def along_y(self, step):
        return (((self.y + step) % 4) * 4 + self.x_hi * 2 + self.core, self.tp)

    def along_z(self, step):
        return (self.ctx, ((self.z + step) % 4) * 2 + self.x_lo)

    def along_x(self, step):
        x = (self.x_hi * 2 + self.x_lo + step) % 4
        return (self.y * 4 + (x // 2) * 2 + self.core, self.z * 2 + x % 2)

    def along_ctx(self, step):
        return ((self.ctx + step) % 16, self.tp)

    def partner(self):
        return (self.ctx, self.z * 2 + 1 - self.x_lo)

    def block(self, step, same):
        x_lo = self.x_lo if same else 1 - self.x_lo
        return ((self.z + step) % 4) * 2 + x_lo


def remote(source, target, send, recv, device):
    return pltpu.make_async_remote_copy(
        src_ref=source, dst_ref=target, send_sem=send, recv_sem=recv, device_id=device, device_id_type=MESH
    )


def tile(index, size):
    return pl.ds(pl.multiple_of(index * size, size), size)


def layer_kernel(
    scale, tokens,
    hidden, cot, gain, short_taps, inner_taps, in_w_hbm, out_w_hbm,
    layer_ref, input_ref, in_grad_ref, out_grad_ref, lag_ref,
    both, out_w, proj, edges, lags, acts, turned, part,
    sums_out, sums_in, y_out, y_in, pass_out, pass_in, x_out, x_in, tp_in, lag_sum, lag_got,
    load_sem, in_w_sem, send_sem, recv_sem, edge_send, edge_recv,
    sib_send, sib_recv, y_send, y_recv, x_send, x_recv, tp_send, tp_recv, lag_send, lag_recv,
):
    here = Place()
    block, width = hidden.shape
    chans = out_w_hbm.shape[0]
    cut = width // 16
    half = block // 2
    group = 2 * block
    wide, span = 72, 64
    steps = chans // 128
    bands = tokens // span
    step_in = 512
    x_cols = (width // 128 * 5 // 32) * 128
    bf16, f32 = jnp.bfloat16, jnp.float32

    out_load = pltpu.make_async_copy(out_w_hbm, out_w, load_sem.at[3])
    barrier = pltpu.get_barrier_semaphore()
    devices = [
        here.sibling(), here.along_y(1), here.along_y(-1), here.along_y(2), here.along_z(1), here.along_z(-1),
        here.along_x(1), here.along_x(-1), here.along_x(2), here.along_ctx(1), here.along_ctx(-1),
    ]
    for device in devices:
        pl.semaphore_signal(barrier, inc=1, device_id=device, device_id_type=MESH)

    sends = {}

    def go(name, build):
        build().start()
        sends[name] = build

    def drained(name):
        sends.pop(name)().wait_send()


    def rows_of(step, same, begin=0, size=block):
        return pl.ds(pl.multiple_of(here.block(step, same) * block + begin, size), size)

    every = pl.ds(0, width)
    by_x = pl.ds(0, x_cols)
    by_z = pl.ds(x_cols, width - x_cols)
    slot_cols = (every, every, every, by_z, by_z, every, every, every, by_x, by_x)

    def gather_copy(which, slot):
        rows, device = (
            lambda: (rows_of(0, True), here.partner()),
            lambda: (rows_of(0, True), here.along_z(1)),
            lambda: (rows_of(0, True), here.along_z(-1)),
            lambda: (rows_of(0, False), here.along_z(1)),
            lambda: (rows_of(0, False), here.along_z(-1)),
            lambda: (rows_of(-1, True, 0, half), here.along_z(1)),
            lambda: (rows_of(1, True, half, half), here.along_z(-1)),
            lambda: (rows_of(2, True), here.partner()),
            lambda: (rows_of(-1, True), here.partner()),
            lambda: (rows_of(1, True), here.partner()),
        )[slot]()
        held = both.at[which, rows, slot_cols[slot]]
        return remote(held, held, send_sem.at[which, slot], recv_sem.at[which, slot], device)

    def gather(which, slot):
        go(("gather", which, slot), lambda: gather_copy(which, slot))

    def arrived(which, slot):
        rows = (
            lambda: rows_of(0, False),
            lambda: rows_of(-1, True),
            lambda: rows_of(1, True),
            lambda: rows_of(-1, False),
            lambda: rows_of(1, False),
            lambda: rows_of(2, True, 0, half),
            lambda: rows_of(2, True, half, half),
            lambda: rows_of(2, False),
            lambda: rows_of(-1, False),
            lambda: rows_of(1, False),
        )[slot]()
        held = both.at[which, rows, slot_cols[slot]]
        remote(held, held, send_sem.at[which, slot], recv_sem.at[which, slot], here.partner()).wait_recv()


    parts = (part, out_w)

    def tp_copy(which, slot):
        source, held = parts[which], tp_in.at[which]
        first = pl.ds(0, half)
        second = pl.ds(half, half)
        rows, place, device = (
            lambda: (rows_of(2, False), held.at[0], here.partner()),
            lambda: (rows_of(1, False), held.at[1], here.along_z(1)),
            lambda: (rows_of(-1, False), held.at[2], here.along_z(-1)),
            lambda: (rows_of(2, True, 0, half), held.at[3, first], here.along_z(1)),
            lambda: (rows_of(2, True, half, half), held.at[3, second], here.along_z(-1)),
            lambda: (rows_of(1, True), held.at[4], here.along_z(1)),
            lambda: (rows_of(-1, True), held.at[5], here.along_z(-1)),
            lambda: (rows_of(0, False), held.at[6], here.partner()),
        )[slot]()
        return remote(source.at[rows], place, tp_send.at[which, slot], tp_recv.at[which, slot], device)

    def tp_go(which, slot):
        go(("tp", which, slot), lambda: tp_copy(which, slot))

    def add_rows(ref, base, length, others, size=128):
        def loop(index, carry):
            at = tile(index, size)
            rows = pl.ds(pl.multiple_of(base + index * size, size), size)
            total = ref[rows, :].astype(f32)
            for other in others:
                total = total + other[at, :].astype(f32)
            ref[rows, :] = total.astype(bf16)
            return carry

        lax.fori_loop(0, length // size, loop, 0)

    def tp_begin(which):
        for slot in range(3):
            tp_go(which, slot)

    def tp_halves(which):
        tp_copy(which, 0).wait_recv()
        add_rows(parts[which], here.block(2, True) * block, block, [tp_in.at[which, 0]], 16)
        tp_go(which, 3)
        tp_go(which, 4)

    def tp_direct(which):
        tp_copy(which, 3).wait_recv()
        add_rows(parts[which], here.block(1, True) * block, half, [tp_in.at[which, 3, pl.ds(0, half)]], 16)
        tp_go(which, 5)
        tp_copy(which, 4).wait_recv()
        add_rows(
            parts[which], here.block(-1, True) * block + half, half, [tp_in.at[which, 3, pl.ds(half, half)]], 16)
        tp_go(which, 6)

    def tp_last(which):
        tp_copy(which, 1).wait_recv()
        tp_copy(which, 2).wait_recv()
        add_rows(parts[which], here.block(0, False) * block, block, [tp_in.at[which, 1], tp_in.at[which, 2]], 16)
        tp_go(which, 7)

    def tp_total(which, index):
        at = tile(index, 16)
        rows = pl.ds(pl.multiple_of(here.tp * block + index * 16, 16), 16)
        total = parts[which][rows, :].astype(f32)
        for slot in (4, 5, 6):
            total = total + tp_in[which, slot, at, :].astype(f32)
        return at, total


    sums = (sums_out, sums_in)
    arriving = (y_out, y_in)
    passing = (pass_out, pass_in)
    crossing = (x_out, x_in)

    def halves(kind):
        size = sums[kind].shape[1] // 2
        return pl.ds(0, size), pl.ds(size, size), size

    def target(index, core):
        y = (here.y + DELTAS[index % 4]) % 4
        x_hi = 1 - here.x_hi if index < 4 else here.x_hi
        return y * 4 + x_hi * 2 + core

    def product(kind, index, core, write):
        cols = tile(target(index, core), cut)

        def one(step, carry):
            rows = tile(step, chans)
            first = 3 * chans if kind == 0 else 0
            left = turned[pl.ds(pl.multiple_of(first + step * chans, chans), chans), :]
            value = jnp.dot(left, both[1 - kind, :, cols], preferred_element_type=f32)
            write(rows, value * scale)
            return carry

        lax.fori_loop(0, (1, 3)[kind], one, 0)

    def sib_copy(kind, sib, index):
        return remote(
            sib.at[index % 4], sums[kind].at[index], sib_send.at[kind, index], sib_recv.at[kind, index],
            here.sibling())

    def for_sibling(kind, sib, index):
        if index >= 4:
            drained(("sib", kind, index - 4))

        def write(rows, value):
            sib[index % 4, rows, :] = value.astype(bf16)

        product(kind, index, 1 - here.core, write)
        go(("sib", kind, index), lambda: sib_copy(kind, sib, index))

    def for_self(kind, sib, index):
        sib_copy(kind, sib, index).wait_recv()

        def write(rows, value):
            held = sums[kind][index, rows, :].astype(f32)
            sums[kind][index, rows, :] = (held + value).astype(bf16)

        product(kind, index, here.core, write)

    def y_copy(kind, far, slot):
        upper, lower, _ = halves(kind)
        index, rows, step = (
            (0, upper, 1), (0, lower, -1), (1, lower, 1), (2, upper, -1), (1, upper, 1), (2, lower, -1)
        )[slot]
        return remote(
            sums[kind].at[far * 4 + index, rows], arriving[kind].at[far, slot],
            y_send.at[kind, far, slot], y_recv.at[kind, far, slot], here.along_y(step),
        )

    def y_go(kind, far, slot):
        go(("y", kind, far, slot), lambda: y_copy(kind, far, slot))

    def y_pass(kind, far):
        size = halves(kind)[2]
        y_copy(kind, far, 0).wait_recv()
        add_rows(sums[kind].at[far * 4 + 1], 0, size, [arriving[kind].at[far, 0]])
        y_go(kind, far, 4)
        y_copy(kind, far, 1).wait_recv()
        add_rows(sums[kind].at[far * 4 + 2], size, size, [arriving[kind].at[far, 1]])
        y_go(kind, far, 5)

    def y_done(kind, far):
        for slot in (3, 4, 2, 5):
            y_copy(kind, far, slot).wait_recv()

    def x_copy(kind, side):
        rows = halves(kind)[side]
        return remote(
            sums[kind].at[3, rows], passing[kind].at[side], x_send.at[kind, side], x_recv.at[kind, side],
            here.along_x((1, -1)[side]))

    def x_forward(kind, side):
        return remote(
            passing[kind].at[side], crossing[kind].at[side], x_send.at[kind, 2 + side], x_recv.at[kind, 2 + side],
            here.along_x((1, -1)[side]))

    def x_begin(kind):
        size = halves(kind)[2]
        y_done(kind, 0)
        add_rows(sums[kind].at[3], 0, size, [arriving[kind].at[0, 3], arriving[kind].at[0, 4]])
        go(("x", kind, 0), lambda: x_copy(kind, 0))
        add_rows(sums[kind].at[3], size, size, [arriving[kind].at[0, 2], arriving[kind].at[0, 5]])
        go(("x", kind, 1), lambda: x_copy(kind, 1))

    def x_go(kind, side):
        go(("x", kind, 2 + side), lambda: x_forward(kind, side))

    def x_on(kind):
        for side in range(2):
            x_copy(kind, side).wait_recv()
            x_go(kind, side)

    def last(kind, side):
        size = halves(kind)[2]
        begin = side * size
        others = [arriving[kind].at[1, slot] for slot in ((3, 4), (2, 5))[side]] + [crossing[kind].at[side]]
        for index in range(size // 128):
            row = begin + index * 128
            total = sums[kind][7, pl.ds(row, 128), :].astype(f32)
            for other in others:
                total = total + other[pl.ds(index * 128, 128), :].astype(f32)
            if kind == 1:
                in_grad_ref[row // chans, :, pl.ds(row % chans, 128)] = total.T.astype(bf16)
            else:
                out_grad_ref[pl.ds(row, 128), :] = total.astype(bf16)

    def lag_copy(step):
        device = (
            lambda: here.sibling(),
            lambda: here.along_x(2),
            lambda: here.along_y(1 - 2 * (here.y % 2)),
            lambda: here.along_y(2),
        )[step]()
        return remote(lag_sum.at[step], lag_got.at[step], lag_send.at[step], lag_recv.at[step], device)

    def lag_step(step):
        lag_copy(step).wait_recv()
        total = lag_sum[step] + lag_got[step]
        if step < 3:
            lag_sum[step + 1] = total
            go(("lag", step + 1), lambda: lag_copy(step + 1))
        else:
            lag_ref[...] = total

    def gather_phase(in_w):
        loads = [pltpu.make_async_copy(in_w_hbm.at[kind], in_w.at[kind], load_sem.at[kind]) for kind in range(3)]
        for copy in loads:
            copy.start()
        out_load.start()

        def normalise(index, carry):
            at = tile(index, 16)
            rows = pl.ds(pl.multiple_of(here.tp * block + index * 16, 16), 16)
            floats = hidden[at, :].astype(f32)
            factor = lax.rsqrt(jnp.mean(floats * floats, axis=-1, keepdims=True) + 1e-05)
            both[0, rows, :] = (floats * factor * gain[...]).astype(bf16)
            both[1, rows, :] = cot[at, :]
            return carry

        lax.fori_loop(0, block // 16, normalise, 0)
        pl.semaphore_wait(barrier, len(devices))

        def project(step):
            begin = ((here.z + step) % 4) * group

            def loop(kind, carry):
                value = jnp.dot(
                    both[0, pl.ds(pl.multiple_of(begin, group), group), :], in_w[kind], preferred_element_type=f32
                )
                proj[kind, pl.ds(pl.multiple_of(8 + begin, 8), group), :] = value.astype(bf16).astype(f32)
                return carry

            lax.fori_loop(0, 3, loop, 0)

        for slot in range(3):
            gather(0, slot)
        arrived(0, 1)
        gather(0, 5)
        gather(0, 8)
        arrived(0, 2)
        gather(0, 6)
        gather(0, 9)
        arrived(0, 0)
        gather(0, 3)
        gather(0, 4)
        for slot in range(3):
            gather(1, slot)
        for copy in loads:
            copy.wait()
        project(0)
        arrived(0, 5)
        arrived(0, 6)
        gather(0, 7)
        arrived(0, 3)
        arrived(0, 8)
        project(-1)
        arrived(0, 4)
        arrived(0, 9)
        project(1)
        arrived(1, 1)
        gather(1, 5)
        gather(1, 8)
        arrived(1, 2)
        gather(1, 6)
        gather(1, 9)
        arrived(0, 7)
        project(2)

    def filter_phase(query, gates, prods, grads, sib):
        def edge_copy():
            return remote(
                proj.at[:, pl.ds(tokens, 8), :], proj.at[:, pl.ds(0, 8), :], edge_send.at[0], edge_recv.at[0],
                here.along_ctx(1))

        def front_copy(which):
            first = pl.ds((0, 2)[which], 2)
            return remote(
                grads.at[first, pl.ds(0, 8), :], edges.at[first], edge_send.at[1 + which], edge_recv.at[1 + which],
                here.along_ctx(-1))

        go(("edge", 0), edge_copy)
        arrived(1, 0)
        gather(1, 3)
        gather(1, 4)
        arrived(1, 5)
        arrived(1, 6)
        gather(1, 7)

        def short(lag, kind, cols):
            return short_taps[lag, pl.ds(kind, 1), cols]

        def inner(lag, cols):
            return inner_taps[pl.ds(lag, 1), cols]

        def behind(value, count):
            return pltpu.roll(value, count, 0)

        def ahead(value, count):
            return pltpu.roll(value, wide - count, 0)

        def forward(index, carry):
            begin = pl.multiple_of((index // steps) * span, span)
            cols = tile(index % steps, 128)
            feats = []
            for kind in range(3):
                held = proj[kind, pl.ds(begin, wide), cols]
                total = short(0, kind, cols) * held
                for lag in (1, 2):
                    total = total + short(lag, kind, cols) * behind(held, lag)
                feats.append(total)
            product = feats[1] * feats[2]
            total = inner(0, cols) * product
            for lag in range(1, 7):
                total = total + inner(lag, cols) * behind(product, lag)
            rows = pl.ds(begin, span)
            query[rows, cols] = feats[0][8:]
            grads[3, rows, cols] = feats[1][8:]
            grads[2, rows, cols] = feats[2][8:]
            gates[rows, cols] = total[8:]
            prods[rows, cols] = product[8:]
            acts[rows, tile(3 * steps + index % steps, 128)] = (feats[0][8:] * total[8:]).astype(bf16)
            return carry

        lax.fori_loop(steps, bands * steps, forward, 0)
        edge_copy().wait_recv()

        @pl.when(here.ctx == 0)
        def _():
            proj[:, pl.ds(0, 8), :] = jnp.zeros((3, 8, chans), f32)

        lax.fori_loop(0, steps, forward, 0)
        go(("edge", 1), lambda: front_copy(1))
        lags[...] = jnp.zeros_like(lags)

        def turn(index, carry):
            turned[tile(index, 128), :] = acts[:, tile(index, 128)].T
            return carry

        lax.fori_loop(3 * steps, 4 * steps, turn, 0)
        out_load.wait()

        def branch_product(index, carry):
            cols = tile(index, chans)
            value = jnp.dot(acts[:, pl.ds(3 * chans, chans)], out_w[:, cols], preferred_element_type=f32)
            part[:, cols] = value.astype(bf16)
            return carry

        lax.fori_loop(0, width // chans, branch_product, 0)

        for slot in (3, 4, 7, 8, 9):
            arrived(1, slot)
        tp_begin(0)
        for_sibling(0, sib, 0)
        for_sibling(0, sib, 1)
        for_sibling(0, sib, 2)
        for_self(0, sib, 0)
        y_go(0, 0, 0)
        y_go(0, 0, 1)
        for_sibling(0, sib, 3)
        for_self(0, sib, 1)
        y_go(0, 0, 2)
        for_self(0, sib, 2)
        y_go(0, 0, 3)
        value = lax.dot_general(both[1], out_w[...], (((1,), (1,)), ((), ())), preferred_element_type=f32)
        grads[0, pl.ds(0, tokens), :] = value * query[...]
        grads[1, pl.ds(0, tokens), :] = value * gates[...]
        go(("edge", 2), lambda: front_copy(0))
        y_pass(0, 0)
        for index in range(4, 8):
            for_sibling(0, sib, index)
            for_self(0, sib, index - 1)
            if index == 5:
                y_go(0, 1, 0)
                y_go(0, 1, 1)
            if index == 6:
                y_go(0, 1, 2)
            if index == 7:
                y_go(0, 1, 3)
        for_self(0, sib, 7)

        def turn_tile(index):
            rows = tile(index // steps, 128)
            for kind in range(3):
                cols = tile(kind * steps + index % steps, 128)
                turned[cols, rows] = acts[rows, cols].T

        def backward(index, carry):
            turn_tile(jnp.maximum(index - 1, 0))
            for part_of in range(2):
                backward_band((index // steps) * 2 + part_of, index % steps)
            return carry

        def backward_band(band, column):
            begin = pl.multiple_of(band * span, span)
            cols = tile(column, 128)
            rows = pl.ds(begin, wide)
            here_rows = pl.ds(begin, span)

            def add_lag(row, value):
                lags[row, :, cols] += jnp.sum(value.reshape(span // 8, 8, 128), axis=0)

            gated = grads[0, rows, cols]
            product = prods[here_rows, cols]
            total = inner(0, cols) * gated
            add_lag(9, gated[:span] * product)
            for lag in range(1, 7):
                moved = ahead(gated, lag)
                total = total + inner(lag, cols) * moved
                add_lag(9 + lag, moved[:span] * product)
            feats = (grads[1, rows, cols], total * grads[2, rows, cols], total * grads[3, rows, cols])
            for kind in range(3):
                feat = feats[kind]
                held = proj[kind, pl.ds(pl.multiple_of(begin + 8, 8), span), cols]
                summed = short(0, kind, cols) * feat[:span]
                add_lag(kind, feat[:span] * held)
                for lag in (1, 2):
                    moved = ahead(feat, lag)[:span]
                    summed = summed + short(lag, kind, cols) * moved
                    add_lag(lag * 3 + kind, moved * held)
                acts[here_rows, tile(kind * steps + column, 128)] = summed.astype(bf16)

        tiles = (bands // 2) * steps
        lax.fori_loop(0, tiles - steps, backward, 0)
        y_pass(0, 1)
        front_copy(1).wait_recv()
        front_copy(0).wait_recv()
        grads[:, pl.ds(tokens, 8), :] = edges[...]

        @pl.when(here.ctx == 15)
        def _():
            grads[pl.ds(0, 2), pl.ds(tokens, 8), :] = jnp.zeros((2, 8, chans), f32)

        lax.fori_loop(tiles - steps, tiles, backward, 0)
        turn_tile(tiles - 1)
        lag_sum[0] = jnp.sum(lags[...], axis=1) * scale
        go(("lag", 0), lambda: lag_copy(0))
        x_begin(0)
        for index in range(3):
            drained(("edge", index))
        for index in range(4, 8):
            drained(("sib", 0, index))

    def reduce_phase(in_w, sib):
        def in_load(step, slot):
            return pltpu.make_async_copy(in_w_hbm.at[:, tile(step, step_in), :], in_w.at[slot], in_w_sem.at[slot])

        in_load(0, 0).start()
        in_load(1, 1).start()

        def gnorm_product():
            def loop(step, carry):
                slot = step % 2
                in_load(step, slot).wait()
                value = jnp.zeros((tokens, step_in), f32)
                for kind in range(3):
                    value = value + lax.dot_general(
                        acts[:, pl.ds(kind * chans, chans)], in_w[slot, kind],
                        (((1,), (1,)), ((), ())), preferred_element_type=f32,
                    )
                out_w[:, tile(step, step_in)] = value.astype(bf16)

                @pl.when(step + 2 < width // step_in)
                def _():
                    in_load(step + 2, slot).start()

                return carry

            lax.fori_loop(0, width // step_in, loop, 0)

        for_sibling(1, sib, 0)
        for_sibling(1, sib, 1)
        for_self(1, sib, 0)
        y_go(1, 0, 0)
        y_go(1, 0, 1)
        tp_halves(0)
        tp_last(0)
        for_sibling(1, sib, 2)
        for_self(1, sib, 1)
        y_go(1, 0, 2)
        for_sibling(1, sib, 3)
        for_self(1, sib, 2)
        y_go(1, 0, 3)
        lag_step(0)
        x_on(0)
        tp_direct(0)
        gnorm_product()
        tp_begin(1)
        y_pass(1, 0)
        lag_step(1)
        for index in range(4, 8):
            for_sibling(1, sib, index)
            for_self(1, sib, index - 1)
        for_self(1, sib, 7)
        for slot in range(4):
            drained(("y", 1, 0, slot))
        y_go(1, 1, 0)
        y_go(1, 1, 1)
        tp_halves(1)
        lag_step(2)
        x_begin(1)
        drained(("y", 1, 0, 4))
        drained(("y", 1, 0, 5))
        y_go(1, 1, 2)
        y_go(1, 1, 3)
        for slot in (5, 6, 7):
            tp_copy(0, slot).wait_recv()

        def layer_finish(index, carry):
            at, total = tp_total(0, index)
            layer_ref[at, :] = (hidden[at, :].astype(f32) + total).astype(bf16)
            return carry

        lax.fori_loop(0, block // 16, layer_finish, 0)
        for side in range(2):
            x_forward(0, side).wait_recv()
        y_done(0, 1)
        last(0, 0)
        last(0, 1)
        lag_step(3)
        y_pass(1, 1)
        x_on(1)
        tp_last(1)
        tp_direct(1)
        for slot in (5, 6, 7):
            tp_copy(1, slot).wait_recv()

        def input_finish(index, carry):
            at, total = tp_total(1, index)
            floats = hidden[at, :].astype(f32)
            factor = lax.rsqrt(jnp.mean(floats * floats, axis=-1, keepdims=True) + 1e-05)
            gained = total * gain[...]
            inner = jnp.mean(floats * gained, axis=-1, keepdims=True) * factor * factor * factor
            input_ref[at, :] = (cot[at, :].astype(f32) + gained * factor - floats * inner).astype(bf16)
            return carry

        lax.fori_loop(0, block // 16, input_finish, 0)
        for side in range(2):
            x_forward(1, side).wait_recv()
        y_done(1, 1)
        last(1, 0)
        last(1, 1)
        for name in list(sends):
            drained(name)

    pl.run_scoped(gather_phase, pltpu.VMEM((3, width, chans), bf16))
    pl.run_scoped(
        filter_phase,
        pltpu.VMEM((tokens, chans), f32),
        pltpu.VMEM((tokens, chans), f32),
        pltpu.VMEM((tokens, chans), f32),
        pltpu.VMEM((4, tokens + 8, chans), f32),
        pltpu.VMEM((4, chans, cut), bf16),
    )
    pl.run_scoped(
        reduce_phase, pltpu.VMEM((2, 3, step_in, chans), bf16), pltpu.VMEM((4, 3 * chans, cut), bf16)
    )


def layer_results(hidden, cot, gain, short_taps, inner_taps, in_weight, out_weight, tokens, scale):
    block, width = hidden.shape
    chans = out_weight.shape[0]
    cut = width // 16
    any_space = pl.BlockSpec(memory_space=pl.ANY)
    vmem_space = pl.BlockSpec(memory_space=pltpu.VMEM)
    bf16, f32 = jnp.bfloat16, jnp.float32
    dma = pltpu.SemaphoreType.DMA
    body = lambda *refs: layer_kernel(scale, tokens, *refs)
    return pl.pallas_call(
        body,
        out_shape=(
            jax.ShapeDtypeStruct((block, width), bf16),
            jax.ShapeDtypeStruct((block, width), bf16),
            jax.ShapeDtypeStruct((3, cut, chans), bf16),
            jax.ShapeDtypeStruct((chans, cut), bf16),
            jax.ShapeDtypeStruct((16, chans), f32),
        ),
        in_specs=[vmem_space] * 5 + [any_space] * 2,
        out_specs=(vmem_space,) * 5,
        scratch_shapes=[
            pltpu.VMEM((2, tokens, width), bf16),
            pltpu.VMEM(out_weight.shape, bf16),
            pltpu.VMEM((3, tokens + 8, chans), f32),
            pltpu.VMEM((4, 8, chans), f32),
            pltpu.VMEM((16, 8, chans), f32),
            pltpu.VMEM((tokens, 4 * chans), bf16),
            pltpu.VMEM((4 * chans, tokens), bf16),
            pltpu.VMEM((tokens, width), bf16),
            pltpu.VMEM((8, chans, cut), bf16),
            pltpu.VMEM((8, 3 * chans, cut), bf16),
            pltpu.VMEM((2, 6, chans // 2, cut), bf16),
            pltpu.VMEM((2, 6, 3 * chans // 2, cut), bf16),
            pltpu.VMEM((2, chans // 2, cut), bf16),
            pltpu.VMEM((2, 3 * chans // 2, cut), bf16),
            pltpu.VMEM((2, chans // 2, cut), bf16),
            pltpu.VMEM((2, 3 * chans // 2, cut), bf16),
            pltpu.VMEM((2, 7, block, width), bf16),
            pltpu.VMEM((4, 16, chans), f32),
            pltpu.VMEM((4, 16, chans), f32),
            dma((4,)), dma((2,)), dma((2, 10)), dma((2, 10)), dma((3,)), dma((3,)),
            dma((2, 8)), dma((2, 8)), dma((2, 2, 6)), dma((2, 2, 6)), dma((2, 4)), dma((2, 4)),
            dma((2, 8)), dma((2, 8)), dma((4,)), dma((4,)),
        ],
        compiler_params=pltpu.CompilerParams(
            collective_id=0, has_side_effects=True, vmem_limit_bytes=63 * 2**20
        ),
        name="whole_layer",
    )(hidden, cot, gain, short_taps, inner_taps, in_weight, out_weight)


def place_kernel(
    layer, grad, kinds, outer, lags, layer_to, grad_to, kinds_to, outer_to, short_to, inner_to,
    layer_at, grad_at, kinds_at, outer_at, sems,
):
    pairs = ((kinds, kinds_at, kinds_to), (layer, layer_at, layer_to), (grad, grad_at, grad_to), (outer, outer_at, outer_to))
    reads = [pltpu.make_async_copy(pair[0], pair[1], sems.at[0, index]) for index, pair in enumerate(pairs)]
    writes = [pltpu.make_async_copy(pair[1], pair[2], sems.at[1, index]) for index, pair in enumerate(pairs)]
    for copy in reads:
        copy.start()
    for lag in range(3):
        short_to[lag] = lags[pl.ds(3 * lag, 3), :]
    inner_to[...] = lags[pl.ds(9, 7), :]
    for read, write in zip(reads, writes):
        read.wait()
        write.start()
    for copy in writes:
        copy.wait()


def placed_results(layer, grad, kinds, outer, lags):
    chans = lags.shape[1]
    any_space = pl.BlockSpec(memory_space=pl.ANY)
    vmem_space = pl.BlockSpec(memory_space=pltpu.VMEM)
    arrays = (layer, grad, kinds, outer)
    return pl.pallas_call(
        place_kernel,
        out_shape=tuple(jax.ShapeDtypeStruct(array.shape, array.dtype) for array in arrays)
        + (jax.ShapeDtypeStruct((3, 3, chans), jnp.float32), jax.ShapeDtypeStruct((7, chans), jnp.float32)),
        in_specs=[any_space] * 4 + [vmem_space],
        out_specs=(any_space,) * 4 + (vmem_space,) * 2,
        scratch_shapes=[pltpu.VMEM(array.shape, array.dtype) for array in arrays] + [pltpu.SemaphoreType.DMA((2, 4))],
        compiler_params=pltpu.CompilerParams(vmem_limit_bytes=60 * 2**20),
        name="place_results",
    )(layer, grad, kinds, outer, lags)


def local(hidden_in, cotangent, norm_gain, in_weight, filter_taps, inner_taps, out_weight):
    tokens = hidden_in.shape[0] * lax.axis_size("tp")
    scale = (tokens * lax.axis_size("ctx")) ** (-0.5)
    gain = norm_gain.reshape(1, -1)
    kinds = jnp.transpose(in_weight, (1, 0, 2))
    layer_out, grad_input, grad_kinds, grad_out_weight, grad_filter, grad_inner = placed_results(
        *layer_results(hidden_in, cotangent, gain, filter_taps, inner_taps, kinds, out_weight, tokens, scale)
    )
    return (layer_out, grad_input, jnp.transpose(grad_kinds, (1, 0, 2)), grad_out_weight, grad_filter, grad_inner)


def solution(mesh):
    placed = (
        P(("ctx", "tp"), None),
        P(("ctx", "tp"), None),
        P(),
        P(None, None, "tp"),
        P(None, None, "tp"),
        P(None, "tp"),
        P("tp", None),
    )
    return jax.shard_map(
        local,
        mesh=mesh,
        in_specs=placed,
        out_specs=(
            P(("ctx", "tp"), None),
            P(("ctx", "tp"), None),
            P("ctx", None, "tp"),
            P("tp", "ctx"),
            P(None, None, "tp"),
            P(None, "tp"),
        ),
        check_vma=False,
    )
```

```python
import jax
import jax.numpy as jnp
from jax import lax
from jax.experimental import pallas as pl
from jax.experimental.pallas import tpu as pltpu
from jax.sharding import PartitionSpec as P

MESH = pl.DeviceIdType.MESH
DELTAS = (2, 1, 3, 0)


class Place:
    def __init__(self):
        ctx, tp = lax.axis_index("ctx"), lax.axis_index("tp")
        self.y, self.x_hi, self.core = ctx // 4, (ctx // 2) % 2, ctx % 2
        self.z, self.x_lo = tp // 2, tp % 2
        self.ctx, self.tp = ctx, tp

    def sibling(self):
        return (self.y * 4 + self.x_hi * 2 + 1 - self.core, self.tp)

    def along_y(self, step):
        return (((self.y + step) % 4) * 4 + self.x_hi * 2 + self.core, self.tp)

    def along_z(self, step):
        return (self.ctx, ((self.z + step) % 4) * 2 + self.x_lo)

    def along_x(self, step):
        x = (self.x_hi * 2 + self.x_lo + step) % 4
        return (self.y * 4 + (x // 2) * 2 + self.core, self.z * 2 + x % 2)

    def along_ctx(self, step):
        return ((self.ctx + step) % 16, self.tp)

    def partner(self):
        return (self.ctx, self.z * 2 + 1 - self.x_lo)

    def block(self, step, same):
        x_lo = self.x_lo if same else 1 - self.x_lo
        return ((self.z + step) % 4) * 2 + x_lo


def remote(source, target, send, recv, device):
    return pltpu.make_async_remote_copy(
        src_ref=source, dst_ref=target, send_sem=send, recv_sem=recv, device_id=device, device_id_type=MESH
    )


def tile(index, size):
    return pl.ds(pl.multiple_of(index * size, size), size)


def layer_kernel(
    scale, tokens,
    hidden, cot, gain, short_taps, inner_taps, in_w_hbm, out_w_hbm,
    layer_ref, input_ref, in_grad_ref, out_grad_ref, lag_ref,
    both, out_w, proj, edges, lags, acts, turned, part,
    sums_out, sums_in, y_out, y_in, pass_out, pass_in, x_out, x_in, tp_in, lag_sum, lag_got,
    load_sem, in_w_sem, send_sem, recv_sem, edge_send, edge_recv,
    sib_send, sib_recv, y_send, y_recv, x_send, x_recv, tp_send, tp_recv, lag_send, lag_recv,
):
    here = Place()
    block, width = hidden.shape
    chans = out_w_hbm.shape[0]
    cut = width // 16
    half = block // 2
    group = 2 * block
    wide, span = 72, 64
    steps = chans // 128
    bands = tokens // span
    step_in = 512
    x_cols = (width // 128 * 5 // 32) * 128
    bf16, f32 = jnp.bfloat16, jnp.float32

    out_load = pltpu.make_async_copy(out_w_hbm, out_w, load_sem.at[3])
    barrier = pltpu.get_barrier_semaphore()
    devices = [
        here.sibling(), here.along_y(1), here.along_y(-1), here.along_y(2), here.along_z(1), here.along_z(-1),
        here.along_x(1), here.along_x(-1), here.along_x(2), here.along_ctx(1), here.along_ctx(-1),
    ]
    for device in devices:
        pl.semaphore_signal(barrier, inc=1, device_id=device, device_id_type=MESH)

    sends = {}

    def go(name, build):
        build().start()
        sends[name] = build

    def drained(name):
        sends.pop(name)().wait_send()


    def rows_of(step, same, begin=0, size=block):
        return pl.ds(pl.multiple_of(here.block(step, same) * block + begin, size), size)

    every = pl.ds(0, width)
    by_x = pl.ds(0, x_cols)
    by_z = pl.ds(x_cols, width - x_cols)
    slot_cols = (every, every, every, by_z, by_z, every, every, every, by_x, by_x)

    def gather_copy(which, slot):
        rows, device = (
            lambda: (rows_of(0, True), here.partner()),
            lambda: (rows_of(0, True), here.along_z(1)),
            lambda: (rows_of(0, True), here.along_z(-1)),
            lambda: (rows_of(0, False), here.along_z(1)),
            lambda: (rows_of(0, False), here.along_z(-1)),
            lambda: (rows_of(-1, True, 0, half), here.along_z(1)),
            lambda: (rows_of(1, True, half, half), here.along_z(-1)),
            lambda: (rows_of(2, True), here.partner()),
            lambda: (rows_of(-1, True), here.partner()),
            lambda: (rows_of(1, True), here.partner()),
        )[slot]()
        held = both.at[which, rows, slot_cols[slot]]
        return remote(held, held, send_sem.at[which, slot], recv_sem.at[which, slot], device)

    def gather(which, slot):
        go(("gather", which, slot), lambda: gather_copy(which, slot))

    def arrived(which, slot):
        rows = (
            lambda: rows_of(0, False),
            lambda: rows_of(-1, True),
            lambda: rows_of(1, True),
            lambda: rows_of(-1, False),
            lambda: rows_of(1, False),
            lambda: rows_of(2, True, 0, half),
            lambda: rows_of(2, True, half, half),
            lambda: rows_of(2, False),
            lambda: rows_of(-1, False),
            lambda: rows_of(1, False),
        )[slot]()
        held = both.at[which, rows, slot_cols[slot]]
        remote(held, held, send_sem.at[which, slot], recv_sem.at[which, slot], here.partner()).wait_recv()


    parts = (part, out_w)

    def tp_copy(which, slot):
        source, held = parts[which], tp_in.at[which]
        first = pl.ds(0, half)
        second = pl.ds(half, half)
        rows, place, device = (
            lambda: (rows_of(2, False), held.at[0], here.partner()),
            lambda: (rows_of(1, False), held.at[1], here.along_z(1)),
            lambda: (rows_of(-1, False), held.at[2], here.along_z(-1)),
            lambda: (rows_of(2, True, 0, half), held.at[3, first], here.along_z(1)),
            lambda: (rows_of(2, True, half, half), held.at[3, second], here.along_z(-1)),
            lambda: (rows_of(1, True), held.at[4], here.along_z(1)),
            lambda: (rows_of(-1, True), held.at[5], here.along_z(-1)),
            lambda: (rows_of(0, False), held.at[6], here.partner()),
        )[slot]()
        return remote(source.at[rows], place, tp_send.at[which, slot], tp_recv.at[which, slot], device)

    def tp_go(which, slot):
        go(("tp", which, slot), lambda: tp_copy(which, slot))

    def add_rows(ref, base, length, others, size=128):
        def loop(index, carry):
            at = tile(index, size)
            rows = pl.ds(pl.multiple_of(base + index * size, size), size)
            total = ref[rows, :].astype(f32)
            for other in others:
                total = total + other[at, :].astype(f32)
            ref[rows, :] = total.astype(bf16)
            return carry

        lax.fori_loop(0, length // size, loop, 0)

    def tp_begin(which):
        for slot in range(3):
            tp_go(which, slot)

    def tp_halves(which):
        tp_copy(which, 0).wait_recv()
        add_rows(parts[which], here.block(2, True) * block, block, [tp_in.at[which, 0]], 16)
        tp_go(which, 3)
        tp_go(which, 4)

    def tp_direct(which):
        tp_copy(which, 3).wait_recv()
        add_rows(parts[which], here.block(1, True) * block, half, [tp_in.at[which, 3, pl.ds(0, half)]], 16)
        tp_go(which, 5)
        tp_copy(which, 4).wait_recv()
        add_rows(
            parts[which], here.block(-1, True) * block + half, half, [tp_in.at[which, 3, pl.ds(half, half)]], 16)
        tp_go(which, 6)

    def tp_last(which):
        tp_copy(which, 1).wait_recv()
        tp_copy(which, 2).wait_recv()
        add_rows(parts[which], here.block(0, False) * block, block, [tp_in.at[which, 1], tp_in.at[which, 2]], 16)
        tp_go(which, 7)

    def tp_total(which, index):
        at = tile(index, 16)
        rows = pl.ds(pl.multiple_of(here.tp * block + index * 16, 16), 16)
        total = parts[which][rows, :].astype(f32)
        for slot in (4, 5, 6):
            total = total + tp_in[which, slot, at, :].astype(f32)
        return at, total


    sums = (sums_out, sums_in)
    arriving = (y_out, y_in)
    passing = (pass_out, pass_in)
    crossing = (x_out, x_in)

    def halves(kind):
        size = sums[kind].shape[1] // 2
        return pl.ds(0, size), pl.ds(size, size), size

    def target(index, core):
        y = (here.y + DELTAS[index % 4]) % 4
        x_hi = 1 - here.x_hi if index < 4 else here.x_hi
        return y * 4 + x_hi * 2 + core

    def product(kind, index, core, write):
        cols = tile(target(index, core), cut)

        def one(step, carry):
            rows = tile(step, chans)
            first = 3 * chans if kind == 0 else 0
            left = turned[pl.ds(pl.multiple_of(first + step * chans, chans), chans), :]
            value = jnp.dot(left, both[1 - kind, :, cols], preferred_element_type=f32)
            write(rows, value * scale)
            return carry

        lax.fori_loop(0, (1, 3)[kind], one, 0)

    def sib_copy(kind, sib, index):
        return remote(
            sib.at[index % 4], sums[kind].at[index], sib_send.at[kind, index], sib_recv.at[kind, index],
            here.sibling())

    def for_sibling(kind, sib, index):
        if index >= 4:
            drained(("sib", kind, index - 4))

        def write(rows, value):
            sib[index % 4, rows, :] = value.astype(bf16)

        product(kind, index, 1 - here.core, write)
        go(("sib", kind, index), lambda: sib_copy(kind, sib, index))

    def for_self(kind, sib, index):
        sib_copy(kind, sib, index).wait_recv()

        def write(rows, value):
            held = sums[kind][index, rows, :].astype(f32)
            sums[kind][index, rows, :] = (held + value).astype(bf16)

        product(kind, index, here.core, write)

    def y_copy(kind, far, slot):
        upper, lower, _ = halves(kind)
        index, rows, step = (
            (0, upper, 1), (0, lower, -1), (1, lower, 1), (2, upper, -1), (1, upper, 1), (2, lower, -1)
        )[slot]
        return remote(
            sums[kind].at[far * 4 + index, rows], arriving[kind].at[far, slot],
            y_send.at[kind, far, slot], y_recv.at[kind, far, slot], here.along_y(step),
        )

    def y_go(kind, far, slot):
        go(("y", kind, far, slot), lambda: y_copy(kind, far, slot))

    def y_pass(kind, far):
        size = halves(kind)[2]
        y_copy(kind, far, 0).wait_recv()
        add_rows(sums[kind].at[far * 4 + 1], 0, size, [arriving[kind].at[far, 0]])
        y_go(kind, far, 4)
        y_copy(kind, far, 1).wait_recv()
        add_rows(sums[kind].at[far * 4 + 2], size, size, [arriving[kind].at[far, 1]])
        y_go(kind, far, 5)

    def y_done(kind, far):
        for slot in (3, 4, 2, 5):
            y_copy(kind, far, slot).wait_recv()

    def x_copy(kind, side):
        rows = halves(kind)[side]
        return remote(
            sums[kind].at[3, rows], passing[kind].at[side], x_send.at[kind, side], x_recv.at[kind, side],
            here.along_x((1, -1)[side]))

    def x_forward(kind, side):
        return remote(
            passing[kind].at[side], crossing[kind].at[side], x_send.at[kind, 2 + side], x_recv.at[kind, 2 + side],
            here.along_x((1, -1)[side]))

    def x_begin(kind):
        size = halves(kind)[2]
        y_done(kind, 0)
        add_rows(sums[kind].at[3], 0, size, [arriving[kind].at[0, 3], arriving[kind].at[0, 4]])
        go(("x", kind, 0), lambda: x_copy(kind, 0))
        add_rows(sums[kind].at[3], size, size, [arriving[kind].at[0, 2], arriving[kind].at[0, 5]])
        go(("x", kind, 1), lambda: x_copy(kind, 1))

    def x_go(kind, side):
        go(("x", kind, 2 + side), lambda: x_forward(kind, side))

    def x_on(kind):
        for side in range(2):
            x_copy(kind, side).wait_recv()
            x_go(kind, side)

    def last(kind, side):
        size = halves(kind)[2]
        begin = side * size
        others = [arriving[kind].at[1, slot] for slot in ((3, 4), (2, 5))[side]] + [crossing[kind].at[side]]
        for index in range(size // 128):
            row = begin + index * 128
            total = sums[kind][7, pl.ds(row, 128), :].astype(f32)
            for other in others:
                total = total + other[pl.ds(index * 128, 128), :].astype(f32)
            if kind == 1:
                in_grad_ref[row // chans, :, pl.ds(row % chans, 128)] = total.T.astype(bf16)
            else:
                out_grad_ref[pl.ds(row, 128), :] = total.astype(bf16)

    def lag_copy(step):
        device = (
            lambda: here.sibling(),
            lambda: here.along_x(2),
            lambda: here.along_y(1 - 2 * (here.y % 2)),
            lambda: here.along_y(2),
        )[step]()
        return remote(lag_sum.at[step], lag_got.at[step], lag_send.at[step], lag_recv.at[step], device)

    def lag_step(step):
        lag_copy(step).wait_recv()
        total = lag_sum[step] + lag_got[step]
        if step < 3:
            lag_sum[step + 1] = total
            go(("lag", step + 1), lambda: lag_copy(step + 1))
        else:
            lag_ref[...] = total

    def gather_phase(in_w):
        loads = [pltpu.make_async_copy(in_w_hbm.at[kind], in_w.at[kind], load_sem.at[kind]) for kind in range(3)]
        for copy in loads:
            copy.start()
        out_load.start()

        def normalise(index, carry):
            at = tile(index, 16)
            rows = pl.ds(pl.multiple_of(here.tp * block + index * 16, 16), 16)
            floats = hidden[at, :].astype(f32)
            factor = lax.rsqrt(jnp.mean(floats * floats, axis=-1, keepdims=True) + 1e-05)
            both[0, rows, :] = (floats * factor * gain[...]).astype(bf16)
            both[1, rows, :] = cot[at, :]
            return carry

        lax.fori_loop(0, block // 16, normalise, 0)
        pl.semaphore_wait(barrier, len(devices))

        def project(step):
            begin = ((here.z + step) % 4) * group

            def loop(kind, carry):
                value = jnp.dot(
                    both[0, pl.ds(pl.multiple_of(begin, group), group), :], in_w[kind], preferred_element_type=f32
                )
                proj[kind, pl.ds(pl.multiple_of(8 + begin, 8), group), :] = value.astype(bf16).astype(f32)
                return carry

            lax.fori_loop(0, 3, loop, 0)

        for slot in range(3):
            gather(0, slot)
        arrived(0, 1)
        gather(0, 5)
        gather(0, 8)
        arrived(0, 2)
        gather(0, 6)
        gather(0, 9)
        arrived(0, 0)
        gather(0, 3)
        gather(0, 4)
        for slot in range(3):
            gather(1, slot)
        for copy in loads:
            copy.wait()
        project(0)
        arrived(0, 5)
        arrived(0, 6)
        gather(0, 7)
        arrived(0, 3)
        arrived(0, 8)
        project(-1)
        arrived(0, 4)
        arrived(0, 9)
        project(1)
        arrived(1, 1)
        gather(1, 5)
        gather(1, 8)
        arrived(1, 2)
        gather(1, 6)
        gather(1, 9)
        arrived(0, 7)
        project(2)

    def filter_phase(query, gates, prods, grads, sib):
        def edge_copy():
            return remote(
                proj.at[:, pl.ds(tokens, 8), :], proj.at[:, pl.ds(0, 8), :], edge_send.at[0], edge_recv.at[0],
                here.along_ctx(1))

        def front_copy(which):
            first = pl.ds((0, 2)[which], 2)
            return remote(
                grads.at[first, pl.ds(0, 8), :], edges.at[first], edge_send.at[1 + which], edge_recv.at[1 + which],
                here.along_ctx(-1))

        go(("edge", 0), edge_copy)
        arrived(1, 0)
        gather(1, 3)
        gather(1, 4)
        arrived(1, 5)
        arrived(1, 6)
        gather(1, 7)

        def short(lag, kind, cols):
            return short_taps[lag, pl.ds(kind, 1), cols]

        def inner(lag, cols):
            return inner_taps[pl.ds(lag, 1), cols]

        def behind(value, count):
            return pltpu.roll(value, count, 0)

        def ahead(value, count):
            return pltpu.roll(value, wide - count, 0)

        def forward(index, carry):
            begin = pl.multiple_of((index // steps) * span, span)
            cols = tile(index % steps, 128)
            feats = []
            for kind in range(3):
                held = proj[kind, pl.ds(begin, wide), cols]
                total = short(0, kind, cols) * held
                for lag in (1, 2):
                    total = total + short(lag, kind, cols) * behind(held, lag)
                feats.append(total)
            product = feats[1] * feats[2]
            total = inner(0, cols) * product
            for lag in range(1, 7):
                total = total + inner(lag, cols) * behind(product, lag)
            rows = pl.ds(begin, span)
            query[rows, cols] = feats[0][8:]
            grads[3, rows, cols] = feats[1][8:]
            grads[2, rows, cols] = feats[2][8:]
            gates[rows, cols] = total[8:]
            prods[rows, cols] = product[8:]
            acts[rows, tile(3 * steps + index % steps, 128)] = (feats[0][8:] * total[8:]).astype(bf16)
            return carry

        lax.fori_loop(steps, bands * steps, forward, 0)
        edge_copy().wait_recv()

        @pl.when(here.ctx == 0)
        def _():
            proj[:, pl.ds(0, 8), :] = jnp.zeros((3, 8, chans), f32)

        lax.fori_loop(0, steps, forward, 0)
        go(("edge", 1), lambda: front_copy(1))
        lags[...] = jnp.zeros_like(lags)

        def turn(index, carry):
            turned[tile(index, 128), :] = acts[:, tile(index, 128)].T
            return carry

        lax.fori_loop(3 * steps, 4 * steps, turn, 0)
        out_load.wait()

        def branch_product(index, carry):
            cols = tile(index, chans)
            value = jnp.dot(acts[:, pl.ds(3 * chans, chans)], out_w[:, cols], preferred_element_type=f32)
            part[:, cols] = value.astype(bf16)
            return carry

        lax.fori_loop(0, width // chans, branch_product, 0)

        for slot in (3, 4, 7, 8, 9):
            arrived(1, slot)
        tp_begin(0)
        for_sibling(0, sib, 0)
        for_sibling(0, sib, 1)
        for_sibling(0, sib, 2)
        for_self(0, sib, 0)
        y_go(0, 0, 0)
        y_go(0, 0, 1)
        for_sibling(0, sib, 3)
        for_self(0, sib, 1)
        y_go(0, 0, 2)
        for_self(0, sib, 2)
        y_go(0, 0, 3)
        value = lax.dot_general(both[1], out_w[...], (((1,), (1,)), ((), ())), preferred_element_type=f32)
        grads[0, pl.ds(0, tokens), :] = value * query[...]
        grads[1, pl.ds(0, tokens), :] = value * gates[...]
        go(("edge", 2), lambda: front_copy(0))
        y_pass(0, 0)
        for index in range(4, 8):
            for_sibling(0, sib, index)
            for_self(0, sib, index - 1)
            if index == 5:
                y_go(0, 1, 0)
                y_go(0, 1, 1)
            if index == 6:
                y_go(0, 1, 2)
            if index == 7:
                y_go(0, 1, 3)
        for_self(0, sib, 7)

        def turn_tile(index):
            rows = tile(index // steps, 128)
            for kind in range(3):
                cols = tile(kind * steps + index % steps, 128)
                turned[cols, rows] = acts[rows, cols].T

        def backward(index, carry):
            turn_tile(jnp.maximum(index - 1, 0))
            for part_of in range(2):
                backward_band((index // steps) * 2 + part_of, index % steps)
            return carry

        def backward_band(band, column):
            begin = pl.multiple_of(band * span, span)
            cols = tile(column, 128)
            rows = pl.ds(begin, wide)
            here_rows = pl.ds(begin, span)

            def add_lag(row, value):
                lags[row, :, cols] += jnp.sum(value.reshape(span // 8, 8, 128), axis=0)

            gated = grads[0, rows, cols]
            product = prods[here_rows, cols]
            total = inner(0, cols) * gated
            add_lag(9, gated[:span] * product)
            for lag in range(1, 7):
                moved = ahead(gated, lag)
                total = total + inner(lag, cols) * moved
                add_lag(9 + lag, moved[:span] * product)
            feats = (grads[1, rows, cols], total * grads[2, rows, cols], total * grads[3, rows, cols])
            for kind in range(3):
                feat = feats[kind]
                held = proj[kind, pl.ds(pl.multiple_of(begin + 8, 8), span), cols]
                summed = short(0, kind, cols) * feat[:span]
                add_lag(kind, feat[:span] * held)
                for lag in (1, 2):
                    moved = ahead(feat, lag)[:span]
                    summed = summed + short(lag, kind, cols) * moved
                    add_lag(lag * 3 + kind, moved * held)
                acts[here_rows, tile(kind * steps + column, 128)] = summed.astype(bf16)

        tiles = (bands // 2) * steps
        lax.fori_loop(0, tiles - steps, backward, 0)
        y_pass(0, 1)
        tp_halves(0)
        tp_last(0)
        front_copy(1).wait_recv()
        front_copy(0).wait_recv()
        grads[:, pl.ds(tokens, 8), :] = edges[...]

        @pl.when(here.ctx == 15)
        def _():
            grads[pl.ds(0, 2), pl.ds(tokens, 8), :] = jnp.zeros((2, 8, chans), f32)

        lax.fori_loop(tiles - steps, tiles, backward, 0)
        turn_tile(tiles - 1)
        lag_sum[0] = jnp.sum(lags[...], axis=1) * scale
        go(("lag", 0), lambda: lag_copy(0))
        x_begin(0)
        for index in range(3):
            drained(("edge", index))
        for index in range(4, 8):
            drained(("sib", 0, index))

    def reduce_phase(in_w, sib):
        def in_load(step, slot):
            return pltpu.make_async_copy(in_w_hbm.at[:, tile(step, step_in), :], in_w.at[slot], in_w_sem.at[slot])

        in_load(0, 0).start()
        in_load(1, 1).start()

        def gnorm_product():
            def loop(step, carry):
                slot = step % 2
                in_load(step, slot).wait()
                value = jnp.zeros((tokens, step_in), f32)
                for kind in range(3):
                    value = value + lax.dot_general(
                        acts[:, pl.ds(kind * chans, chans)], in_w[slot, kind],
                        (((1,), (1,)), ((), ())), preferred_element_type=f32,
                    )
                out_w[:, tile(step, step_in)] = value.astype(bf16)

                @pl.when(step + 2 < width // step_in)
                def _():
                    in_load(step + 2, slot).start()

                return carry

            lax.fori_loop(0, width // step_in, loop, 0)

        for_sibling(1, sib, 0)
        for_sibling(1, sib, 1)
        for_self(1, sib, 0)
        y_go(1, 0, 0)
        y_go(1, 0, 1)
        tp_direct(0)
        for_sibling(1, sib, 2)
        for_self(1, sib, 1)
        y_go(1, 0, 2)
        for_sibling(1, sib, 3)
        for_self(1, sib, 2)
        y_go(1, 0, 3)
        lag_step(0)
        x_on(0)
        gnorm_product()
        tp_begin(1)
        y_pass(1, 0)
        lag_step(1)
        for index in range(4, 8):
            for_sibling(1, sib, index)
            for_self(1, sib, index - 1)
        for_self(1, sib, 7)
        for slot in range(4):
            drained(("y", 1, 0, slot))
        y_go(1, 1, 0)
        y_go(1, 1, 1)
        tp_halves(1)
        tp_last(1)
        lag_step(2)
        x_begin(1)
        drained(("y", 1, 0, 4))
        drained(("y", 1, 0, 5))
        y_go(1, 1, 2)
        y_go(1, 1, 3)
        for slot in (5, 6, 7):
            tp_copy(0, slot).wait_recv()

        def layer_finish(index, carry):
            at, total = tp_total(0, index)
            layer_ref[at, :] = (hidden[at, :].astype(f32) + total).astype(bf16)
            return carry

        lax.fori_loop(0, block // 16, layer_finish, 0)
        tp_direct(1)
        for side in range(2):
            x_forward(0, side).wait_recv()
        y_done(0, 1)
        last(0, 0)
        last(0, 1)
        lag_step(3)
        y_pass(1, 1)
        x_on(1)
        for slot in (5, 6, 7):
            tp_copy(1, slot).wait_recv()

        def input_finish(index, carry):
            at, total = tp_total(1, index)
            floats = hidden[at, :].astype(f32)
            factor = lax.rsqrt(jnp.mean(floats * floats, axis=-1, keepdims=True) + 1e-05)
            gained = total * gain[...]
            inner = jnp.mean(floats * gained, axis=-1, keepdims=True) * factor * factor * factor
            input_ref[at, :] = (cot[at, :].astype(f32) + gained * factor - floats * inner).astype(bf16)
            return carry

        lax.fori_loop(0, block // 16, input_finish, 0)
        for side in range(2):
            x_forward(1, side).wait_recv()
        y_done(1, 1)
        last(1, 0)
        last(1, 1)
        for name in list(sends):
            drained(name)

    pl.run_scoped(gather_phase, pltpu.VMEM((3, width, chans), bf16))
    pl.run_scoped(
        filter_phase,
        pltpu.VMEM((tokens, chans), f32),
        pltpu.VMEM((tokens, chans), f32),
        pltpu.VMEM((tokens, chans), f32),
        pltpu.VMEM((4, tokens + 8, chans), f32),
        pltpu.VMEM((4, chans, cut), bf16),
    )
    pl.run_scoped(
        reduce_phase, pltpu.VMEM((2, 3, step_in, chans), bf16), pltpu.VMEM((4, 3 * chans, cut), bf16)
    )


def layer_results(hidden, cot, gain, short_taps, inner_taps, in_weight, out_weight, tokens, scale):
    block, width = hidden.shape
    chans = out_weight.shape[0]
    cut = width // 16
    any_space = pl.BlockSpec(memory_space=pl.ANY)
    vmem_space = pl.BlockSpec(memory_space=pltpu.VMEM)
    bf16, f32 = jnp.bfloat16, jnp.float32
    dma = pltpu.SemaphoreType.DMA
    body = lambda *refs: layer_kernel(scale, tokens, *refs)
    return pl.pallas_call(
        body,
        out_shape=(
            jax.ShapeDtypeStruct((block, width), bf16),
            jax.ShapeDtypeStruct((block, width), bf16),
            jax.ShapeDtypeStruct((3, cut, chans), bf16),
            jax.ShapeDtypeStruct((chans, cut), bf16),
            jax.ShapeDtypeStruct((16, chans), f32),
        ),
        in_specs=[vmem_space] * 5 + [any_space] * 2,
        out_specs=(vmem_space,) * 5,
        scratch_shapes=[
            pltpu.VMEM((2, tokens, width), bf16),
            pltpu.VMEM(out_weight.shape, bf16),
            pltpu.VMEM((3, tokens + 8, chans), f32),
            pltpu.VMEM((4, 8, chans), f32),
            pltpu.VMEM((16, 8, chans), f32),
            pltpu.VMEM((tokens, 4 * chans), bf16),
            pltpu.VMEM((4 * chans, tokens), bf16),
            pltpu.VMEM((tokens, width), bf16),
            pltpu.VMEM((8, chans, cut), bf16),
            pltpu.VMEM((8, 3 * chans, cut), bf16),
            pltpu.VMEM((2, 6, chans // 2, cut), bf16),
            pltpu.VMEM((2, 6, 3 * chans // 2, cut), bf16),
            pltpu.VMEM((2, chans // 2, cut), bf16),
            pltpu.VMEM((2, 3 * chans // 2, cut), bf16),
            pltpu.VMEM((2, chans // 2, cut), bf16),
            pltpu.VMEM((2, 3 * chans // 2, cut), bf16),
            pltpu.VMEM((2, 7, block, width), bf16),
            pltpu.VMEM((4, 16, chans), f32),
            pltpu.VMEM((4, 16, chans), f32),
            dma((4,)), dma((2,)), dma((2, 10)), dma((2, 10)), dma((3,)), dma((3,)),
            dma((2, 8)), dma((2, 8)), dma((2, 2, 6)), dma((2, 2, 6)), dma((2, 4)), dma((2, 4)),
            dma((2, 8)), dma((2, 8)), dma((4,)), dma((4,)),
        ],
        compiler_params=pltpu.CompilerParams(
            collective_id=0, has_side_effects=True, vmem_limit_bytes=63 * 2**20
        ),
        name="whole_layer",
    )(hidden, cot, gain, short_taps, inner_taps, in_weight, out_weight)


def place_kernel(
    layer, grad, kinds, outer, lags, layer_to, grad_to, kinds_to, outer_to, short_to, inner_to,
    layer_at, grad_at, kinds_at, outer_at, sems,
):
    pairs = ((kinds, kinds_at, kinds_to), (layer, layer_at, layer_to), (grad, grad_at, grad_to), (outer, outer_at, outer_to))
    reads = [pltpu.make_async_copy(pair[0], pair[1], sems.at[0, index]) for index, pair in enumerate(pairs)]
    writes = [pltpu.make_async_copy(pair[1], pair[2], sems.at[1, index]) for index, pair in enumerate(pairs)]
    for copy in reads:
        copy.start()
    for lag in range(3):
        short_to[lag] = lags[pl.ds(3 * lag, 3), :]
    inner_to[...] = lags[pl.ds(9, 7), :]
    for read, write in zip(reads, writes):
        read.wait()
        write.start()
    for copy in writes:
        copy.wait()


def placed_results(layer, grad, kinds, outer, lags):
    chans = lags.shape[1]
    any_space = pl.BlockSpec(memory_space=pl.ANY)
    vmem_space = pl.BlockSpec(memory_space=pltpu.VMEM)
    arrays = (layer, grad, kinds, outer)
    return pl.pallas_call(
        place_kernel,
        out_shape=tuple(jax.ShapeDtypeStruct(array.shape, array.dtype) for array in arrays)
        + (jax.ShapeDtypeStruct((3, 3, chans), jnp.float32), jax.ShapeDtypeStruct((7, chans), jnp.float32)),
        in_specs=[any_space] * 4 + [vmem_space],
        out_specs=(any_space,) * 4 + (vmem_space,) * 2,
        scratch_shapes=[pltpu.VMEM(array.shape, array.dtype) for array in arrays] + [pltpu.SemaphoreType.DMA((2, 4))],
        compiler_params=pltpu.CompilerParams(vmem_limit_bytes=60 * 2**20),
        name="place_results",
    )(layer, grad, kinds, outer, lags)


def local(hidden_in, cotangent, norm_gain, in_weight, filter_taps, inner_taps, out_weight):
    tokens = hidden_in.shape[0] * lax.axis_size("tp")
    scale = (tokens * lax.axis_size("ctx")) ** (-0.5)
    gain = norm_gain.reshape(1, -1)
    kinds = jnp.transpose(in_weight, (1, 0, 2))
    layer_out, grad_input, grad_kinds, grad_out_weight, grad_filter, grad_inner = placed_results(
        *layer_results(hidden_in, cotangent, gain, filter_taps, inner_taps, kinds, out_weight, tokens, scale)
    )
    return (layer_out, grad_input, jnp.transpose(grad_kinds, (1, 0, 2)), grad_out_weight, grad_filter, grad_inner)


def solution(mesh):
    placed = (
        P(("ctx", "tp"), None),
        P(("ctx", "tp"), None),
        P(),
        P(None, None, "tp"),
        P(None, None, "tp"),
        P(None, "tp"),
        P("tp", None),
    )
    return jax.shard_map(
        local,
        mesh=mesh,
        in_specs=placed,
        out_specs=(
            P(("ctx", "tp"), None),
            P(("ctx", "tp"), None),
            P("ctx", None, "tp"),
            P("tp", "ctx"),
            P(None, None, "tp"),
            P(None, "tp"),
        ),
        check_vma=False,
    )
```

```python
import jax
import jax.numpy as jnp
from jax import lax
from jax.experimental import pallas as pl
from jax.experimental.pallas import tpu as pltpu
from jax.sharding import PartitionSpec as P

MESH = pl.DeviceIdType.MESH
DELTAS = (2, 1, 3, 0)


class Place:
    def __init__(self):
        ctx, tp = lax.axis_index("ctx"), lax.axis_index("tp")
        self.y, self.x_hi, self.core = ctx // 4, (ctx // 2) % 2, ctx % 2
        self.z, self.x_lo = tp // 2, tp % 2
        self.ctx, self.tp = ctx, tp

    def sibling(self):
        return (self.y * 4 + self.x_hi * 2 + 1 - self.core, self.tp)

    def along_y(self, step):
        return (((self.y + step) % 4) * 4 + self.x_hi * 2 + self.core, self.tp)

    def along_z(self, step):
        return (self.ctx, ((self.z + step) % 4) * 2 + self.x_lo)

    def along_x(self, step):
        x = (self.x_hi * 2 + self.x_lo + step) % 4
        return (self.y * 4 + (x // 2) * 2 + self.core, self.z * 2 + x % 2)

    def at(self, y, x, core):
        return (y * 4 + (x // 2) * 2 + core, self.z * 2 + x % 2)

    def partner(self):
        return self.along_x((1 - 2 * self.core) * (1 - 2 * self.x_lo))

    def last_block(self):
        x_hi, x_lo = self.x_hi, self.x_lo
        return jnp.where(self.core == 1, x_hi * x_lo + (1 - x_hi) * (1 - x_lo), x_hi)

    def following(self):
        x_hi, x_lo, core = self.x_hi, self.x_lo, self.core
        held = x_hi * x_lo + (1 - x_hi) * (1 - x_lo)
        x = (1 - core) * ((2 * x_hi + 3 * x_lo) % 4) + core * ((1 - held) * 2 + x_lo)
        return self.at((self.y + core * held) % 4, x, 1 - core)

    def preceding(self):
        x_hi, x_lo, core = self.x_hi, self.x_lo, self.core
        held = x_hi * (1 - x_lo) + (1 - x_hi) * x_lo
        x = core * (held * 2 + x_lo) + (1 - core) * (((1 - x_hi) * 2 + 2 - x_lo) % 4)
        return self.at((self.y - (1 - core) * (1 - x_hi)) % 4, x, 1 - core)

    def block(self, step, same):
        x_lo = self.x_lo if same else 1 - self.x_lo
        return ((self.z + step) % 4) * 2 + x_lo


def remote(source, target, send, recv, device):
    return pltpu.make_async_remote_copy(
        src_ref=source, dst_ref=target, send_sem=send, recv_sem=recv, device_id=device, device_id_type=MESH
    )


def tile(index, size):
    return pl.ds(pl.multiple_of(index * size, size), size)


def layer_kernel(
    scale, tokens,
    hidden, cot, gain, short_taps, inner_taps, in_w_hbm, out_w_hbm,
    layer_ref, input_ref, in_grad_ref, out_grad_ref, lag_ref,
    both, out_w, proj, first_in, before_in, last_in, after_in, lags, acts, turned, part,
    sums_out, sums_in, y_out, y_in, pass_out, pass_in, x_out, x_in, tp_in, lag_sum, lag_got,
    load_sem, in_w_sem, send_sem, recv_sem, edge_send, edge_recv,
    sib_send, sib_recv, y_send, y_recv, x_send, x_recv, tp_send, tp_recv, lag_send, lag_recv,
):
    here = Place()
    block, width = hidden.shape
    chans = out_w_hbm.shape[0]
    cut = width // 16
    half = block // 2
    group = 2 * block
    wide, span = 72, 64
    steps = chans // 128
    bands = tokens // span
    step_in = 512
    x_cols = (width // 128 * 3 // 4) * 128
    bf16, f32 = jnp.bfloat16, jnp.float32

    out_load = pltpu.make_async_copy(out_w_hbm, out_w, load_sem.at[3])
    barrier = pltpu.get_barrier_semaphore()
    devices = [
        here.sibling(), here.along_y(1), here.along_y(-1), here.along_y(2), here.along_z(1), here.along_z(-1),
        here.along_x(1), here.along_x(-1), here.along_x(2), here.following(), here.preceding(),
    ]
    for device in devices:
        pl.semaphore_signal(barrier, inc=1, device_id=device, device_id_type=MESH)

    sends = {}

    def go(name, build):
        build().start()
        sends[name] = build

    def drained(name):
        sends.pop(name)().wait_send()


    def rows_of(step, same, begin=0, size=block):
        return pl.ds(pl.multiple_of(here.block(step, same) * block + begin, size), size)

    every = pl.ds(0, width)
    by_x = pl.ds(0, x_cols)
    by_z = pl.ds(x_cols, width - x_cols)
    slot_cols = (every, every, every, by_z, by_z, every, every, every, by_x, by_x)

    def gather_copy(which, slot):
        rows, device = (
            lambda: (rows_of(0, True), here.partner()),
            lambda: (rows_of(0, True), here.along_z(1)),
            lambda: (rows_of(0, True), here.along_z(-1)),
            lambda: (rows_of(0, False), here.along_z(1)),
            lambda: (rows_of(0, False), here.along_z(-1)),
            lambda: (rows_of(-1, True, 0, half), here.along_z(1)),
            lambda: (rows_of(1, True, half, half), here.along_z(-1)),
            lambda: (rows_of(2, True), here.partner()),
            lambda: (rows_of(-1, True), here.partner()),
            lambda: (rows_of(1, True), here.partner()),
        )[slot]()
        held = both.at[which, rows, slot_cols[slot]]
        return remote(held, held, send_sem.at[which, slot], recv_sem.at[which, slot], device)

    def gather(which, slot):
        go(("gather", which, slot), lambda: gather_copy(which, slot))

    def arrived(which, slot):
        rows = (
            lambda: rows_of(0, False),
            lambda: rows_of(-1, True),
            lambda: rows_of(1, True),
            lambda: rows_of(-1, False),
            lambda: rows_of(1, False),
            lambda: rows_of(2, True, 0, half),
            lambda: rows_of(2, True, half, half),
            lambda: rows_of(2, False),
            lambda: rows_of(-1, False),
            lambda: rows_of(1, False),
        )[slot]()
        held = both.at[which, rows, slot_cols[slot]]
        remote(held, held, send_sem.at[which, slot], recv_sem.at[which, slot], here.partner()).wait_recv()


    parts = (part, out_w)

    def tp_copy(which, slot):
        source, held = parts[which], tp_in.at[which]
        first = pl.ds(0, half)
        second = pl.ds(half, half)
        rows, place, device = (
            lambda: (rows_of(2, False), held.at[0], here.partner()),
            lambda: (rows_of(1, False), held.at[1], here.along_z(1)),
            lambda: (rows_of(-1, False), held.at[2], here.along_z(-1)),
            lambda: (rows_of(2, True, 0, half), held.at[3, first], here.along_z(1)),
            lambda: (rows_of(2, True, half, half), held.at[3, second], here.along_z(-1)),
            lambda: (rows_of(1, True), held.at[4], here.along_z(1)),
            lambda: (rows_of(-1, True), held.at[5], here.along_z(-1)),
            lambda: (rows_of(0, False), held.at[6], here.partner()),
        )[slot]()
        return remote(source.at[rows], place, tp_send.at[which, slot], tp_recv.at[which, slot], device)

    def tp_go(which, slot):
        go(("tp", which, slot), lambda: tp_copy(which, slot))

    def add_rows(ref, base, length, others, size=128):
        def loop(index, carry):
            at = tile(index, size)
            rows = pl.ds(pl.multiple_of(base + index * size, size), size)
            total = ref[rows, :].astype(f32)
            for other in others:
                total = total + other[at, :].astype(f32)
            ref[rows, :] = total.astype(bf16)
            return carry

        lax.fori_loop(0, length // size, loop, 0)

    def tp_begin(which):
        for slot in range(3):
            tp_go(which, slot)

    def tp_halves(which):
        tp_copy(which, 0).wait_recv()
        add_rows(parts[which], here.block(2, True) * block, block, [tp_in.at[which, 0]], 16)
        tp_go(which, 3)
        tp_go(which, 4)

    def tp_direct(which):
        tp_copy(which, 3).wait_recv()
        add_rows(parts[which], here.block(1, True) * block, half, [tp_in.at[which, 3, pl.ds(0, half)]], 16)
        tp_go(which, 5)
        tp_copy(which, 4).wait_recv()
        add_rows(
            parts[which], here.block(-1, True) * block + half, half, [tp_in.at[which, 3, pl.ds(half, half)]], 16)
        tp_go(which, 6)

    def tp_last(which):
        tp_copy(which, 1).wait_recv()
        tp_copy(which, 2).wait_recv()
        add_rows(parts[which], here.block(0, False) * block, block, [tp_in.at[which, 1], tp_in.at[which, 2]], 16)
        tp_go(which, 7)

    def tp_total(which, index):
        at = tile(index, 16)
        rows = pl.ds(pl.multiple_of(here.tp * block + index * 16, 16), 16)
        total = parts[which][rows, :].astype(f32)
        for slot in (4, 5, 6):
            total = total + tp_in[which, slot, at, :].astype(f32)
        return at, total


    sums = (sums_out, sums_in)
    arriving = (y_out, y_in)
    passing = (pass_out, pass_in)
    crossing = (x_out, x_in)

    def halves(kind):
        size = sums[kind].shape[1] // 2
        return pl.ds(0, size), pl.ds(size, size), size

    def target(index, core):
        y = (here.y + DELTAS[index % 4]) % 4
        x_hi = 1 - here.x_hi if index < 4 else here.x_hi
        return y * 4 + x_hi * 2 + core

    def product(kind, index, core, write):
        cols = tile(target(index, core), cut)

        def one(step, carry):
            rows = tile(step, chans)
            first = 3 * chans if kind == 0 else 0
            left = turned[pl.ds(pl.multiple_of(first + step * chans, chans), chans), :]
            value = jnp.dot(left, both[1 - kind, :, cols], preferred_element_type=f32)
            write(rows, value * scale)
            return carry

        lax.fori_loop(0, (1, 3)[kind], one, 0)

    def sib_copy(kind, sib, index):
        return remote(
            sib.at[index % 4], sums[kind].at[index], sib_send.at[kind, index], sib_recv.at[kind, index],
            here.sibling())

    def for_sibling(kind, sib, index):
        if index >= 4:
            drained(("sib", kind, index - 4))

        def write(rows, value):
            sib[index % 4, rows, :] = value.astype(bf16)

        product(kind, index, 1 - here.core, write)
        go(("sib", kind, index), lambda: sib_copy(kind, sib, index))

    def for_self(kind, sib, index):
        sib_copy(kind, sib, index).wait_recv()

        def write(rows, value):
            held = sums[kind][index, rows, :].astype(f32)
            sums[kind][index, rows, :] = (held + value).astype(bf16)

        product(kind, index, here.core, write)

    def y_copy(kind, far, slot):
        upper, lower, _ = halves(kind)
        index, rows, step = (
            (0, upper, 1), (0, lower, -1), (1, lower, 1), (2, upper, -1), (1, upper, 1), (2, lower, -1)
        )[slot]
        return remote(
            sums[kind].at[far * 4 + index, rows], arriving[kind].at[far, slot],
            y_send.at[kind, far, slot], y_recv.at[kind, far, slot], here.along_y(step),
        )

    def y_go(kind, far, slot):
        go(("y", kind, far, slot), lambda: y_copy(kind, far, slot))

    def y_pass(kind, far):
        size = halves(kind)[2]
        y_copy(kind, far, 0).wait_recv()
        add_rows(sums[kind].at[far * 4 + 1], 0, size, [arriving[kind].at[far, 0]])
        y_go(kind, far, 4)
        y_copy(kind, far, 1).wait_recv()
        add_rows(sums[kind].at[far * 4 + 2], size, size, [arriving[kind].at[far, 1]])
        y_go(kind, far, 5)

    def y_done(kind, far):
        for slot in (3, 4, 2, 5):
            y_copy(kind, far, slot).wait_recv()

    def x_copy(kind, side):
        rows = halves(kind)[side]
        return remote(
            sums[kind].at[3, rows], passing[kind].at[side], x_send.at[kind, side], x_recv.at[kind, side],
            here.along_x((1, -1)[side]))

    def x_forward(kind, side):
        return remote(
            passing[kind].at[side], crossing[kind].at[side], x_send.at[kind, 2 + side], x_recv.at[kind, 2 + side],
            here.along_x((1, -1)[side]))

    def x_begin(kind):
        size = halves(kind)[2]
        y_done(kind, 0)
        add_rows(sums[kind].at[3], 0, size, [arriving[kind].at[0, 3], arriving[kind].at[0, 4]])
        go(("x", kind, 0), lambda: x_copy(kind, 0))
        add_rows(sums[kind].at[3], size, size, [arriving[kind].at[0, 2], arriving[kind].at[0, 5]])
        go(("x", kind, 1), lambda: x_copy(kind, 1))

    def x_go(kind, side):
        go(("x", kind, 2 + side), lambda: x_forward(kind, side))

    def x_on(kind):
        for side in range(2):
            x_copy(kind, side).wait_recv()
            x_go(kind, side)

    def last(kind, side):
        size = halves(kind)[2]
        begin = side * size
        others = [arriving[kind].at[1, slot] for slot in ((3, 4), (2, 5))[side]] + [crossing[kind].at[side]]
        for index in range(size // 128):
            row = begin + index * 128
            total = sums[kind][7, pl.ds(row, 128), :].astype(f32)
            for other in others:
                total = total + other[pl.ds(index * 128, 128), :].astype(f32)
            if kind == 1:
                in_grad_ref[row // chans, :, pl.ds(row % chans, 128)] = total.T.astype(bf16)
            else:
                out_grad_ref[pl.ds(row, 128), :] = total.astype(bf16)

    def lag_copy(step):
        device = (
            lambda: here.sibling(),
            lambda: here.along_x(2),
            lambda: here.along_y(1 - 2 * (here.y % 2)),
            lambda: here.along_y(2),
        )[step]()
        return remote(lag_sum.at[step], lag_got.at[step], lag_send.at[step], lag_recv.at[step], device)

    def lag_step(step):
        lag_copy(step).wait_recv()
        total = lag_sum[step] + lag_got[step]
        if step < 3:
            lag_sum[step + 1] = total
            go(("lag", step + 1), lambda: lag_copy(step + 1))
        else:
            lag_ref[...] = total

    def gather_phase(in_w):
        loads = [pltpu.make_async_copy(in_w_hbm.at[kind], in_w.at[kind], load_sem.at[kind]) for kind in range(3)]
        for copy in loads:
            copy.start()
        out_load.start()

        def normalise(index, carry):
            at = tile(index, 16)
            rows = pl.ds(pl.multiple_of(here.tp * block + index * 16, 16), 16)
            floats = hidden[at, :].astype(f32)
            factor = lax.rsqrt(jnp.mean(floats * floats, axis=-1, keepdims=True) + 1e-05)
            both[0, rows, :] = (floats * factor * gain[...]).astype(bf16)
            both[1, rows, :] = cot[at, :]
            return carry

        lax.fori_loop(0, block // 16, normalise, 0)
        pl.semaphore_wait(barrier, len(devices))

        def project(step):
            begin = ((here.z + step) % 4) * group

            def loop(kind, carry):
                value = jnp.dot(
                    both[0, pl.ds(pl.multiple_of(begin, group), group), :], in_w[kind], preferred_element_type=f32
                )
                value = value.astype(bf16).astype(f32)
                for index in range(2):
                    first = (begin // block + index) * wide + 8
                    proj[kind, pl.ds(pl.multiple_of(first, 8), block), :] = value[index * block : (index + 1) * block]
                return carry

            lax.fori_loop(0, 3, loop, 0)

        for slot in range(3):
            gather(0, slot)
        gather(1, 0)
        arrived(0, 1)
        gather(0, 5)
        gather(0, 8)
        arrived(0, 2)
        gather(0, 6)
        gather(0, 9)
        arrived(0, 0)
        gather(0, 3)
        gather(0, 4)
        gather(1, 1)
        gather(1, 2)
        for copy in loads:
            copy.wait()
        project(0)
        arrived(0, 5)
        arrived(0, 6)
        gather(0, 7)
        arrived(0, 3)
        arrived(0, 8)
        project(-1)
        arrived(0, 4)
        arrived(0, 9)
        project(1)
        arrived(1, 1)
        gather(1, 5)
        gather(1, 8)
        arrived(1, 2)
        gather(1, 6)
        gather(1, 9)
        arrived(1, 0)
        gather(1, 3)
        gather(1, 4)
        arrived(0, 7)
        project(2)

    def filter_phase(query, gates, prods, grads, ends, heads, sib):
        def first_copy():
            return remote(
                proj.at[:, pl.ds(7 * wide + span, 8), :], first_in, edge_send.at[0], edge_recv.at[0], here.following())

        def before_copy():
            return remote(ends, before_in, edge_send.at[1], edge_recv.at[1], here.along_x(2))

        def last_copy(which):
            kinds = pl.ds((0, 2)[which], 2)
            return remote(
                grads.at[kinds, pl.ds(0, 8), :], last_in.at[kinds], edge_send.at[2 + which], edge_recv.at[2 + which],
                here.preceding())

        def after_copy(which):
            kinds = pl.ds((0, 2)[which], 2)
            return remote(
                heads.at[kinds], after_in.at[kinds], edge_send.at[4 + which], edge_recv.at[4 + which],
                here.along_x(2))

        def edge_rows(target, kinds, source, offset):
            for kind in kinds:
                for pair in range(4):
                    rows = [source[kind, pl.ds((2 * pair + index) * wide + offset, 8), :] for index in range(2)]
                    target[kind, pl.ds(pair * 16, 16), :] = jnp.concatenate(rows).astype(bf16)

        def share(target, kinds, copy, source):
            @pl.when(here.core == 1)
            def _():
                copy().wait_recv()

            @pl.when(here.core == 0)
            def _():
                for kind in kinds:
                    target[kind] = source[kind]

        edge_rows(ends, range(3), proj, span)
        go(("edge", 0), first_copy)

        @pl.when(here.core == 1)
        def _():
            before_copy().start()

        arrived(1, 5)
        arrived(1, 6)
        gather(1, 7)
        first_copy().wait_recv()
        share(before_in, range(3), before_copy, ends)
        for kind in range(3):
            proj[kind, pl.ds(0, 8), :] = first_in[kind] * jnp.where(here.ctx == 0, 0.0, 1.0).astype(f32)
            for pair in range(4):
                rows = before_in[kind, pl.ds(pair * 16, 16), :].astype(f32)
                proj[kind, pl.ds((2 * pair + 1) * wide, 8), :] = rows[:8]
                if pair < 3:
                    proj[kind, pl.ds((2 * pair + 2) * wide, 8), :] = rows[8:]

        def short(lag, kind, cols):
            return short_taps[lag, pl.ds(kind, 1), cols]

        def inner(lag, cols):
            return inner_taps[pl.ds(lag, 1), cols]

        def behind(value, count):
            return pltpu.roll(value, count, 0)

        def ahead(value, count):
            return pltpu.roll(value, wide - count, 0)

        def forward(index, carry):
            begin = pl.multiple_of((index // steps) * span, span)
            first = pl.multiple_of((index // steps) * wide, 8)
            cols = tile(index % steps, 128)
            feats = []
            for kind in range(3):
                held = proj[kind, pl.ds(first, wide), cols]
                total = short(0, kind, cols) * held
                for lag in (1, 2):
                    total = total + short(lag, kind, cols) * behind(held, lag)
                feats.append(total)
            product = feats[1] * feats[2]
            total = inner(0, cols) * product
            for lag in range(1, 7):
                total = total + inner(lag, cols) * behind(product, lag)
            rows = pl.ds(begin, span)
            query[rows, cols] = feats[0][8:]
            grads[3, pl.ds(first, span), cols] = feats[1][8:]
            grads[2, pl.ds(first, span), cols] = feats[2][8:]
            gates[rows, cols] = total[8:]
            prods[rows, cols] = product[8:]
            acts[rows, tile(3 * steps + index % steps, 128)] = (feats[0][8:] * total[8:]).astype(bf16)
            return carry

        lax.fori_loop(0, bands * steps, forward, 0)
        edge_rows(heads, (2, 3), grads, 0)
        go(("edge", 3), lambda: last_copy(1))

        @pl.when(here.core == 1)
        def _():
            after_copy(1).start()

        lags[...] = jnp.zeros_like(lags)

        def turn(index, carry):
            turned[tile(index, 128), :] = acts[:, tile(index, 128)].T
            return carry

        lax.fori_loop(3 * steps, 4 * steps, turn, 0)
        out_load.wait()

        def branch_product(index, carry):
            cols = tile(index, chans)
            value = jnp.dot(acts[:, pl.ds(3 * chans, chans)], out_w[:, cols], preferred_element_type=f32)
            part[:, cols] = value.astype(bf16)
            return carry

        lax.fori_loop(0, width // chans, branch_product, 0)

        for slot in (3, 4, 7, 8, 9):
            arrived(1, slot)
        tp_begin(0)
        for_sibling(0, sib, 0)
        for_sibling(0, sib, 1)
        for_sibling(0, sib, 2)
        for_self(0, sib, 0)
        y_go(0, 0, 0)
        y_go(0, 0, 1)
        for_sibling(0, sib, 3)
        for_self(0, sib, 1)
        y_go(0, 0, 2)
        for_self(0, sib, 2)
        y_go(0, 0, 3)
        value = lax.dot_general(both[1], out_w[...], (((1,), (1,)), ((), ())), preferred_element_type=f32)
        for index in range(8):
            rows = pl.ds(index * span, span)
            grads[0, pl.ds(index * wide, span), :] = value[index * span : (index + 1) * span] * query[rows, :]
            grads[1, pl.ds(index * wide, span), :] = value[index * span : (index + 1) * span] * gates[rows, :]
        edge_rows(heads, (0, 1), grads, 0)
        go(("edge", 2), lambda: last_copy(0))

        @pl.when(here.core == 1)
        def _():
            after_copy(0).start()

        y_pass(0, 0)
        for index in range(4, 8):
            for_sibling(0, sib, index)
            for_self(0, sib, index - 1)
            if index == 5:
                y_go(0, 1, 0)
                y_go(0, 1, 1)
            if index == 6:
                y_go(0, 1, 2)
            if index == 7:
                y_go(0, 1, 3)
        for_self(0, sib, 7)
        for which in range(2):
            last_copy(which).wait_recv()
            share(after_in, ((0, 1), (2, 3))[which], lambda which=which: after_copy(which), heads)
        ended = (here.core == 1) & (here.y == 3) & (here.last_block() == 1)
        for kind in range(4):
            kept = jnp.where(ended, 0.0, 1.0).astype(f32) if kind < 2 else 1.0
            grads[kind, pl.ds(7 * wide + span, 8), :] = last_in[kind] * kept
            for pair in range(4):
                rows = after_in[kind, pl.ds(pair * 16, 16), :].astype(f32)
                if pair > 0:
                    grads[kind, pl.ds((2 * pair - 1) * wide + span, 8), :] = rows[:8]
                grads[kind, pl.ds(2 * pair * wide + span, 8), :] = rows[8:]

        def turn_tile(index):
            rows = tile(index // steps, 128)
            for kind in range(3):
                cols = tile(kind * steps + index % steps, 128)
                turned[cols, rows] = acts[rows, cols].T

        def backward(index, carry):
            turn_tile(jnp.maximum(index - 1, 0))
            for part_of in range(2):
                backward_band((index // steps) * 2 + part_of, index % steps)
            return carry

        def backward_band(band, column):
            begin = pl.multiple_of(band * span, span)
            first = pl.multiple_of(band * wide, 8)
            cols = tile(column, 128)
            rows = pl.ds(first, wide)
            here_rows = pl.ds(begin, span)

            def add_lag(row, value):
                lags[row, :, cols] += jnp.sum(value.reshape(span // 8, 8, 128), axis=0)

            gated = grads[0, rows, cols]
            product = prods[here_rows, cols]
            total = inner(0, cols) * gated
            add_lag(9, gated[:span] * product)
            for lag in range(1, 7):
                moved = ahead(gated, lag)
                total = total + inner(lag, cols) * moved
                add_lag(9 + lag, moved[:span] * product)
            feats = (grads[1, rows, cols], total * grads[2, rows, cols], total * grads[3, rows, cols])
            for kind in range(3):
                feat = feats[kind]
                held = proj[kind, pl.ds(pl.multiple_of(first + 8, 8), span), cols]
                summed = short(0, kind, cols) * feat[:span]
                add_lag(kind, feat[:span] * held)
                for lag in (1, 2):
                    moved = ahead(feat, lag)[:span]
                    summed = summed + short(lag, kind, cols) * moved
                    add_lag(lag * 3 + kind, moved * held)
                acts[here_rows, tile(kind * steps + column, 128)] = summed.astype(bf16)

        tiles = (bands // 2) * steps
        lax.fori_loop(0, tiles - steps, backward, 0)
        y_pass(0, 1)
        tp_halves(0)
        tp_last(0)
        lax.fori_loop(tiles - steps, tiles, backward, 0)
        turn_tile(tiles - 1)
        lag_sum[0] = jnp.sum(lags[...], axis=1) * scale
        go(("lag", 0), lambda: lag_copy(0))
        x_begin(0)
        for index in (0, 2, 3):
            drained(("edge", index))

        @pl.when(here.core == 1)
        def _():
            before_copy().wait_send()
            after_copy(0).wait_send()
            after_copy(1).wait_send()

        for index in range(4, 8):
            drained(("sib", 0, index))

    def reduce_phase(in_w, sib):
        def in_load(step, slot):
            return pltpu.make_async_copy(in_w_hbm.at[:, tile(step, step_in), :], in_w.at[slot], in_w_sem.at[slot])

        in_load(0, 0).start()
        in_load(1, 1).start()

        def gnorm_product():
            def loop(step, carry):
                slot = step % 2
                in_load(step, slot).wait()
                value = jnp.zeros((tokens, step_in), f32)
                for kind in range(3):
                    value = value + lax.dot_general(
                        acts[:, pl.ds(kind * chans, chans)], in_w[slot, kind],
                        (((1,), (1,)), ((), ())), preferred_element_type=f32,
                    )
                out_w[:, tile(step, step_in)] = value.astype(bf16)

                @pl.when(step + 2 < width // step_in)
                def _():
                    in_load(step + 2, slot).start()

                return carry

            lax.fori_loop(0, width // step_in, loop, 0)

        for_sibling(1, sib, 0)
        for_sibling(1, sib, 1)
        for_self(1, sib, 0)
        y_go(1, 0, 0)
        y_go(1, 0, 1)
        tp_direct(0)
        for_sibling(1, sib, 2)
        for_self(1, sib, 1)
        y_go(1, 0, 2)
        for_sibling(1, sib, 3)
        for_self(1, sib, 2)
        y_go(1, 0, 3)
        lag_step(0)
        x_on(0)
        gnorm_product()
        tp_begin(1)
        y_pass(1, 0)
        lag_step(1)
        for index in range(4, 8):
            for_sibling(1, sib, index)
            for_self(1, sib, index - 1)
        for_self(1, sib, 7)
        for slot in range(4):
            drained(("y", 1, 0, slot))
        y_go(1, 1, 0)
        y_go(1, 1, 1)
        tp_halves(1)
        tp_last(1)
        lag_step(2)
        x_begin(1)
        drained(("y", 1, 0, 4))
        drained(("y", 1, 0, 5))
        y_go(1, 1, 2)
        y_go(1, 1, 3)
        for slot in (5, 6, 7):
            tp_copy(0, slot).wait_recv()

        def layer_finish(index, carry):
            at, total = tp_total(0, index)
            layer_ref[at, :] = (hidden[at, :].astype(f32) + total).astype(bf16)
            return carry

        lax.fori_loop(0, block // 16, layer_finish, 0)
        tp_direct(1)
        for side in range(2):
            x_forward(0, side).wait_recv()
        y_done(0, 1)
        last(0, 0)
        last(0, 1)
        lag_step(3)
        y_pass(1, 1)
        x_on(1)
        for slot in (5, 6, 7):
            tp_copy(1, slot).wait_recv()

        def input_finish(index, carry):
            at, total = tp_total(1, index)
            floats = hidden[at, :].astype(f32)
            factor = lax.rsqrt(jnp.mean(floats * floats, axis=-1, keepdims=True) + 1e-05)
            gained = total * gain[...]
            inner = jnp.mean(floats * gained, axis=-1, keepdims=True) * factor * factor * factor
            input_ref[at, :] = (cot[at, :].astype(f32) + gained * factor - floats * inner).astype(bf16)
            return carry

        lax.fori_loop(0, block // 16, input_finish, 0)
        for side in range(2):
            x_forward(1, side).wait_recv()
        y_done(1, 1)
        last(1, 0)
        last(1, 1)
        for name in list(sends):
            drained(name)

    pl.run_scoped(gather_phase, pltpu.VMEM((3, width, chans), bf16))
    pl.run_scoped(
        filter_phase,
        pltpu.VMEM((tokens, chans), f32),
        pltpu.VMEM((tokens, chans), f32),
        pltpu.VMEM((tokens, chans), f32),
        pltpu.VMEM((4, bands * wide, chans), f32),
        pltpu.VMEM((3, bands * 8, chans), bf16),
        pltpu.VMEM((4, bands * 8, chans), bf16),
        pltpu.VMEM((4, chans, cut), bf16),
    )
    pl.run_scoped(
        reduce_phase, pltpu.VMEM((2, 3, step_in, chans), bf16), pltpu.VMEM((4, 3 * chans, cut), bf16)
    )


def layer_results(hidden, cot, gain, short_taps, inner_taps, in_weight, out_weight, tokens, scale):
    block, width = hidden.shape
    chans = out_weight.shape[0]
    cut = width // 16
    any_space = pl.BlockSpec(memory_space=pl.ANY)
    vmem_space = pl.BlockSpec(memory_space=pltpu.VMEM)
    bf16, f32 = jnp.bfloat16, jnp.float32
    dma = pltpu.SemaphoreType.DMA
    body = lambda *refs: layer_kernel(scale, tokens, *refs)
    return pl.pallas_call(
        body,
        out_shape=(
            jax.ShapeDtypeStruct((block, width), bf16),
            jax.ShapeDtypeStruct((block, width), bf16),
            jax.ShapeDtypeStruct((3, cut, chans), bf16),
            jax.ShapeDtypeStruct((chans, cut), bf16),
            jax.ShapeDtypeStruct((16, chans), f32),
        ),
        in_specs=[vmem_space] * 5 + [any_space] * 2,
        out_specs=(vmem_space,) * 5,
        scratch_shapes=[
            pltpu.VMEM((2, tokens, width), bf16),
            pltpu.VMEM(out_weight.shape, bf16),
            pltpu.VMEM((3, tokens + 64, chans), f32),
            pltpu.VMEM((3, 8, chans), f32),
            pltpu.VMEM((3, 64, chans), bf16),
            pltpu.VMEM((4, 8, chans), f32),
            pltpu.VMEM((4, 64, chans), bf16),
            pltpu.VMEM((16, 8, chans), f32),
            pltpu.VMEM((tokens, 4 * chans), bf16),
            pltpu.VMEM((4 * chans, tokens), bf16),
            pltpu.VMEM((tokens, width), bf16),
            pltpu.VMEM((8, chans, cut), bf16),
            pltpu.VMEM((8, 3 * chans, cut), bf16),
            pltpu.VMEM((2, 6, chans // 2, cut), bf16),
            pltpu.VMEM((2, 6, 3 * chans // 2, cut), bf16),
            pltpu.VMEM((2, chans // 2, cut), bf16),
            pltpu.VMEM((2, 3 * chans // 2, cut), bf16),
            pltpu.VMEM((2, chans // 2, cut), bf16),
            pltpu.VMEM((2, 3 * chans // 2, cut), bf16),
            pltpu.VMEM((2, 7, block, width), bf16),
            pltpu.VMEM((4, 16, chans), f32),
            pltpu.VMEM((4, 16, chans), f32),
            dma((4,)), dma((2,)), dma((2, 10)), dma((2, 10)), dma((6,)), dma((6,)),
            dma((2, 8)), dma((2, 8)), dma((2, 2, 6)), dma((2, 2, 6)), dma((2, 4)), dma((2, 4)),
            dma((2, 8)), dma((2, 8)), dma((4,)), dma((4,)),
        ],
        compiler_params=pltpu.CompilerParams(
            collective_id=0, has_side_effects=True, vmem_limit_bytes=63 * 2**20
        ),
        name="whole_layer",
    )(hidden, cot, gain, short_taps, inner_taps, in_weight, out_weight)


def place_kernel(
    layer, grad, kinds, outer, lags, layer_to, grad_to, kinds_to, outer_to, short_to, inner_to,
    layer_at, grad_at, kinds_at, outer_at, sems,
):
    pairs = ((kinds, kinds_at, kinds_to), (layer, layer_at, layer_to), (grad, grad_at, grad_to), (outer, outer_at, outer_to))
    reads = [pltpu.make_async_copy(pair[0], pair[1], sems.at[0, index]) for index, pair in enumerate(pairs)]
    writes = [pltpu.make_async_copy(pair[1], pair[2], sems.at[1, index]) for index, pair in enumerate(pairs)]
    for copy in reads:
        copy.start()
    for lag in range(3):
        short_to[lag] = lags[pl.ds(3 * lag, 3), :]
    inner_to[...] = lags[pl.ds(9, 7), :]
    for read, write in zip(reads, writes):
        read.wait()
        write.start()
    for copy in writes:
        copy.wait()


def placed_results(layer, grad, kinds, outer, lags):
    chans = lags.shape[1]
    any_space = pl.BlockSpec(memory_space=pl.ANY)
    vmem_space = pl.BlockSpec(memory_space=pltpu.VMEM)
    arrays = (layer, grad, kinds, outer)
    return pl.pallas_call(
        place_kernel,
        out_shape=tuple(jax.ShapeDtypeStruct(array.shape, array.dtype) for array in arrays)
        + (jax.ShapeDtypeStruct((3, 3, chans), jnp.float32), jax.ShapeDtypeStruct((7, chans), jnp.float32)),
        in_specs=[any_space] * 4 + [vmem_space],
        out_specs=(any_space,) * 4 + (vmem_space,) * 2,
        scratch_shapes=[pltpu.VMEM(array.shape, array.dtype) for array in arrays] + [pltpu.SemaphoreType.DMA((2, 4))],
        compiler_params=pltpu.CompilerParams(vmem_limit_bytes=60 * 2**20),
        name="place_results",
    )(layer, grad, kinds, outer, lags)


def local(hidden_in, cotangent, norm_gain, in_weight, filter_taps, inner_taps, out_weight):
    tokens = hidden_in.shape[0] * lax.axis_size("tp")
    scale = (tokens * lax.axis_size("ctx")) ** (-0.5)
    gain = norm_gain.reshape(1, -1)
    kinds = jnp.transpose(in_weight, (1, 0, 2))
    layer_out, grad_input, grad_kinds, grad_out_weight, grad_filter, grad_inner = placed_results(
        *layer_results(hidden_in, cotangent, gain, filter_taps, inner_taps, kinds, out_weight, tokens, scale)
    )
    return (layer_out, grad_input, jnp.transpose(grad_kinds, (1, 0, 2)), grad_out_weight, grad_filter, grad_inner)


def solution(mesh):
    placed = (
        P(("ctx", "tp"), None),
        P(("ctx", "tp"), None),
        P(),
        P(None, None, "tp"),
        P(None, None, "tp"),
        P(None, "tp"),
        P("tp", None),
    )
    return jax.shard_map(
        local,
        mesh=mesh,
        in_specs=placed,
        out_specs=(
            P(("ctx", "tp"), None),
            P(("ctx", "tp"), None),
            P("ctx", None, "tp"),
            P("tp", "ctx"),
            P(None, None, "tp"),
            P(None, "tp"),
        ),
        check_vma=False,
    )
```

```python
import jax
import jax.numpy as jnp
from jax import lax
from jax.experimental import pallas as pl
from jax.experimental.pallas import tpu as pltpu
from jax.sharding import PartitionSpec as P

MESH = pl.DeviceIdType.MESH
DELTAS = (2, 1, 3, 0)


class Place:
    def __init__(self):
        ctx, tp = lax.axis_index("ctx"), lax.axis_index("tp")
        self.y, self.x_hi, self.core = ctx // 4, (ctx // 2) % 2, ctx % 2
        self.z, self.x_lo = tp // 2, tp % 2
        self.ctx, self.tp = ctx, tp

    def sibling(self):
        return (self.y * 4 + self.x_hi * 2 + 1 - self.core, self.tp)

    def along_y(self, step):
        return (((self.y + step) % 4) * 4 + self.x_hi * 2 + self.core, self.tp)

    def along_z(self, step):
        return (self.ctx, ((self.z + step) % 4) * 2 + self.x_lo)

    def along_x(self, step):
        x = (self.x_hi * 2 + self.x_lo + step) % 4
        return (self.y * 4 + (x // 2) * 2 + self.core, self.z * 2 + x % 2)

    def at(self, y, x, core):
        return (y * 4 + (x // 2) * 2 + core, self.z * 2 + x % 2)

    def partner(self):
        return self.along_x((1 - 2 * self.core) * (1 - 2 * self.x_lo))

    def last_block(self):
        x_hi, x_lo = self.x_hi, self.x_lo
        return jnp.where(self.core == 1, x_hi * x_lo + (1 - x_hi) * (1 - x_lo), x_hi)

    def following(self):
        x_hi, x_lo, core = self.x_hi, self.x_lo, self.core
        held = x_hi * x_lo + (1 - x_hi) * (1 - x_lo)
        x = (1 - core) * ((2 * x_hi + 3 * x_lo) % 4) + core * ((1 - held) * 2 + x_lo)
        return self.at((self.y + core * held) % 4, x, 1 - core)

    def preceding(self):
        x_hi, x_lo, core = self.x_hi, self.x_lo, self.core
        held = x_hi * (1 - x_lo) + (1 - x_hi) * x_lo
        x = core * (held * 2 + x_lo) + (1 - core) * (((1 - x_hi) * 2 + 2 - x_lo) % 4)
        return self.at((self.y - (1 - core) * (1 - x_hi)) % 4, x, 1 - core)

    def block(self, step, same):
        x_lo = self.x_lo if same else 1 - self.x_lo
        return ((self.z + step) % 4) * 2 + x_lo


def remote(source, target, send, recv, device):
    return pltpu.make_async_remote_copy(
        src_ref=source, dst_ref=target, send_sem=send, recv_sem=recv, device_id=device, device_id_type=MESH
    )


def tile(index, size):
    return pl.ds(pl.multiple_of(index * size, size), size)


def layer_kernel(
    scale, tokens,
    hidden, cot, gain, short_taps, inner_taps, in_w_hbm, out_w_hbm,
    layer_ref, input_ref, in_grad_ref, out_grad_ref, lag_ref,
    both, out_w, proj, first_in, before_in, last_in, after_in, lags, acts, turned,
    sums_out, sums_in, sums_val, y_out, y_in, y_val, pass_out, pass_in, pass_val, x_out, x_in, x_val,
    tp_in, lag_sum, lag_got,
    load_sem, in_w_sem, send_sem, recv_sem, edge_send, edge_recv,
    sib_send, sib_recv, y_send, y_recv, x_send, x_recv, tp_send, tp_recv, lag_send, lag_recv,
):
    here = Place()
    block, width = hidden.shape
    chans = out_w_hbm.shape[0]
    cut = width // 16
    half = block // 2
    group = 2 * block
    wide, span = 72, 64
    steps = chans // 128
    bands = tokens // span
    step_in = 512
    x_cols = (width // 128 * 3 // 4) * 128
    bf16, f32 = jnp.bfloat16, jnp.float32

    out_load = pltpu.make_async_copy(out_w_hbm, out_w, load_sem.at[3])
    barrier = pltpu.get_barrier_semaphore()
    devices = [
        here.sibling(), here.along_y(1), here.along_y(-1), here.along_y(2), here.along_z(1), here.along_z(-1),
        here.along_x(1), here.along_x(-1), here.along_x(2), here.following(), here.preceding(),
    ]
    for device in devices:
        pl.semaphore_signal(barrier, inc=1, device_id=device, device_id_type=MESH)

    sends = {}

    def go(name, build):
        build().start()
        sends[name] = build

    def drained(name):
        sends.pop(name)().wait_send()


    def rows_of(step, same, begin=0, size=block):
        return pl.ds(pl.multiple_of(here.block(step, same) * block + begin, size), size)

    every = pl.ds(0, width)
    by_x = pl.ds(0, x_cols)
    by_z = pl.ds(x_cols, width - x_cols)
    slot_cols = (every, every, every, by_z, by_z, every, every, every, by_x, by_x)

    def gather_copy(which, slot):
        rows, device = (
            lambda: (rows_of(0, True), here.partner()),
            lambda: (rows_of(0, True), here.along_z(1)),
            lambda: (rows_of(0, True), here.along_z(-1)),
            lambda: (rows_of(0, False), here.along_z(1)),
            lambda: (rows_of(0, False), here.along_z(-1)),
            lambda: (rows_of(-1, True, 0, half), here.along_z(1)),
            lambda: (rows_of(1, True, half, half), here.along_z(-1)),
            lambda: (rows_of(2, True), here.partner()),
            lambda: (rows_of(-1, True), here.partner()),
            lambda: (rows_of(1, True), here.partner()),
        )[slot]()
        held = both.at[which, rows, slot_cols[slot]]
        return remote(held, held, send_sem.at[which, slot], recv_sem.at[which, slot], device)

    def gather(which, slot):
        go(("gather", which, slot), lambda: gather_copy(which, slot))

    def arrived(which, slot):
        rows = (
            lambda: rows_of(0, False),
            lambda: rows_of(-1, True),
            lambda: rows_of(1, True),
            lambda: rows_of(-1, False),
            lambda: rows_of(1, False),
            lambda: rows_of(2, True, 0, half),
            lambda: rows_of(2, True, half, half),
            lambda: rows_of(2, False),
            lambda: rows_of(-1, False),
            lambda: rows_of(1, False),
        )[slot]()
        held = both.at[which, rows, slot_cols[slot]]
        remote(held, held, send_sem.at[which, slot], recv_sem.at[which, slot], here.partner()).wait_recv()


    parts = [None, out_w]

    def tp_copy(which, slot):
        source, held = parts[which], tp_in.at[which]
        first = pl.ds(0, half)
        second = pl.ds(half, half)
        rows, place, device = (
            lambda: (rows_of(2, False), held.at[0], here.partner()),
            lambda: (rows_of(1, False), held.at[1], here.along_z(1)),
            lambda: (rows_of(-1, False), held.at[2], here.along_z(-1)),
            lambda: (rows_of(2, True, 0, half), held.at[3, first], here.along_z(1)),
            lambda: (rows_of(2, True, half, half), held.at[3, second], here.along_z(-1)),
            lambda: (rows_of(1, True), held.at[4], here.along_z(1)),
            lambda: (rows_of(-1, True), held.at[5], here.along_z(-1)),
            lambda: (rows_of(0, False), held.at[6], here.partner()),
        )[slot]()
        return remote(source.at[rows], place, tp_send.at[which, slot], tp_recv.at[which, slot], device)

    def tp_go(which, slot):
        go(("tp", which, slot), lambda: tp_copy(which, slot))

    def add_rows(ref, base, length, others, size=128):
        def loop(index, carry):
            at = tile(index, size)
            rows = pl.ds(pl.multiple_of(base + index * size, size), size)
            total = ref[rows, :].astype(f32)
            for other in others:
                total = total + other[at, :].astype(f32)
            ref[rows, :] = total.astype(bf16)
            return carry

        lax.fori_loop(0, length // size, loop, 0)

    def tp_begin(which):
        for slot in range(3):
            tp_go(which, slot)

    def tp_halves(which):
        tp_copy(which, 0).wait_recv()
        add_rows(parts[which], here.block(2, True) * block, block, [tp_in.at[which, 0]], 16)
        tp_go(which, 3)
        tp_go(which, 4)

    def tp_direct(which):
        tp_copy(which, 3).wait_recv()
        add_rows(parts[which], here.block(1, True) * block, half, [tp_in.at[which, 3, pl.ds(0, half)]], 16)
        tp_go(which, 5)
        tp_copy(which, 4).wait_recv()
        add_rows(
            parts[which], here.block(-1, True) * block + half, half, [tp_in.at[which, 3, pl.ds(half, half)]], 16)
        tp_go(which, 6)

    def tp_last(which):
        tp_copy(which, 1).wait_recv()
        tp_copy(which, 2).wait_recv()
        add_rows(parts[which], here.block(0, False) * block, block, [tp_in.at[which, 1], tp_in.at[which, 2]], 16)
        tp_go(which, 7)

    def tp_total(which, index):
        at = tile(index, 16)
        rows = pl.ds(pl.multiple_of(here.tp * block + index * 16, 16), 16)
        total = parts[which][rows, :].astype(f32)
        for slot in (4, 5, 6):
            total = total + tp_in[which, slot, at, :].astype(f32)
        return at, total


    sums = (sums_out, sums_in, sums_val)
    arriving = (y_out, y_in, y_val)
    passing = (pass_out, pass_in, pass_val)
    crossing = (x_out, x_in, x_val)

    def halves(kind):
        size = sums[kind].shape[1] // 2
        return pl.ds(0, size), pl.ds(size, size), size

    def target(index, core):
        y = (here.y + DELTAS[index % 4]) % 4
        x_hi = 1 - here.x_hi if index < 4 else here.x_hi
        return y * 4 + x_hi * 2 + core

    def product(kind, index, core, write):
        cols = tile(target(index, core), cut)

        def one(step, carry):
            rows = tile(step, chans)
            first = (3, 0, 2)[kind] * chans
            left = turned[pl.ds(pl.multiple_of(first + step * chans, chans), chans), :]
            value = jnp.dot(left, both[(1, 0, 0)[kind], :, cols], preferred_element_type=f32)
            write(rows, value * scale)
            return carry

        lax.fori_loop(0, (1, 2, 1)[kind], one, 0)

    def sib_copy(kind, sib, index):
        return remote(
            sib.at[index % 4], sums[kind].at[index], sib_send.at[kind, index], sib_recv.at[kind, index],
            here.sibling())

    def for_sibling(kind, sib, index):
        if index >= 4:
            drained(("sib", kind, index - 4))

        def write(rows, value):
            sib[index % 4, rows, :] = value.astype(bf16)

        product(kind, index, 1 - here.core, write)
        go(("sib", kind, index), lambda: sib_copy(kind, sib, index))

    def for_self(kind, sib, index):
        sib_copy(kind, sib, index).wait_recv()

        def write(rows, value):
            held = sums[kind][index, rows, :].astype(f32)
            sums[kind][index, rows, :] = (held + value).astype(bf16)

        product(kind, index, here.core, write)

    def y_copy(kind, far, slot):
        upper, lower, _ = halves(kind)
        index, rows, step = (
            (0, upper, 1), (0, lower, -1), (1, lower, 1), (2, upper, -1), (1, upper, 1), (2, lower, -1)
        )[slot]
        return remote(
            sums[kind].at[far * 4 + index, rows], arriving[kind].at[far if kind < 2 else 0, slot],
            y_send.at[kind, far, slot], y_recv.at[kind, far, slot], here.along_y(step),
        )

    def y_go(kind, far, slot):
        go(("y", kind, far, slot), lambda: y_copy(kind, far, slot))

    def y_pass(kind, far):
        size = halves(kind)[2]
        y_copy(kind, far, 0).wait_recv()
        held = arriving[kind].at[far if kind < 2 else 0]
        add_rows(sums[kind].at[far * 4 + 1], 0, size, [held.at[0]])
        y_go(kind, far, 4)
        y_copy(kind, far, 1).wait_recv()
        add_rows(sums[kind].at[far * 4 + 2], size, size, [held.at[1]])
        y_go(kind, far, 5)

    def y_done(kind, far):
        for slot in (3, 4, 2, 5):
            y_copy(kind, far, slot).wait_recv()

    def x_copy(kind, side):
        rows = halves(kind)[side]
        source = sums[kind].at[3, rows] if kind < 2 else sums[kind].at[pl.ds(0, 4), rows]
        return remote(
            source, passing[kind].at[side], x_send.at[kind, side], x_recv.at[kind, side],
            here.along_x((1, -1)[side]))

    def x_forward(kind, side):
        return remote(
            passing[kind].at[side], crossing[kind].at[side], x_send.at[kind, 2 + side], x_recv.at[kind, 2 + side],
            here.along_x((1, -1)[side]))

    def x_begin(kind):
        size = halves(kind)[2]
        y_done(kind, 0)
        add_rows(sums[kind].at[3], 0, size, [arriving[kind].at[0, 3], arriving[kind].at[0, 4]])
        go(("x", kind, 0), lambda: x_copy(kind, 0))
        add_rows(sums[kind].at[3], size, size, [arriving[kind].at[0, 2], arriving[kind].at[0, 5]])
        go(("x", kind, 1), lambda: x_copy(kind, 1))

    def x_go(kind, side):
        go(("x", kind, 2 + side), lambda: x_forward(kind, side))

    def x_on(kind):
        for side in range(2):
            x_copy(kind, side).wait_recv()
            x_go(kind, side)

    def last(kind, side):
        size = halves(kind)[2]
        begin = side * size
        slots = ((3, 4), (2, 5))[side]
        if kind < 2:
            others = [arriving[kind].at[1, slot] for slot in slots] + [crossing[kind].at[side]]
        else:
            others = [arriving[kind].at[0, slot] for slot in slots]
        for index in range(size // 128):
            row = begin + index * 128
            total = sums[kind][7, pl.ds(row, 128), :].astype(f32)
            for other in others:
                total = total + other[pl.ds(index * 128, 128), :].astype(f32)
            if kind == 0:
                out_grad_ref[pl.ds(row, 128), :] = total.astype(bf16)
            else:
                to = row // chans if kind == 1 else 2
                in_grad_ref[to, :, pl.ds(row % chans, 128)] = total.T.astype(bf16)

    def lag_copy(step):
        device = (
            lambda: here.sibling(),
            lambda: here.along_x(2),
            lambda: here.along_y(1 - 2 * (here.y % 2)),
            lambda: here.along_y(2),
        )[step]()
        return remote(lag_sum.at[step], lag_got.at[step], lag_send.at[step], lag_recv.at[step], device)

    def lag_step(step):
        lag_copy(step).wait_recv()
        total = lag_sum[step] + lag_got[step]
        if step < 3:
            lag_sum[step + 1] = total
            go(("lag", step + 1), lambda: lag_copy(step + 1))
        else:
            lag_ref[...] = total

    def gather_phase(in_w):
        loads = [pltpu.make_async_copy(in_w_hbm.at[kind], in_w.at[kind], load_sem.at[kind]) for kind in range(3)]
        for copy in loads:
            copy.start()
        out_load.start()

        def normalise(index, carry):
            at = tile(index, 16)
            rows = pl.ds(pl.multiple_of(here.tp * block + index * 16, 16), 16)
            floats = hidden[at, :].astype(f32)
            factor = lax.rsqrt(jnp.mean(floats * floats, axis=-1, keepdims=True) + 1e-05)
            both[0, rows, :] = (floats * factor * gain[...]).astype(bf16)
            both[1, rows, :] = cot[at, :]
            return carry

        lax.fori_loop(0, block // 16, normalise, 0)
        pl.semaphore_wait(barrier, len(devices))

        def project(step):
            begin = ((here.z + step) % 4) * group

            def loop(kind, carry):
                value = jnp.dot(
                    both[0, pl.ds(pl.multiple_of(begin, group), group), :], in_w[kind], preferred_element_type=f32
                )
                value = value.astype(bf16).astype(f32)
                for index in range(2):
                    first = (begin // block + index) * wide + 8
                    proj[kind, pl.ds(pl.multiple_of(first, 8), block), :] = value[index * block : (index + 1) * block]
                return carry

            lax.fori_loop(0, 3, loop, 0)

        for slot in range(3):
            gather(0, slot)
        gather(1, 0)
        arrived(0, 1)
        gather(0, 5)
        gather(0, 8)
        arrived(0, 2)
        gather(0, 6)
        gather(0, 9)
        arrived(0, 0)
        gather(0, 3)
        gather(0, 4)
        gather(1, 1)
        gather(1, 2)
        for copy in loads:
            copy.wait()
        project(0)
        arrived(0, 5)
        arrived(0, 6)
        gather(0, 7)
        arrived(0, 3)
        arrived(0, 8)
        project(-1)
        arrived(0, 4)
        arrived(0, 9)
        project(1)
        arrived(1, 1)
        gather(1, 5)
        gather(1, 8)
        arrived(1, 2)
        gather(1, 6)
        gather(1, 9)
        arrived(1, 0)
        gather(1, 3)
        gather(1, 4)
        arrived(0, 7)
        project(2)

    def filter_phase(query, gates, prods, grads, ends, heads, sib):
        def first_copy():
            return remote(
                proj.at[:, pl.ds(7 * wide + span, 8), :], first_in, edge_send.at[0], edge_recv.at[0], here.following())

        def before_copy():
            return remote(ends, before_in, edge_send.at[1], edge_recv.at[1], here.along_x(2))

        def last_copy(which):
            kinds = pl.ds((0, 2)[which], 2)
            return remote(
                grads.at[kinds, pl.ds(0, 8), :], last_in.at[kinds], edge_send.at[2 + which], edge_recv.at[2 + which],
                here.preceding())

        def after_copy(which):
            kinds = pl.ds((0, 2)[which], 2)
            return remote(
                heads.at[kinds], after_in.at[kinds], edge_send.at[4 + which], edge_recv.at[4 + which],
                here.along_x(2))

        def edge_rows(target, kinds, source, offset):
            for kind in kinds:
                for pair in range(4):
                    rows = [source[kind, pl.ds((2 * pair + index) * wide + offset, 8), :] for index in range(2)]
                    target[kind, pl.ds(pair * 16, 16), :] = jnp.concatenate(rows).astype(bf16)

        def share(target, kinds, copy, source):
            @pl.when(here.core == 1)
            def _():
                copy().wait_recv()

            @pl.when(here.core == 0)
            def _():
                for kind in kinds:
                    target[kind] = source[kind]

        edge_rows(ends, range(3), proj, span)
        go(("edge", 0), first_copy)

        @pl.when(here.core == 1)
        def _():
            before_copy().start()

        arrived(1, 5)
        arrived(1, 6)
        gather(1, 7)
        first_copy().wait_recv()
        share(before_in, range(3), before_copy, ends)
        for kind in range(3):
            proj[kind, pl.ds(0, 8), :] = first_in[kind] * jnp.where(here.ctx == 0, 0.0, 1.0).astype(f32)
            for pair in range(4):
                rows = before_in[kind, pl.ds(pair * 16, 16), :].astype(f32)
                proj[kind, pl.ds((2 * pair + 1) * wide, 8), :] = rows[:8]
                if pair < 3:
                    proj[kind, pl.ds((2 * pair + 2) * wide, 8), :] = rows[8:]

        def short(lag, kind, cols):
            return short_taps[lag, pl.ds(kind, 1), cols]

        def inner(lag, cols):
            return inner_taps[pl.ds(lag, 1), cols]

        def behind(value, count):
            return pltpu.roll(value, count, 0)

        def ahead(value, count):
            return pltpu.roll(value, wide - count, 0)

        def forward(index, carry):
            begin = pl.multiple_of((index // steps) * span, span)
            first = pl.multiple_of((index // steps) * wide, 8)
            cols = tile(index % steps, 128)
            feats = []
            for kind in range(3):
                held = proj[kind, pl.ds(first, wide), cols]
                total = short(0, kind, cols) * held
                for lag in (1, 2):
                    total = total + short(lag, kind, cols) * behind(held, lag)
                feats.append(total)
            product = feats[1] * feats[2]
            total = inner(0, cols) * product
            for lag in range(1, 7):
                total = total + inner(lag, cols) * behind(product, lag)
            rows = pl.ds(begin, span)
            query[rows, cols] = feats[0][8:]
            grads[3, pl.ds(first, span), cols] = feats[1][8:]
            grads[2, pl.ds(first, span), cols] = feats[2][8:]
            gates[rows, cols] = total[8:]
            prods[rows, cols] = product[8:]
            acts[rows, tile(3 * steps + index % steps, 128)] = (feats[0][8:] * total[8:]).astype(bf16)
            return carry

        lax.fori_loop(0, bands * steps, forward, 0)
        edge_rows(heads, (2, 3), grads, 0)
        go(("edge", 3), lambda: last_copy(1))

        @pl.when(here.core == 1)
        def _():
            after_copy(1).start()

        lags[...] = jnp.zeros_like(lags)

        def turn(index, carry):
            turned[tile(index, 128), :] = acts[:, tile(index, 128)].T
            return carry

        lax.fori_loop(3 * steps, 4 * steps, turn, 0)
        out_load.wait()

        def branch_product(index, carry):
            cols = tile(index, chans)
            value = jnp.dot(acts[:, pl.ds(3 * chans, chans)], out_w[:, cols], preferred_element_type=f32)
            parts[0][:, cols] = value.astype(bf16)
            return carry

        lax.fori_loop(0, width // chans, branch_product, 0)

        for slot in (3, 4, 7, 8, 9):
            arrived(1, slot)
        tp_begin(0)
        for_sibling(0, sib, 0)
        for_sibling(0, sib, 1)
        for_sibling(0, sib, 2)
        for_self(0, sib, 0)
        y_go(0, 0, 0)
        y_go(0, 0, 1)
        for_sibling(0, sib, 3)
        for_self(0, sib, 1)
        y_go(0, 0, 2)
        for_self(0, sib, 2)
        y_go(0, 0, 3)
        value = lax.dot_general(both[1], out_w[...], (((1,), (1,)), ((), ())), preferred_element_type=f32)
        for index in range(8):
            rows = pl.ds(index * span, span)
            grads[0, pl.ds(index * wide, span), :] = value[index * span : (index + 1) * span] * query[rows, :]
            grads[1, pl.ds(index * wide, span), :] = value[index * span : (index + 1) * span] * gates[rows, :]
        edge_rows(heads, (0, 1), grads, 0)
        go(("edge", 2), lambda: last_copy(0))

        @pl.when(here.core == 1)
        def _():
            after_copy(0).start()

        y_pass(0, 0)
        for index in range(4, 8):
            for_sibling(0, sib, index)
            for_self(0, sib, index - 1)
            if index == 5:
                y_go(0, 1, 0)
                y_go(0, 1, 1)
            if index == 6:
                y_go(0, 1, 2)
            if index == 7:
                y_go(0, 1, 3)
        for_self(0, sib, 7)
        for which in range(2):
            last_copy(which).wait_recv()
            share(after_in, ((0, 1), (2, 3))[which], lambda which=which: after_copy(which), heads)
        ended = (here.core == 1) & (here.y == 3) & (here.last_block() == 1)
        for kind in range(4):
            kept = jnp.where(ended, 0.0, 1.0).astype(f32) if kind < 2 else 1.0
            grads[kind, pl.ds(7 * wide + span, 8), :] = last_in[kind] * kept
            for pair in range(4):
                rows = after_in[kind, pl.ds(pair * 16, 16), :].astype(f32)
                if pair > 0:
                    grads[kind, pl.ds((2 * pair - 1) * wide + span, 8), :] = rows[:8]
                grads[kind, pl.ds(2 * pair * wide + span, 8), :] = rows[8:]

        def turn_tile(index):
            rows = tile(index // steps, 128)
            for kind in range(3):
                cols = tile(kind * steps + index % steps, 128)
                turned[cols, rows] = acts[rows, cols].T

        def backward(index, carry):
            turn_tile(jnp.maximum(index - 1, 0))
            for part_of in range(2):
                backward_band((index // steps) * 2 + part_of, index % steps)
            return carry

        def backward_band(band, column):
            begin = pl.multiple_of(band * span, span)
            first = pl.multiple_of(band * wide, 8)
            cols = tile(column, 128)
            rows = pl.ds(first, wide)
            here_rows = pl.ds(begin, span)

            def add_lag(row, value):
                lags[row, :, cols] += jnp.sum(value.reshape(span // 8, 8, 128), axis=0)

            gated = grads[0, rows, cols]
            product = prods[here_rows, cols]
            total = inner(0, cols) * gated
            add_lag(9, gated[:span] * product)
            for lag in range(1, 7):
                moved = ahead(gated, lag)
                total = total + inner(lag, cols) * moved
                add_lag(9 + lag, moved[:span] * product)
            feats = (grads[1, rows, cols], total * grads[2, rows, cols], total * grads[3, rows, cols])
            for kind in range(3):
                feat = feats[kind]
                held = proj[kind, pl.ds(pl.multiple_of(first + 8, 8), span), cols]
                summed = short(0, kind, cols) * feat[:span]
                add_lag(kind, feat[:span] * held)
                for lag in (1, 2):
                    moved = ahead(feat, lag)[:span]
                    summed = summed + short(lag, kind, cols) * moved
                    add_lag(lag * 3 + kind, moved * held)
                acts[here_rows, tile(kind * steps + column, 128)] = summed.astype(bf16)

        tiles = (bands // 2) * steps
        lax.fori_loop(0, tiles - steps, backward, 0)
        y_pass(0, 1)
        tp_halves(0)
        tp_last(0)
        lax.fori_loop(tiles - steps, tiles, backward, 0)
        turn_tile(tiles - 1)
        lag_sum[0] = jnp.sum(lags[...], axis=1) * scale
        go(("lag", 0), lambda: lag_copy(0))
        x_begin(0)
        for index in (0, 2, 3):
            drained(("edge", index))

        @pl.when(here.core == 1)
        def _():
            before_copy().wait_send()
            after_copy(0).wait_send()
            after_copy(1).wait_send()

        for index in range(4, 8):
            drained(("sib", 0, index))

    def reduce_phase(in_w, sib, sib_val):
        def in_load(step, slot):
            return pltpu.make_async_copy(in_w_hbm.at[:, tile(step, step_in), :], in_w.at[slot], in_w_sem.at[slot])

        in_load(0, 0).start()
        in_load(1, 1).start()

        def gnorm_product():
            def loop(step, carry):
                slot = step % 2
                in_load(step, slot).wait()
                value = jnp.zeros((tokens, step_in), f32)
                for kind in range(3):
                    value = value + lax.dot_general(
                        acts[:, pl.ds(kind * chans, chans)], in_w[slot, kind],
                        (((1,), (1,)), ((), ())), preferred_element_type=f32,
                    )
                out_w[:, tile(step, step_in)] = value.astype(bf16)

                @pl.when(step + 2 < width // step_in)
                def _():
                    in_load(step + 2, slot).start()

                return carry

            lax.fori_loop(0, width // step_in, loop, 0)

        for_sibling(1, sib, 0)
        for_sibling(1, sib, 1)
        for_self(1, sib, 0)
        y_go(1, 0, 0)
        y_go(1, 0, 1)
        tp_direct(0)
        for_sibling(2, sib_val, 0)
        for index in range(1, 4):
            for_sibling(2, sib_val, index)
            for_self(2, sib_val, index - 1)
        for_self(2, sib_val, 3)
        for side in range(2):
            go(("x", 2, side), lambda side=side: x_copy(2, side))
        for_sibling(1, sib, 2)
        for_self(1, sib, 1)
        y_go(1, 0, 2)
        for_sibling(1, sib, 3)
        for_self(1, sib, 2)
        y_go(1, 0, 3)
        lag_step(0)
        x_on(0)
        gnorm_product()
        tp_begin(1)
        y_pass(1, 0)
        lag_step(1)
        x_on(2)
        for index in range(4, 8):
            for_sibling(1, sib, index)
            for_self(1, sib, index - 1)
        for_self(1, sib, 7)
        for slot in range(4):
            drained(("y", 1, 0, slot))
        y_go(1, 1, 0)
        y_go(1, 1, 1)
        for index in range(4, 8):
            for_sibling(2, sib_val, index)
            if index > 4:
                for_self(2, sib_val, index - 1)
        for_self(2, sib_val, 7)
        tp_halves(1)
        tp_last(1)
        lag_step(2)
        x_begin(1)
        drained(("y", 1, 0, 4))
        drained(("y", 1, 0, 5))
        y_go(1, 1, 2)
        y_go(1, 1, 3)
        for slot in (5, 6, 7):
            tp_copy(0, slot).wait_recv()

        def layer_finish(index, carry):
            at, total = tp_total(0, index)
            layer_ref[at, :] = (hidden[at, :].astype(f32) + total).astype(bf16)
            return carry

        lax.fori_loop(0, block // 16, layer_finish, 0)
        tp_direct(1)
        for side in range(2):
            x_forward(0, side).wait_recv()
        y_done(0, 1)
        last(0, 0)
        last(0, 1)
        lag_step(3)
        y_pass(1, 1)
        size = halves(2)[2]
        for side in range(2):
            x_forward(2, side).wait_recv()
            for index in range(4):
                add_rows(sums_val.at[4 + index], side * size, size, [x_val.at[side, index]])
        for slot in range(4):
            y_go(2, 1, slot)
        x_on(1)
        y_pass(2, 1)
        for slot in (5, 6, 7):
            tp_copy(1, slot).wait_recv()

        def input_finish(index, carry):
            at, total = tp_total(1, index)
            floats = hidden[at, :].astype(f32)
            factor = lax.rsqrt(jnp.mean(floats * floats, axis=-1, keepdims=True) + 1e-05)
            gained = total * gain[...]
            inner = jnp.mean(floats * gained, axis=-1, keepdims=True) * factor * factor * factor
            input_ref[at, :] = (cot[at, :].astype(f32) + gained * factor - floats * inner).astype(bf16)
            return carry

        lax.fori_loop(0, block // 16, input_finish, 0)
        for side in range(2):
            x_forward(1, side).wait_recv()
        y_done(1, 1)
        last(1, 0)
        last(1, 1)
        y_done(2, 1)
        last(2, 0)
        last(2, 1)
        for name in list(sends):
            drained(name)

    def later_phases(part):
        parts[0] = part
        pl.run_scoped(
            filter_phase,
            pltpu.VMEM((tokens, chans), f32),
            pltpu.VMEM((tokens, chans), f32),
            pltpu.VMEM((tokens, chans), f32),
            pltpu.VMEM((4, bands * wide, chans), f32),
            pltpu.VMEM((3, bands * 8, chans), bf16),
            pltpu.VMEM((4, bands * 8, chans), bf16),
            pltpu.VMEM((4, chans, cut), bf16),
        )
        pl.run_scoped(
            reduce_phase,
            pltpu.VMEM((2, 3, step_in, chans), bf16),
            pltpu.VMEM((4, 2 * chans, cut), bf16),
            pltpu.VMEM((4, chans, cut), bf16),
        )

    pl.run_scoped(gather_phase, pltpu.VMEM((3, width, chans), bf16))
    pl.run_scoped(later_phases, pltpu.VMEM((tokens, width), bf16))


def layer_results(hidden, cot, gain, short_taps, inner_taps, in_weight, out_weight, tokens, scale):
    block, width = hidden.shape
    chans = out_weight.shape[0]
    cut = width // 16
    any_space = pl.BlockSpec(memory_space=pl.ANY)
    vmem_space = pl.BlockSpec(memory_space=pltpu.VMEM)
    bf16, f32 = jnp.bfloat16, jnp.float32
    dma = pltpu.SemaphoreType.DMA
    body = lambda *refs: layer_kernel(scale, tokens, *refs)
    return pl.pallas_call(
        body,
        out_shape=(
            jax.ShapeDtypeStruct((block, width), bf16),
            jax.ShapeDtypeStruct((block, width), bf16),
            jax.ShapeDtypeStruct((3, cut, chans), bf16),
            jax.ShapeDtypeStruct((chans, cut), bf16),
            jax.ShapeDtypeStruct((16, chans), f32),
        ),
        in_specs=[vmem_space] * 5 + [any_space] * 2,
        out_specs=(vmem_space,) * 5,
        scratch_shapes=[
            pltpu.VMEM((2, tokens, width), bf16),
            pltpu.VMEM(out_weight.shape, bf16),
            pltpu.VMEM((3, tokens + 64, chans), f32),
            pltpu.VMEM((3, 8, chans), f32),
            pltpu.VMEM((3, 64, chans), bf16),
            pltpu.VMEM((4, 8, chans), f32),
            pltpu.VMEM((4, 64, chans), bf16),
            pltpu.VMEM((16, 8, chans), f32),
            pltpu.VMEM((tokens, 4 * chans), bf16),
            pltpu.VMEM((4 * chans, tokens), bf16),
            pltpu.VMEM((8, chans, cut), bf16),
            pltpu.VMEM((8, 2 * chans, cut), bf16),
            pltpu.VMEM((8, chans, cut), bf16),
            pltpu.VMEM((2, 6, chans // 2, cut), bf16),
            pltpu.VMEM((2, 6, chans, cut), bf16),
            pltpu.VMEM((1, 6, chans // 2, cut), bf16),
            pltpu.VMEM((2, chans // 2, cut), bf16),
            pltpu.VMEM((2, chans, cut), bf16),
            pltpu.VMEM((2, 4, chans // 2, cut), bf16),
            pltpu.VMEM((2, chans // 2, cut), bf16),
            pltpu.VMEM((2, chans, cut), bf16),
            pltpu.VMEM((2, 4, chans // 2, cut), bf16),
            pltpu.VMEM((2, 7, block, width), bf16),
            pltpu.VMEM((4, 16, chans), f32),
            pltpu.VMEM((4, 16, chans), f32),
            dma((4,)), dma((2,)), dma((2, 10)), dma((2, 10)), dma((6,)), dma((6,)),
            dma((3, 8)), dma((3, 8)), dma((3, 2, 6)), dma((3, 2, 6)), dma((3, 4)), dma((3, 4)),
            dma((2, 8)), dma((2, 8)), dma((4,)), dma((4,)),
        ],
        compiler_params=pltpu.CompilerParams(
            collective_id=0, has_side_effects=True, vmem_limit_bytes=63 * 2**20
        ),
        name="whole_layer",
    )(hidden, cot, gain, short_taps, inner_taps, in_weight, out_weight)


def place_kernel(
    layer, grad, kinds, outer, lags, layer_to, grad_to, kinds_to, outer_to, short_to, inner_to,
    layer_at, grad_at, kinds_at, outer_at, sems,
):
    pairs = ((kinds, kinds_at, kinds_to), (layer, layer_at, layer_to), (grad, grad_at, grad_to), (outer, outer_at, outer_to))
    reads = [pltpu.make_async_copy(pair[0], pair[1], sems.at[0, index]) for index, pair in enumerate(pairs)]
    writes = [pltpu.make_async_copy(pair[1], pair[2], sems.at[1, index]) for index, pair in enumerate(pairs)]
    for copy in reads:
        copy.start()
    for lag in range(3):
        short_to[lag] = lags[pl.ds(3 * lag, 3), :]
    inner_to[...] = lags[pl.ds(9, 7), :]
    for read, write in zip(reads, writes):
        read.wait()
        write.start()
    for copy in writes:
        copy.wait()


def placed_results(layer, grad, kinds, outer, lags):
    chans = lags.shape[1]
    any_space = pl.BlockSpec(memory_space=pl.ANY)
    vmem_space = pl.BlockSpec(memory_space=pltpu.VMEM)
    arrays = (layer, grad, kinds, outer)
    return pl.pallas_call(
        place_kernel,
        out_shape=tuple(jax.ShapeDtypeStruct(array.shape, array.dtype) for array in arrays)
        + (jax.ShapeDtypeStruct((3, 3, chans), jnp.float32), jax.ShapeDtypeStruct((7, chans), jnp.float32)),
        in_specs=[any_space] * 4 + [vmem_space],
        out_specs=(any_space,) * 4 + (vmem_space,) * 2,
        scratch_shapes=[pltpu.VMEM(array.shape, array.dtype) for array in arrays] + [pltpu.SemaphoreType.DMA((2, 4))],
        compiler_params=pltpu.CompilerParams(vmem_limit_bytes=60 * 2**20),
        name="place_results",
    )(layer, grad, kinds, outer, lags)


def local(hidden_in, cotangent, norm_gain, in_weight, filter_taps, inner_taps, out_weight):
    tokens = hidden_in.shape[0] * lax.axis_size("tp")
    scale = (tokens * lax.axis_size("ctx")) ** (-0.5)
    gain = norm_gain.reshape(1, -1)
    kinds = jnp.transpose(in_weight, (1, 0, 2))
    layer_out, grad_input, grad_kinds, grad_out_weight, grad_filter, grad_inner = placed_results(
        *layer_results(hidden_in, cotangent, gain, filter_taps, inner_taps, kinds, out_weight, tokens, scale)
    )
    return (layer_out, grad_input, jnp.transpose(grad_kinds, (1, 0, 2)), grad_out_weight, grad_filter, grad_inner)


def solution(mesh):
    placed = (
        P(("ctx", "tp"), None),
        P(("ctx", "tp"), None),
        P(),
        P(None, None, "tp"),
        P(None, None, "tp"),
        P(None, "tp"),
        P("tp", None),
    )
    return jax.shard_map(
        local,
        mesh=mesh,
        in_specs=placed,
        out_specs=(
            P(("ctx", "tp"), None),
            P(("ctx", "tp"), None),
            P("ctx", None, "tp"),
            P("tp", "ctx"),
            P(None, None, "tp"),
            P(None, "tp"),
        ),
        check_vma=False,
    )
```

```python
import jax
import jax.numpy as jnp
from jax import lax
from jax.experimental import pallas as pl
from jax.experimental.pallas import tpu as pltpu
from jax.sharding import PartitionSpec as P

MESH = pl.DeviceIdType.MESH
DELTAS = (2, 1, 3, 0)


class Place:
    def __init__(self):
        ctx, tp = lax.axis_index("ctx"), lax.axis_index("tp")
        self.y, self.x_hi, self.core = ctx // 4, (ctx // 2) % 2, ctx % 2
        self.z, self.x_lo = tp // 2, tp % 2
        self.ctx, self.tp = ctx, tp

    def sibling(self):
        return (self.y * 4 + self.x_hi * 2 + 1 - self.core, self.tp)

    def along_y(self, step):
        return (((self.y + step) % 4) * 4 + self.x_hi * 2 + self.core, self.tp)

    def along_z(self, step):
        return (self.ctx, ((self.z + step) % 4) * 2 + self.x_lo)

    def along_x(self, step):
        x = (self.x_hi * 2 + self.x_lo + step) % 4
        return (self.y * 4 + (x // 2) * 2 + self.core, self.z * 2 + x % 2)

    def at(self, y, x, core):
        return (y * 4 + (x // 2) * 2 + core, self.z * 2 + x % 2)

    def partner(self):
        return self.along_x((1 - 2 * self.core) * (1 - 2 * self.x_lo))

    def last_block(self):
        x_hi, x_lo = self.x_hi, self.x_lo
        return jnp.where(self.core == 1, x_hi * x_lo + (1 - x_hi) * (1 - x_lo), x_hi)

    def following(self):
        x_hi, x_lo, core = self.x_hi, self.x_lo, self.core
        held = x_hi * x_lo + (1 - x_hi) * (1 - x_lo)
        x = (1 - core) * ((2 * x_hi + 3 * x_lo) % 4) + core * ((1 - held) * 2 + x_lo)
        return self.at((self.y + core * held) % 4, x, 1 - core)

    def preceding(self):
        x_hi, x_lo, core = self.x_hi, self.x_lo, self.core
        held = x_hi * (1 - x_lo) + (1 - x_hi) * x_lo
        x = core * (held * 2 + x_lo) + (1 - core) * (((1 - x_hi) * 2 + 2 - x_lo) % 4)
        return self.at((self.y - (1 - core) * (1 - x_hi)) % 4, x, 1 - core)

    def block(self, step, same):
        x_lo = self.x_lo if same else 1 - self.x_lo
        return ((self.z + step) % 4) * 2 + x_lo


def remote(source, target, send, recv, device):
    return pltpu.make_async_remote_copy(
        src_ref=source, dst_ref=target, send_sem=send, recv_sem=recv, device_id=device, device_id_type=MESH
    )


def tile(index, size):
    return pl.ds(pl.multiple_of(index * size, size), size)


def layer_kernel(
    scale, tokens,
    hidden_hbm, cot_hbm, gain_hbm, short_hbm, inner_hbm, in_w_hbm, out_w_hbm,
    layer_hbm, input_hbm, in_grad_hbm, out_grad_hbm, lag_hbm,
    hidden, cot, gain, short_taps, inner_taps, layer_ref, input_ref, in_grad_ref, out_grad_ref, lag_ref,
    both, out_w, proj, first_in, before_in, last_in, after_in, lags, acts, turned, part,
    sums_out, sums_in, y_out, y_in, pass_out, pass_in, x_out, x_in, tp_in, lag_sum, lag_got,
    load_sem, row_sem, result_sem, in_w_sem, send_sem, recv_sem, edge_send, edge_recv,
    sib_send, sib_recv, y_send, y_recv, x_send, x_recv, tp_send, tp_recv, lag_send, lag_recv,
):
    here = Place()
    block, width = hidden.shape
    chans = out_w_hbm.shape[0]
    cut = width // 16
    half = block // 2
    group = 2 * block
    wide, span = 72, 64
    steps = chans // 128
    bands = tokens // span
    step_in = 512
    x_cols = (width // 128 * 3 // 4) * 128
    bf16, f32 = jnp.bfloat16, jnp.float32

    out_load = pltpu.make_async_copy(out_w_hbm, out_w, load_sem.at[3])
    barrier = pltpu.get_barrier_semaphore()
    devices = [
        here.sibling(), here.along_y(1), here.along_y(-1), here.along_y(2), here.along_z(1), here.along_z(-1),
        here.along_x(1), here.along_x(-1), here.along_x(2), here.following(), here.preceding(),
    ]
    for device in devices:
        pl.semaphore_signal(barrier, inc=1, device_id=device, device_id_type=MESH)
    row_loads = [
        pltpu.make_async_copy(source, target, row_sem.at[index])
        for index, (source, target) in enumerate(
            ((hidden_hbm, hidden), (cot_hbm, cot), (gain_hbm, gain), (short_hbm, short_taps), (inner_hbm, inner_taps)))
    ]
    for copy in row_loads:
        copy.start()

    def result(index):
        source, target = (
            (layer_ref, layer_hbm), (input_ref, input_hbm), (in_grad_ref, in_grad_hbm),
            (out_grad_ref, out_grad_hbm), (lag_ref, lag_hbm),
        )[index]
        return pltpu.make_async_copy(source, target, result_sem.at[index])

    sends = {}

    def go(name, build):
        build().start()
        sends[name] = build

    def drained(name):
        sends.pop(name)().wait_send()


    def rows_of(step, same, begin=0, size=block):
        return pl.ds(pl.multiple_of(here.block(step, same) * block + begin, size), size)

    every = pl.ds(0, width)
    by_x = pl.ds(0, x_cols)
    by_z = pl.ds(x_cols, width - x_cols)
    slot_cols = (every, every, every, by_z, by_z, every, every, every, by_x, by_x)

    def gather_copy(which, slot):
        rows, device = (
            lambda: (rows_of(0, True), here.partner()),
            lambda: (rows_of(0, True), here.along_z(1)),
            lambda: (rows_of(0, True), here.along_z(-1)),
            lambda: (rows_of(0, False), here.along_z(1)),
            lambda: (rows_of(0, False), here.along_z(-1)),
            lambda: (rows_of(-1, True, 0, half), here.along_z(1)),
            lambda: (rows_of(1, True, half, half), here.along_z(-1)),
            lambda: (rows_of(2, True), here.partner()),
            lambda: (rows_of(-1, True), here.partner()),
            lambda: (rows_of(1, True), here.partner()),
        )[slot]()
        held = both.at[which, rows, slot_cols[slot]]
        return remote(held, held, send_sem.at[which, slot], recv_sem.at[which, slot], device)

    def gather(which, slot):
        go(("gather", which, slot), lambda: gather_copy(which, slot))

    def arrived(which, slot):
        rows = (
            lambda: rows_of(0, False),
            lambda: rows_of(-1, True),
            lambda: rows_of(1, True),
            lambda: rows_of(-1, False),
            lambda: rows_of(1, False),
            lambda: rows_of(2, True, 0, half),
            lambda: rows_of(2, True, half, half),
            lambda: rows_of(2, False),
            lambda: rows_of(-1, False),
            lambda: rows_of(1, False),
        )[slot]()
        held = both.at[which, rows, slot_cols[slot]]
        remote(held, held, send_sem.at[which, slot], recv_sem.at[which, slot], here.partner()).wait_recv()


    parts = (part, out_w)

    def tp_copy(which, slot):
        source, held = parts[which], tp_in.at[which]
        first = pl.ds(0, half)
        second = pl.ds(half, half)
        rows, place, device = (
            lambda: (rows_of(2, False), held.at[0], here.partner()),
            lambda: (rows_of(1, False), held.at[1], here.along_z(1)),
            lambda: (rows_of(-1, False), held.at[2], here.along_z(-1)),
            lambda: (rows_of(2, True, 0, half), held.at[3, first], here.along_z(1)),
            lambda: (rows_of(2, True, half, half), held.at[3, second], here.along_z(-1)),
            lambda: (rows_of(1, True), held.at[4], here.along_z(1)),
            lambda: (rows_of(-1, True), held.at[5], here.along_z(-1)),
            lambda: (rows_of(0, False), held.at[6], here.partner()),
        )[slot]()
        return remote(source.at[rows], place, tp_send.at[which, slot], tp_recv.at[which, slot], device)

    def tp_go(which, slot):
        go(("tp", which, slot), lambda: tp_copy(which, slot))

    def add_rows(ref, base, length, others, size=128):
        def loop(index, carry):
            at = tile(index, size)
            rows = pl.ds(pl.multiple_of(base + index * size, size), size)
            total = ref[rows, :].astype(f32)
            for other in others:
                total = total + other[at, :].astype(f32)
            ref[rows, :] = total.astype(bf16)
            return carry

        lax.fori_loop(0, length // size, loop, 0)

    def tp_begin(which):
        for slot in range(3):
            tp_go(which, slot)

    def tp_halves(which):
        tp_copy(which, 0).wait_recv()
        add_rows(parts[which], here.block(2, True) * block, block, [tp_in.at[which, 0]], 16)
        tp_go(which, 3)
        tp_go(which, 4)

    def tp_direct(which):
        tp_copy(which, 3).wait_recv()
        add_rows(parts[which], here.block(1, True) * block, half, [tp_in.at[which, 3, pl.ds(0, half)]], 16)
        tp_go(which, 5)
        tp_copy(which, 4).wait_recv()
        add_rows(
            parts[which], here.block(-1, True) * block + half, half, [tp_in.at[which, 3, pl.ds(half, half)]], 16)
        tp_go(which, 6)

    def tp_last(which):
        tp_copy(which, 1).wait_recv()
        tp_copy(which, 2).wait_recv()
        add_rows(parts[which], here.block(0, False) * block, block, [tp_in.at[which, 1], tp_in.at[which, 2]], 16)
        tp_go(which, 7)

    def tp_total(which, index):
        at = tile(index, 16)
        rows = pl.ds(pl.multiple_of(here.tp * block + index * 16, 16), 16)
        total = parts[which][rows, :].astype(f32)
        for slot in (4, 5, 6):
            total = total + tp_in[which, slot, at, :].astype(f32)
        return at, total


    sums = (sums_out, sums_in)
    arriving = (y_out, y_in)
    passing = (pass_out, pass_in)
    crossing = (x_out, x_in)

    def halves(kind):
        size = sums[kind].shape[1] // 2
        return pl.ds(0, size), pl.ds(size, size), size

    def target(index, core):
        y = (here.y + DELTAS[index % 4]) % 4
        x_hi = 1 - here.x_hi if index < 4 else here.x_hi
        return y * 4 + x_hi * 2 + core

    def product(kind, index, core, write):
        cols = tile(target(index, core), cut)

        def one(step, carry):
            rows = tile(step, chans)
            first = 3 * chans if kind == 0 else 0
            left = turned[pl.ds(pl.multiple_of(first + step * chans, chans), chans), :]
            value = jnp.dot(left, both[1 - kind, :, cols], preferred_element_type=f32)
            write(rows, value * scale)
            return carry

        lax.fori_loop(0, (1, 3)[kind], one, 0)

    def sib_copy(kind, sib, index):
        return remote(
            sib.at[index % 4], sums[kind].at[index], sib_send.at[kind, index], sib_recv.at[kind, index],
            here.sibling())

    def for_sibling(kind, sib, index):
        if index >= 4:
            drained(("sib", kind, index - 4))

        def write(rows, value):
            sib[index % 4, rows, :] = value.astype(bf16)

        product(kind, index, 1 - here.core, write)
        go(("sib", kind, index), lambda: sib_copy(kind, sib, index))

    def for_self(kind, sib, index):
        sib_copy(kind, sib, index).wait_recv()

        def write(rows, value):
            held = sums[kind][index, rows, :].astype(f32)
            sums[kind][index, rows, :] = (held + value).astype(bf16)

        product(kind, index, here.core, write)

    def y_copy(kind, far, slot):
        upper, lower, _ = halves(kind)
        index, rows, step = (
            (0, upper, 1), (0, lower, -1), (1, lower, 1), (2, upper, -1), (1, upper, 1), (2, lower, -1)
        )[slot]
        return remote(
            sums[kind].at[far * 4 + index, rows], arriving[kind].at[far, slot],
            y_send.at[kind, far, slot], y_recv.at[kind, far, slot], here.along_y(step),
        )

    def y_go(kind, far, slot):
        go(("y", kind, far, slot), lambda: y_copy(kind, far, slot))

    def y_pass(kind, far):
        size = halves(kind)[2]
        y_copy(kind, far, 0).wait_recv()
        add_rows(sums[kind].at[far * 4 + 1], 0, size, [arriving[kind].at[far, 0]])
        y_go(kind, far, 4)
        y_copy(kind, far, 1).wait_recv()
        add_rows(sums[kind].at[far * 4 + 2], size, size, [arriving[kind].at[far, 1]])
        y_go(kind, far, 5)

    def y_done(kind, far):
        for slot in (3, 4, 2, 5):
            y_copy(kind, far, slot).wait_recv()

    def x_copy(kind, side):
        rows = halves(kind)[side]
        return remote(
            sums[kind].at[3, rows], passing[kind].at[side], x_send.at[kind, side], x_recv.at[kind, side],
            here.along_x((1, -1)[side]))

    def x_forward(kind, side):
        return remote(
            passing[kind].at[side], crossing[kind].at[side], x_send.at[kind, 2 + side], x_recv.at[kind, 2 + side],
            here.along_x((1, -1)[side]))

    def x_begin(kind):
        size = halves(kind)[2]
        y_done(kind, 0)
        add_rows(sums[kind].at[3], 0, size, [arriving[kind].at[0, 3], arriving[kind].at[0, 4]])
        go(("x", kind, 0), lambda: x_copy(kind, 0))
        add_rows(sums[kind].at[3], size, size, [arriving[kind].at[0, 2], arriving[kind].at[0, 5]])
        go(("x", kind, 1), lambda: x_copy(kind, 1))

    def x_go(kind, side):
        go(("x", kind, 2 + side), lambda: x_forward(kind, side))

    def x_on(kind):
        for side in range(2):
            x_copy(kind, side).wait_recv()
            x_go(kind, side)

    def last(kind, side):
        size = halves(kind)[2]
        begin = side * size
        others = [arriving[kind].at[1, slot] for slot in ((3, 4), (2, 5))[side]] + [crossing[kind].at[side]]
        for index in range(size // 128):
            row = begin + index * 128
            total = sums[kind][7, pl.ds(row, 128), :].astype(f32)
            for other in others:
                total = total + other[pl.ds(index * 128, 128), :].astype(f32)
            if kind == 1:
                in_grad_ref[row // chans, :, pl.ds(row % chans, 128)] = total.T.astype(bf16)
            else:
                out_grad_ref[pl.ds(row, 128), :] = total.astype(bf16)

    def lag_copy(step):
        device = (
            lambda: here.sibling(),
            lambda: here.along_x(2),
            lambda: here.along_y(1 - 2 * (here.y % 2)),
            lambda: here.along_y(2),
        )[step]()
        return remote(lag_sum.at[step], lag_got.at[step], lag_send.at[step], lag_recv.at[step], device)

    def lag_step(step):
        lag_copy(step).wait_recv()
        total = lag_sum[step] + lag_got[step]
        if step < 3:
            lag_sum[step + 1] = total
            go(("lag", step + 1), lambda: lag_copy(step + 1))
        else:
            lag_ref[...] = total

    def gather_phase(in_w):
        loads = [pltpu.make_async_copy(in_w_hbm.at[kind], in_w.at[kind], load_sem.at[kind]) for kind in range(3)]
        for copy in loads:
            copy.start()
        out_load.start()
        for copy in row_loads:
            copy.wait()

        def normalise(index, carry):
            at = tile(index, 16)
            rows = pl.ds(pl.multiple_of(here.tp * block + index * 16, 16), 16)
            floats = hidden[at, :].astype(f32)
            factor = lax.rsqrt(jnp.mean(floats * floats, axis=-1, keepdims=True) + 1e-05)
            both[0, rows, :] = (floats * factor * gain[...]).astype(bf16)
            both[1, rows, :] = cot[at, :]
            return carry

        lax.fori_loop(0, block // 16, normalise, 0)
        pl.semaphore_wait(barrier, len(devices))

        def project(step):
            begin = ((here.z + step) % 4) * group

            def loop(kind, carry):
                value = jnp.dot(
                    both[0, pl.ds(pl.multiple_of(begin, group), group), :], in_w[kind], preferred_element_type=f32
                )
                value = value.astype(bf16).astype(f32)
                for index in range(2):
                    first = (begin // block + index) * wide + 8
                    proj[kind, pl.ds(pl.multiple_of(first, 8), block), :] = value[index * block : (index + 1) * block]
                return carry

            lax.fori_loop(0, 3, loop, 0)

        for slot in range(3):
            gather(0, slot)
        gather(1, 0)
        arrived(0, 1)
        gather(0, 5)
        gather(0, 8)
        arrived(0, 2)
        gather(0, 6)
        gather(0, 9)
        arrived(0, 0)
        gather(0, 3)
        gather(0, 4)
        gather(1, 1)
        gather(1, 2)
        for copy in loads:
            copy.wait()
        project(0)
        arrived(0, 5)
        arrived(0, 6)
        gather(0, 7)
        arrived(0, 3)
        arrived(0, 8)
        project(-1)
        arrived(0, 4)
        arrived(0, 9)
        project(1)
        arrived(1, 1)
        gather(1, 5)
        gather(1, 8)
        arrived(1, 2)
        gather(1, 6)
        gather(1, 9)
        arrived(1, 0)
        gather(1, 3)
        gather(1, 4)
        arrived(0, 7)
        project(2)

    def filter_phase(query, gates, prods, grads, ends, heads, sib):
        def first_copy():
            return remote(
                proj.at[:, pl.ds(7 * wide + span, 8), :], first_in, edge_send.at[0], edge_recv.at[0], here.following())

        def before_copy():
            return remote(ends, before_in, edge_send.at[1], edge_recv.at[1], here.along_x(2))

        def last_copy(which):
            kinds = pl.ds((0, 2)[which], 2)
            return remote(
                grads.at[kinds, pl.ds(0, 8), :], last_in.at[kinds], edge_send.at[2 + which], edge_recv.at[2 + which],
                here.preceding())

        def after_copy(which):
            kinds = pl.ds((0, 2)[which], 2)
            return remote(
                heads.at[kinds], after_in.at[kinds], edge_send.at[4 + which], edge_recv.at[4 + which],
                here.along_x(2))

        def edge_rows(target, kinds, source, offset):
            for kind in kinds:
                for pair in range(4):
                    rows = [source[kind, pl.ds((2 * pair + index) * wide + offset, 8), :] for index in range(2)]
                    target[kind, pl.ds(pair * 16, 16), :] = jnp.concatenate(rows).astype(bf16)

        def share(target, kinds, copy, source):
            @pl.when(here.core == 1)
            def _():
                copy().wait_recv()

            @pl.when(here.core == 0)
            def _():
                for kind in kinds:
                    target[kind] = source[kind]

        edge_rows(ends, range(3), proj, span)
        go(("edge", 0), first_copy)

        @pl.when(here.core == 1)
        def _():
            before_copy().start()

        arrived(1, 5)
        arrived(1, 6)
        gather(1, 7)
        first_copy().wait_recv()
        share(before_in, range(3), before_copy, ends)
        for kind in range(3):
            proj[kind, pl.ds(0, 8), :] = first_in[kind] * jnp.where(here.ctx == 0, 0.0, 1.0).astype(f32)
            for pair in range(4):
                rows = before_in[kind, pl.ds(pair * 16, 16), :].astype(f32)
                proj[kind, pl.ds((2 * pair + 1) * wide, 8), :] = rows[:8]
                if pair < 3:
                    proj[kind, pl.ds((2 * pair + 2) * wide, 8), :] = rows[8:]

        def short(lag, kind, cols):
            return short_taps[lag, pl.ds(kind, 1), cols]

        def inner(lag, cols):
            return inner_taps[pl.ds(lag, 1), cols]

        def behind(value, count):
            return pltpu.roll(value, count, 0)

        def ahead(value, count):
            return pltpu.roll(value, wide - count, 0)

        def forward(index, carry):
            begin = pl.multiple_of((index // steps) * span, span)
            first = pl.multiple_of((index // steps) * wide, 8)
            cols = tile(index % steps, 128)
            feats = []
            for kind in range(3):
                held = proj[kind, pl.ds(first, wide), cols]
                total = short(0, kind, cols) * held
                for lag in (1, 2):
                    total = total + short(lag, kind, cols) * behind(held, lag)
                feats.append(total)
            product = feats[1] * feats[2]
            total = inner(0, cols) * product
            for lag in range(1, 7):
                total = total + inner(lag, cols) * behind(product, lag)
            rows = pl.ds(begin, span)
            query[rows, cols] = feats[0][8:]
            grads[3, pl.ds(first, span), cols] = feats[1][8:]
            grads[2, pl.ds(first, span), cols] = feats[2][8:]
            gates[rows, cols] = total[8:]
            prods[rows, cols] = product[8:]
            acts[rows, tile(3 * steps + index % steps, 128)] = (feats[0][8:] * total[8:]).astype(bf16)
            return carry

        lax.fori_loop(0, bands * steps, forward, 0)
        edge_rows(heads, (2, 3), grads, 0)
        go(("edge", 3), lambda: last_copy(1))

        @pl.when(here.core == 1)
        def _():
            after_copy(1).start()

        lags[...] = jnp.zeros_like(lags)

        def turn(index, carry):
            turned[tile(index, 128), :] = acts[:, tile(index, 128)].T
            return carry

        lax.fori_loop(3 * steps, 4 * steps, turn, 0)
        out_load.wait()

        def branch_product(index, carry):
            cols = tile(index, chans)
            value = jnp.dot(acts[:, pl.ds(3 * chans, chans)], out_w[:, cols], preferred_element_type=f32)
            part[:, cols] = value.astype(bf16)
            return carry

        lax.fori_loop(0, width // chans, branch_product, 0)

        for slot in (3, 4, 7, 8, 9):
            arrived(1, slot)
        tp_begin(0)
        for_sibling(0, sib, 0)
        for_sibling(0, sib, 1)
        for_sibling(0, sib, 2)
        for_self(0, sib, 0)
        y_go(0, 0, 0)
        y_go(0, 0, 1)
        for_sibling(0, sib, 3)
        for_self(0, sib, 1)
        y_go(0, 0, 2)
        for_self(0, sib, 2)
        y_go(0, 0, 3)
        value = lax.dot_general(both[1], out_w[...], (((1,), (1,)), ((), ())), preferred_element_type=f32)
        for index in range(8):
            rows = pl.ds(index * span, span)
            grads[0, pl.ds(index * wide, span), :] = value[index * span : (index + 1) * span] * query[rows, :]
            grads[1, pl.ds(index * wide, span), :] = value[index * span : (index + 1) * span] * gates[rows, :]
        edge_rows(heads, (0, 1), grads, 0)
        go(("edge", 2), lambda: last_copy(0))

        @pl.when(here.core == 1)
        def _():
            after_copy(0).start()

        y_pass(0, 0)
        for index in range(4, 8):
            for_sibling(0, sib, index)
            for_self(0, sib, index - 1)
            if index == 5:
                y_go(0, 1, 0)
                y_go(0, 1, 1)
            if index == 6:
                y_go(0, 1, 2)
            if index == 7:
                y_go(0, 1, 3)
        for_self(0, sib, 7)
        for which in range(2):
            last_copy(which).wait_recv()
            share(after_in, ((0, 1), (2, 3))[which], lambda which=which: after_copy(which), heads)
        ended = (here.core == 1) & (here.y == 3) & (here.last_block() == 1)
        for kind in range(4):
            kept = jnp.where(ended, 0.0, 1.0).astype(f32) if kind < 2 else 1.0
            grads[kind, pl.ds(7 * wide + span, 8), :] = last_in[kind] * kept
            for pair in range(4):
                rows = after_in[kind, pl.ds(pair * 16, 16), :].astype(f32)
                if pair > 0:
                    grads[kind, pl.ds((2 * pair - 1) * wide + span, 8), :] = rows[:8]
                grads[kind, pl.ds(2 * pair * wide + span, 8), :] = rows[8:]

        def turn_tile(index):
            rows = tile(index // steps, 128)
            for kind in range(3):
                cols = tile(kind * steps + index % steps, 128)
                turned[cols, rows] = acts[rows, cols].T

        def backward(index, carry):
            turn_tile(jnp.maximum(index - 1, 0))
            for part_of in range(2):
                backward_band((index // steps) * 2 + part_of, index % steps)
            return carry

        def backward_band(band, column):
            begin = pl.multiple_of(band * span, span)
            first = pl.multiple_of(band * wide, 8)
            cols = tile(column, 128)
            rows = pl.ds(first, wide)
            here_rows = pl.ds(begin, span)

            def add_lag(row, value):
                lags[row, :, cols] += jnp.sum(value.reshape(span // 8, 8, 128), axis=0)

            gated = grads[0, rows, cols]
            product = prods[here_rows, cols]
            total = inner(0, cols) * gated
            add_lag(9, gated[:span] * product)
            for lag in range(1, 7):
                moved = ahead(gated, lag)
                total = total + inner(lag, cols) * moved
                add_lag(9 + lag, moved[:span] * product)
            feats = (grads[1, rows, cols], total * grads[2, rows, cols], total * grads[3, rows, cols])
            for kind in range(3):
                feat = feats[kind]
                held = proj[kind, pl.ds(pl.multiple_of(first + 8, 8), span), cols]
                summed = short(0, kind, cols) * feat[:span]
                add_lag(kind, feat[:span] * held)
                for lag in (1, 2):
                    moved = ahead(feat, lag)[:span]
                    summed = summed + short(lag, kind, cols) * moved
                    add_lag(lag * 3 + kind, moved * held)
                acts[here_rows, tile(kind * steps + column, 128)] = summed.astype(bf16)

        tiles = (bands // 2) * steps
        lax.fori_loop(0, tiles - steps, backward, 0)
        y_pass(0, 1)
        tp_halves(0)
        tp_last(0)
        lax.fori_loop(tiles - steps, tiles, backward, 0)
        turn_tile(tiles - 1)
        lag_sum[0] = jnp.sum(lags[...], axis=1) * scale
        go(("lag", 0), lambda: lag_copy(0))
        x_begin(0)
        for index in (0, 2, 3):
            drained(("edge", index))

        @pl.when(here.core == 1)
        def _():
            before_copy().wait_send()
            after_copy(0).wait_send()
            after_copy(1).wait_send()

        for index in range(4, 8):
            drained(("sib", 0, index))

    def reduce_phase(in_w, sib):
        def in_loads(step, slot):
            return [
                pltpu.make_async_copy(
                    in_w_hbm.at[kind, tile(step, step_in), :], in_w.at[slot, :, pl.ds(kind * chans, chans)],
                    in_w_sem.at[slot, kind])
                for kind in range(3)
            ]

        for step in range(2):
            for copy in in_loads(step, step):
                copy.start()

        def gnorm_product(first, count):
            def loop(step, carry):
                slot = step % 2
                for copy in in_loads(step, slot):
                    copy.wait()
                value = lax.dot_general(
                    acts[:, pl.ds(0, 3 * chans)], in_w[slot], (((1,), (1,)), ((), ())), preferred_element_type=f32)
                out_w[:, tile(step, step_in)] = value.astype(bf16)

                @pl.when(step + 2 < width // step_in)
                def _():
                    for copy in in_loads(step + 2, slot):
                        copy.start()

                return carry

            lax.fori_loop(first, first + count, loop, 0)

        for_sibling(1, sib, 0)
        for_sibling(1, sib, 1)
        for_self(1, sib, 0)
        y_go(1, 0, 0)
        y_go(1, 0, 1)
        tp_direct(0)
        for_sibling(1, sib, 2)
        for_self(1, sib, 1)
        y_go(1, 0, 2)
        for_sibling(1, sib, 3)
        for_self(1, sib, 2)
        y_go(1, 0, 3)
        lag_step(0)
        x_on(0)
        in_steps = width // step_in
        gnorm_product(0, in_steps // 2)
        y_pass(1, 0)
        gnorm_product(in_steps // 2, in_steps // 2)
        tp_begin(1)
        for_sibling(1, sib, 4)
        for_sibling(1, sib, 5)
        for_self(1, sib, 4)
        y_go(1, 1, 0)
        y_go(1, 1, 1)
        lag_step(1)
        for_sibling(1, sib, 6)
        for_self(1, sib, 5)
        y_go(1, 1, 2)
        for_sibling(1, sib, 7)
        for_self(1, sib, 6)
        y_go(1, 1, 3)
        for_self(1, sib, 3)
        for_self(1, sib, 7)
        tp_halves(1)
        tp_last(1)
        lag_step(2)
        x_begin(1)
        for slot in (5, 6, 7):
            tp_copy(0, slot).wait_recv()

        def layer_finish(index, carry):
            at, total = tp_total(0, index)
            layer_ref[at, :] = (hidden[at, :].astype(f32) + total).astype(bf16)
            return carry

        lax.fori_loop(0, block // 16, layer_finish, 0)
        result(0).start()
        tp_direct(1)
        for side in range(2):
            x_forward(0, side).wait_recv()
        y_done(0, 1)
        last(0, 0)
        last(0, 1)
        result(3).start()
        lag_step(3)
        result(4).start()
        y_pass(1, 1)
        x_on(1)
        for slot in (5, 6, 7):
            tp_copy(1, slot).wait_recv()

        def input_finish(index, carry):
            at, total = tp_total(1, index)
            floats = hidden[at, :].astype(f32)
            factor = lax.rsqrt(jnp.mean(floats * floats, axis=-1, keepdims=True) + 1e-05)
            gained = total * gain[...]
            inner = jnp.mean(floats * gained, axis=-1, keepdims=True) * factor * factor * factor
            input_ref[at, :] = (cot[at, :].astype(f32) + gained * factor - floats * inner).astype(bf16)
            return carry

        lax.fori_loop(0, block // 16, input_finish, 0)
        result(1).start()
        for side in range(2):
            x_forward(1, side).wait_recv()
        y_done(1, 1)
        last(1, 0)
        last(1, 1)
        result(2).start()
        for name in list(sends):
            drained(name)
        for index in range(5):
            result(index).wait()

    pl.run_scoped(gather_phase, pltpu.VMEM((3, width, chans), bf16))
    pl.run_scoped(
        filter_phase,
        pltpu.VMEM((tokens, chans), f32),
        pltpu.VMEM((tokens, chans), f32),
        pltpu.VMEM((tokens, chans), f32),
        pltpu.VMEM((4, bands * wide, chans), f32),
        pltpu.VMEM((3, bands * 8, chans), bf16),
        pltpu.VMEM((4, bands * 8, chans), bf16),
        pltpu.VMEM((4, chans, cut), bf16),
    )
    pl.run_scoped(
        reduce_phase, pltpu.VMEM((2, step_in, 3 * chans), bf16), pltpu.VMEM((4, 3 * chans, cut), bf16)
    )


def layer_results(hidden, cot, gain, short_taps, inner_taps, in_weight, out_weight, tokens, scale):
    block, width = hidden.shape
    chans = out_weight.shape[0]
    cut = width // 16
    any_space = pl.BlockSpec(memory_space=pl.ANY)
    bf16, f32 = jnp.bfloat16, jnp.float32
    dma = pltpu.SemaphoreType.DMA
    body = lambda *refs: layer_kernel(scale, tokens, *refs)
    return pl.pallas_call(
        body,
        out_shape=(
            jax.ShapeDtypeStruct((block, width), bf16),
            jax.ShapeDtypeStruct((block, width), bf16),
            jax.ShapeDtypeStruct((3, cut, chans), bf16),
            jax.ShapeDtypeStruct((chans, cut), bf16),
            jax.ShapeDtypeStruct((16, chans), f32),
        ),
        in_specs=[any_space] * 7,
        out_specs=(any_space,) * 5,
        scratch_shapes=[
            pltpu.VMEM(hidden.shape, bf16),
            pltpu.VMEM(cot.shape, bf16),
            pltpu.VMEM(gain.shape, f32),
            pltpu.VMEM(short_taps.shape, f32),
            pltpu.VMEM(inner_taps.shape, f32),
            pltpu.VMEM((block, width), bf16),
            pltpu.VMEM((block, width), bf16),
            pltpu.VMEM((3, cut, chans), bf16),
            pltpu.VMEM((chans, cut), bf16),
            pltpu.VMEM((16, chans), f32),
            pltpu.VMEM((2, tokens, width), bf16),
            pltpu.VMEM(out_weight.shape, bf16),
            pltpu.VMEM((3, tokens + 64, chans), f32),
            pltpu.VMEM((3, 8, chans), f32),
            pltpu.VMEM((3, 64, chans), bf16),
            pltpu.VMEM((4, 8, chans), f32),
            pltpu.VMEM((4, 64, chans), bf16),
            pltpu.VMEM((16, 8, chans), f32),
            pltpu.VMEM((tokens, 4 * chans), bf16),
            pltpu.VMEM((4 * chans, tokens), bf16),
            pltpu.VMEM((tokens, width), bf16),
            pltpu.VMEM((8, chans, cut), bf16),
            pltpu.VMEM((8, 3 * chans, cut), bf16),
            pltpu.VMEM((2, 6, chans // 2, cut), bf16),
            pltpu.VMEM((2, 6, 3 * chans // 2, cut), bf16),
            pltpu.VMEM((2, chans // 2, cut), bf16),
            pltpu.VMEM((2, 3 * chans // 2, cut), bf16),
            pltpu.VMEM((2, chans // 2, cut), bf16),
            pltpu.VMEM((2, 3 * chans // 2, cut), bf16),
            pltpu.VMEM((2, 7, block, width), bf16),
            pltpu.VMEM((4, 16, chans), f32),
            pltpu.VMEM((4, 16, chans), f32),
            dma((4,)), dma((5,)), dma((5,)), dma((2, 3)), dma((2, 10)), dma((2, 10)), dma((6,)), dma((6,)),
            dma((2, 8)), dma((2, 8)), dma((2, 2, 6)), dma((2, 2, 6)), dma((2, 4)), dma((2, 4)),
            dma((2, 8)), dma((2, 8)), dma((4,)), dma((4,)),
        ],
        compiler_params=pltpu.CompilerParams(
            collective_id=0, has_side_effects=True, vmem_limit_bytes=63 * 2**20
        ),
        name="whole_layer",
    )(hidden, cot, gain, short_taps, inner_taps, in_weight, out_weight)


def place_kernel(
    layer, grad, kinds, outer, lags, layer_to, grad_to, kinds_to, outer_to, short_to, inner_to,
    layer_at, grad_at, kinds_at, outer_at, lags_at, short_at, inner_at, read_sems, write_sems,
):
    ends = (
        (lags, lags_at, None), (kinds, kinds_at, kinds_to), (layer, layer_at, layer_to), (grad, grad_at, grad_to),
        (outer, outer_at, outer_to), (None, short_at, short_to), (None, inner_at, inner_to),
    )
    reads = [pltpu.make_async_copy(ends[index][0], ends[index][1], read_sems.at[index]) for index in range(5)]
    writes = [pltpu.make_async_copy(ends[index][1], ends[index][2], write_sems.at[index - 1]) for index in range(1, 7)]
    for copy in reads:
        copy.start()
    reads[0].wait()
    for lag in range(3):
        short_at[lag] = lags_at[pl.ds(3 * lag, 3), :]
    inner_at[...] = lags_at[pl.ds(9, 7), :]
    writes[4].start()
    writes[5].start()
    for index in range(4):
        reads[index + 1].wait()
        writes[index].start()
    for copy in writes:
        copy.wait()


def placed_results(layer, grad, kinds, outer, lags):
    chans = lags.shape[1]
    any_space = pl.BlockSpec(memory_space=pl.ANY)
    arrays = (layer, grad, kinds, outer)
    ends = ((3, 3, chans), (7, chans))
    return pl.pallas_call(
        place_kernel,
        out_shape=tuple(jax.ShapeDtypeStruct(array.shape, array.dtype) for array in arrays)
        + tuple(jax.ShapeDtypeStruct(shape, jnp.float32) for shape in ends),
        in_specs=[any_space] * 5,
        out_specs=(any_space,) * 6,
        scratch_shapes=[pltpu.VMEM(array.shape, array.dtype) for array in (*arrays, lags)]
        + [pltpu.VMEM(shape, jnp.float32) for shape in ends]
        + [pltpu.SemaphoreType.DMA((5,)), pltpu.SemaphoreType.DMA((6,))],
        compiler_params=pltpu.CompilerParams(vmem_limit_bytes=60 * 2**20),
        name="place_results",
    )(layer, grad, kinds, outer, lags)


def local(hidden_in, cotangent, norm_gain, in_weight, filter_taps, inner_taps, out_weight):
    tokens = hidden_in.shape[0] * lax.axis_size("tp")
    scale = (tokens * lax.axis_size("ctx")) ** (-0.5)
    gain = norm_gain.reshape(1, -1)
    kinds = jnp.transpose(in_weight, (1, 0, 2))
    layer_out, grad_input, grad_kinds, grad_out_weight, grad_filter, grad_inner = placed_results(
        *layer_results(hidden_in, cotangent, gain, filter_taps, inner_taps, kinds, out_weight, tokens, scale)
    )
    return (layer_out, grad_input, jnp.transpose(grad_kinds, (1, 0, 2)), grad_out_weight, grad_filter, grad_inner)


def solution(mesh):
    placed = (
        P(("ctx", "tp"), None),
        P(("ctx", "tp"), None),
        P(),
        P(None, None, "tp"),
        P(None, None, "tp"),
        P(None, "tp"),
        P("tp", None),
    )
    return jax.shard_map(
        local,
        mesh=mesh,
        in_specs=placed,
        out_specs=(
            P(("ctx", "tp"), None),
            P(("ctx", "tp"), None),
            P("ctx", None, "tp"),
            P("tp", "ctx"),
            P(None, None, "tp"),
            P(None, "tp"),
        ),
        check_vma=False,
    )
```

```python
import jax
import jax.numpy as jnp
from jax import lax
from jax.experimental import pallas as pl
from jax.experimental.pallas import tpu as pltpu
from jax.sharding import PartitionSpec as P

MESH = pl.DeviceIdType.MESH
DELTAS = (2, 1, 3, 0)


class Place:
    def __init__(self):
        ctx, tp = lax.axis_index("ctx"), lax.axis_index("tp")
        self.y, self.x_hi, self.core = ctx // 4, (ctx // 2) % 2, ctx % 2
        self.z, self.x_lo = tp // 2, tp % 2
        self.ctx, self.tp = ctx, tp

    def sibling(self):
        return (self.y * 4 + self.x_hi * 2 + 1 - self.core, self.tp)

    def along_y(self, step):
        return (((self.y + step) % 4) * 4 + self.x_hi * 2 + self.core, self.tp)

    def along_z(self, step):
        return (self.ctx, ((self.z + step) % 4) * 2 + self.x_lo)

    def along_x(self, step):
        x = (self.x_hi * 2 + self.x_lo + step) % 4
        return (self.y * 4 + (x // 2) * 2 + self.core, self.z * 2 + x % 2)

    def at(self, y, x, core):
        return (y * 4 + (x // 2) * 2 + core, self.z * 2 + x % 2)

    def partner(self):
        return self.along_x((1 - 2 * self.core) * (1 - 2 * self.x_lo))

    def last_block(self):
        x_hi, x_lo = self.x_hi, self.x_lo
        return jnp.where(self.core == 1, x_hi * x_lo + (1 - x_hi) * (1 - x_lo), x_hi)

    def following(self):
        x_hi, x_lo, core = self.x_hi, self.x_lo, self.core
        held = x_hi * x_lo + (1 - x_hi) * (1 - x_lo)
        x = (1 - core) * ((2 * x_hi + 3 * x_lo) % 4) + core * ((1 - held) * 2 + x_lo)
        return self.at((self.y + core * held) % 4, x, 1 - core)

    def preceding(self):
        x_hi, x_lo, core = self.x_hi, self.x_lo, self.core
        held = x_hi * (1 - x_lo) + (1 - x_hi) * x_lo
        x = core * (held * 2 + x_lo) + (1 - core) * (((1 - x_hi) * 2 + 2 - x_lo) % 4)
        return self.at((self.y - (1 - core) * (1 - x_hi)) % 4, x, 1 - core)

    def block(self, step, same):
        x_lo = self.x_lo if same else 1 - self.x_lo
        return ((self.z + step) % 4) * 2 + x_lo


def remote(source, target, send, recv, device):
    return pltpu.make_async_remote_copy(
        src_ref=source, dst_ref=target, send_sem=send, recv_sem=recv, device_id=device, device_id_type=MESH
    )


def tile(index, size):
    return pl.ds(pl.multiple_of(index * size, size), size)


def layer_kernel(
    scale, tokens,
    hidden_hbm, cot_hbm, gain_hbm, short_hbm, inner_hbm, in_w_hbm, out_w_hbm,
    layer_hbm, input_hbm, in_grad_hbm, out_grad_hbm, lag_hbm,
    hidden, cot, gain, short_taps, inner_taps, layer_ref, input_ref, in_grad_ref, out_grad_ref, lag_ref,
    both, out_w, proj, first_in, before_in, last_in, after_in, lags, acts, turned, part,
    sums_out, sums_in, y_out, y_in, pass_out, pass_in, x_out, x_in, tp_in, lag_sum, lag_got,
    load_sem, row_sem, result_sem, in_w_sem, send_sem, recv_sem, edge_send, edge_recv,
    sib_send, sib_recv, y_send, y_recv, x_send, x_recv, tp_send, tp_recv, lag_send, lag_recv,
):
    here = Place()
    block, width = hidden.shape
    chans = out_w_hbm.shape[0]
    cut = width // 16
    half = block // 2
    group = 2 * block
    wide, span = 72, 64
    steps = chans // 128
    bands = tokens // span
    step_in = 512
    x_cols = ((width // 128 * 3 // 4) * 128, (width // 128 // 2) * 128)
    bf16, f32 = jnp.bfloat16, jnp.float32

    out_load = pltpu.make_async_copy(out_w_hbm, out_w, load_sem.at[3])
    barrier = pltpu.get_barrier_semaphore()
    devices = [
        here.sibling(), here.along_y(1), here.along_y(-1), here.along_y(2), here.along_z(1), here.along_z(-1),
        here.along_x(1), here.along_x(-1), here.along_x(2), here.following(), here.preceding(),
    ]
    for device in devices:
        pl.semaphore_signal(barrier, inc=1, device_id=device, device_id_type=MESH)
    row_loads = [
        pltpu.make_async_copy(source, target, row_sem.at[index])
        for index, (source, target) in enumerate(
            ((hidden_hbm, hidden), (cot_hbm, cot), (gain_hbm, gain), (short_hbm, short_taps), (inner_hbm, inner_taps)))
    ]
    for copy in row_loads:
        copy.start()

    def result(index):
        source, target = (
            (layer_ref, layer_hbm), (input_ref, input_hbm), (in_grad_ref, in_grad_hbm),
            (out_grad_ref, out_grad_hbm), (lag_ref, lag_hbm),
        )[index]
        return pltpu.make_async_copy(source, target, result_sem.at[index])

    sends = {}

    def go(name, build):
        build().start()
        sends[name] = build

    def drained(name):
        sends.pop(name)().wait_send()


    def rows_of(step, same, begin=0, size=block):
        return pl.ds(pl.multiple_of(here.block(step, same) * block + begin, size), size)

    every = pl.ds(0, width)

    def slot_cols(which, slot):
        by_x = pl.ds(0, x_cols[which])
        by_z = pl.ds(x_cols[which], width - x_cols[which])
        return (every, every, every, by_z, by_z, every, every, every, by_x, by_x)[slot]

    def gather_copy(which, slot):
        rows, device = (
            lambda: (rows_of(0, True), here.partner()),
            lambda: (rows_of(0, True), here.along_z(1)),
            lambda: (rows_of(0, True), here.along_z(-1)),
            lambda: (rows_of(0, False), here.along_z(1)),
            lambda: (rows_of(0, False), here.along_z(-1)),
            lambda: (rows_of(-1, True, 0, half), here.along_z(1)),
            lambda: (rows_of(1, True, half, half), here.along_z(-1)),
            lambda: (rows_of(2, True), here.partner()),
            lambda: (rows_of(-1, True), here.partner()),
            lambda: (rows_of(1, True), here.partner()),
        )[slot]()
        held = both.at[which, rows, slot_cols(which, slot)]
        return remote(held, held, send_sem.at[which, slot], recv_sem.at[which, slot], device)

    def gather(which, slot):
        go(("gather", which, slot), lambda: gather_copy(which, slot))

    def arrived(which, slot):
        rows = (
            lambda: rows_of(0, False),
            lambda: rows_of(-1, True),
            lambda: rows_of(1, True),
            lambda: rows_of(-1, False),
            lambda: rows_of(1, False),
            lambda: rows_of(2, True, 0, half),
            lambda: rows_of(2, True, half, half),
            lambda: rows_of(2, False),
            lambda: rows_of(-1, False),
            lambda: rows_of(1, False),
        )[slot]()
        held = both.at[which, rows, slot_cols(which, slot)]
        remote(held, held, send_sem.at[which, slot], recv_sem.at[which, slot], here.partner()).wait_recv()


    parts = (part, out_w)

    def tp_copy(which, slot):
        source, held = parts[which], tp_in.at[which]
        first = pl.ds(0, half)
        second = pl.ds(half, half)
        rows, place, device = (
            lambda: (rows_of(2, False), held.at[0], here.partner()),
            lambda: (rows_of(1, False), held.at[1], here.along_z(1)),
            lambda: (rows_of(-1, False), held.at[2], here.along_z(-1)),
            lambda: (rows_of(2, True, 0, half), held.at[3, first], here.along_z(1)),
            lambda: (rows_of(2, True, half, half), held.at[3, second], here.along_z(-1)),
            lambda: (rows_of(1, True), held.at[4], here.along_z(1)),
            lambda: (rows_of(-1, True), held.at[5], here.along_z(-1)),
            lambda: (rows_of(0, False), held.at[6], here.partner()),
        )[slot]()
        return remote(source.at[rows], place, tp_send.at[which, slot], tp_recv.at[which, slot], device)

    def tp_go(which, slot):
        go(("tp", which, slot), lambda: tp_copy(which, slot))

    def add_rows(ref, base, length, others, size=128):
        def loop(index, carry):
            at = tile(index, size)
            rows = pl.ds(pl.multiple_of(base + index * size, size), size)
            total = ref[rows, :].astype(f32)
            for other in others:
                total = total + other[at, :].astype(f32)
            ref[rows, :] = total.astype(bf16)
            return carry

        lax.fori_loop(0, length // size, loop, 0)

    def tp_begin(which):
        for slot in range(3):
            tp_go(which, slot)

    def tp_halves(which):
        tp_copy(which, 0).wait_recv()
        add_rows(parts[which], here.block(2, True) * block, block, [tp_in.at[which, 0]], 16)
        tp_go(which, 3)
        tp_go(which, 4)

    def tp_direct(which):
        tp_copy(which, 3).wait_recv()
        add_rows(parts[which], here.block(1, True) * block, half, [tp_in.at[which, 3, pl.ds(0, half)]], 16)
        tp_go(which, 5)
        tp_copy(which, 4).wait_recv()
        add_rows(
            parts[which], here.block(-1, True) * block + half, half, [tp_in.at[which, 3, pl.ds(half, half)]], 16)
        tp_go(which, 6)

    def tp_last(which):
        tp_copy(which, 1).wait_recv()
        tp_copy(which, 2).wait_recv()
        add_rows(parts[which], here.block(0, False) * block, block, [tp_in.at[which, 1], tp_in.at[which, 2]], 16)
        tp_go(which, 7)

    def tp_total(which, index):
        at = tile(index, 16)
        rows = pl.ds(pl.multiple_of(here.tp * block + index * 16, 16), 16)
        total = parts[which][rows, :].astype(f32)
        for slot in (4, 5, 6):
            total = total + tp_in[which, slot, at, :].astype(f32)
        return at, total


    sums = (sums_out, sums_in)
    arriving = (y_out, y_in)
    passing = (pass_out, pass_in)
    crossing = (x_out, x_in)

    def halves(kind):
        size = sums[kind].shape[1] // 2
        return pl.ds(0, size), pl.ds(size, size), size

    def target(index, core):
        y = (here.y + DELTAS[index % 4]) % 4
        x_hi = 1 - here.x_hi if index < 4 else here.x_hi
        return y * 4 + x_hi * 2 + core

    def product(kind, index, core, write):
        cols = tile(target(index, core), cut)

        def one(step, carry):
            rows = tile(step, chans)
            first = 3 * chans if kind == 0 else 0
            left = turned[pl.ds(pl.multiple_of(first + step * chans, chans), chans), :]
            value = jnp.dot(left, both[1 - kind, :, cols], preferred_element_type=f32)
            write(rows, value * scale)
            return carry

        lax.fori_loop(0, (1, 3)[kind], one, 0)

    def sib_copy(kind, sib, index):
        return remote(
            sib.at[index % 4], sums[kind].at[index], sib_send.at[kind, index], sib_recv.at[kind, index],
            here.sibling())

    def for_sibling(kind, sib, index):
        if index >= 4:
            drained(("sib", kind, index - 4))

        def write(rows, value):
            sib[index % 4, rows, :] = value.astype(bf16)

        product(kind, index, 1 - here.core, write)
        go(("sib", kind, index), lambda: sib_copy(kind, sib, index))

    def for_self(kind, sib, index):
        sib_copy(kind, sib, index).wait_recv()

        def write(rows, value):
            held = sums[kind][index, rows, :].astype(f32)
            sums[kind][index, rows, :] = (held + value).astype(bf16)

        product(kind, index, here.core, write)

    def y_copy(kind, far, slot):
        upper, lower, _ = halves(kind)
        index, rows, step = (
            (0, upper, 1), (0, lower, -1), (1, lower, 1), (2, upper, -1), (1, upper, 1), (2, lower, -1)
        )[slot]
        return remote(
            sums[kind].at[far * 4 + index, rows], arriving[kind].at[far, slot],
            y_send.at[kind, far, slot], y_recv.at[kind, far, slot], here.along_y(step),
        )

    def y_go(kind, far, slot):
        go(("y", kind, far, slot), lambda: y_copy(kind, far, slot))

    def y_pass(kind, far):
        size = halves(kind)[2]
        y_copy(kind, far, 0).wait_recv()
        add_rows(sums[kind].at[far * 4 + 1], 0, size, [arriving[kind].at[far, 0]])
        y_go(kind, far, 4)
        y_copy(kind, far, 1).wait_recv()
        add_rows(sums[kind].at[far * 4 + 2], size, size, [arriving[kind].at[far, 1]])
        y_go(kind, far, 5)

    def y_done(kind, far):
        for slot in (3, 4, 2, 5):
            y_copy(kind, far, slot).wait_recv()

    def x_copy(kind, side):
        rows = halves(kind)[side]
        return remote(
            sums[kind].at[3, rows], passing[kind].at[side], x_send.at[kind, side], x_recv.at[kind, side],
            here.along_x((1, -1)[side]))

    def x_forward(kind, side):
        return remote(
            passing[kind].at[side], crossing[kind].at[side], x_send.at[kind, 2 + side], x_recv.at[kind, 2 + side],
            here.along_x((1, -1)[side]))

    def x_begin(kind):
        size = halves(kind)[2]
        y_done(kind, 0)
        add_rows(sums[kind].at[3], 0, size, [arriving[kind].at[0, 3], arriving[kind].at[0, 4]])
        go(("x", kind, 0), lambda: x_copy(kind, 0))
        add_rows(sums[kind].at[3], size, size, [arriving[kind].at[0, 2], arriving[kind].at[0, 5]])
        go(("x", kind, 1), lambda: x_copy(kind, 1))

    def x_go(kind, side):
        go(("x", kind, 2 + side), lambda: x_forward(kind, side))

    def x_on(kind):
        for side in range(2):
            x_copy(kind, side).wait_recv()
            x_go(kind, side)

    def last(kind, side):
        size = halves(kind)[2]
        begin = side * size
        others = [arriving[kind].at[1, slot] for slot in ((3, 4), (2, 5))[side]] + [crossing[kind].at[side]]
        for index in range(size // 128):
            row = begin + index * 128
            total = sums[kind][7, pl.ds(row, 128), :].astype(f32)
            for other in others:
                total = total + other[pl.ds(index * 128, 128), :].astype(f32)
            if kind == 1:
                in_grad_ref[row // chans, :, pl.ds(row % chans, 128)] = total.T.astype(bf16)
            else:
                out_grad_ref[pl.ds(row, 128), :] = total.astype(bf16)

    def lag_copy(step):
        device = (
            lambda: here.sibling(),
            lambda: here.along_x(2),
            lambda: here.along_y(1 - 2 * (here.y % 2)),
            lambda: here.along_y(2),
        )[step]()
        return remote(lag_sum.at[step], lag_got.at[step], lag_send.at[step], lag_recv.at[step], device)

    def lag_step(step):
        lag_copy(step).wait_recv()
        total = lag_sum[step] + lag_got[step]
        if step < 3:
            lag_sum[step + 1] = total
            go(("lag", step + 1), lambda: lag_copy(step + 1))
        else:
            lag_ref[...] = total

    def gather_phase(in_w):
        loads = [pltpu.make_async_copy(in_w_hbm.at[kind], in_w.at[kind], load_sem.at[kind]) for kind in range(3)]
        for copy in loads:
            copy.start()
        out_load.start()
        for copy in row_loads:
            copy.wait()

        def normalise(index, carry):
            at = tile(index, 16)
            rows = pl.ds(pl.multiple_of(here.tp * block + index * 16, 16), 16)
            floats = hidden[at, :].astype(f32)
            factor = lax.rsqrt(jnp.mean(floats * floats, axis=-1, keepdims=True) + 1e-05)
            both[0, rows, :] = (floats * factor * gain[...]).astype(bf16)
            both[1, rows, :] = cot[at, :]
            return carry

        lax.fori_loop(0, block // 16, normalise, 0)
        pl.semaphore_wait(barrier, len(devices))

        def project(step):
            begin = ((here.z + step) % 4) * group

            def loop(kind, carry):
                value = jnp.dot(
                    both[0, pl.ds(pl.multiple_of(begin, group), group), :], in_w[kind], preferred_element_type=f32
                )
                value = value.astype(bf16).astype(f32)
                for index in range(2):
                    first = (begin // block + index) * wide + 8
                    proj[kind, pl.ds(pl.multiple_of(first, 8), block), :] = value[index * block : (index + 1) * block]
                return carry

            lax.fori_loop(0, 3, loop, 0)

        for slot in range(3):
            gather(0, slot)
        gather(1, 0)
        arrived(0, 1)
        gather(0, 5)
        gather(0, 8)
        arrived(0, 2)
        gather(0, 6)
        gather(0, 9)
        arrived(0, 0)
        gather(0, 3)
        gather(0, 4)
        for copy in loads:
            copy.wait()
        project(0)
        arrived(0, 5)
        arrived(0, 6)
        gather(0, 7)
        gather(1, 1)
        gather(1, 2)
        arrived(0, 3)
        arrived(0, 8)
        project(-1)
        arrived(0, 4)
        arrived(0, 9)
        project(1)
        arrived(0, 7)
        project(2)

    def filter_phase(query, gates, prods, grads, ends, heads, sib):
        def first_copy():
            return remote(
                proj.at[:, pl.ds(7 * wide + span, 8), :], first_in, edge_send.at[0], edge_recv.at[0], here.following())

        def before_copy():
            return remote(ends, before_in, edge_send.at[1], edge_recv.at[1], here.along_x(2))

        def last_copy(which):
            kinds = pl.ds((0, 2)[which], 2)
            return remote(
                grads.at[kinds, pl.ds(0, 8), :], last_in.at[kinds], edge_send.at[2 + which], edge_recv.at[2 + which],
                here.preceding())

        def after_copy(which):
            kinds = pl.ds((0, 2)[which], 2)
            return remote(
                heads.at[kinds], after_in.at[kinds], edge_send.at[4 + which], edge_recv.at[4 + which],
                here.along_x(2))

        def edge_rows(target, kinds, source, offset):
            for kind in kinds:
                for pair in range(4):
                    rows = [source[kind, pl.ds((2 * pair + index) * wide + offset, 8), :] for index in range(2)]
                    target[kind, pl.ds(pair * 16, 16), :] = jnp.concatenate(rows).astype(bf16)

        def share(target, kinds, copy, source):
            @pl.when(here.core == 1)
            def _():
                copy().wait_recv()

            @pl.when(here.core == 0)
            def _():
                for kind in kinds:
                    target[kind] = source[kind]

        edge_rows(ends, range(3), proj, span)
        go(("edge", 0), first_copy)

        @pl.when(here.core == 1)
        def _():
            before_copy().start()

        arrived(1, 1)
        gather(1, 5)
        gather(1, 8)
        arrived(1, 2)
        gather(1, 6)
        gather(1, 9)
        arrived(1, 0)
        arrived(1, 5)
        arrived(1, 6)
        gather(1, 7)
        gather(1, 3)
        gather(1, 4)
        first_copy().wait_recv()
        share(before_in, range(3), before_copy, ends)
        for kind in range(3):
            proj[kind, pl.ds(0, 8), :] = first_in[kind] * jnp.where(here.ctx == 0, 0.0, 1.0).astype(f32)
            for pair in range(4):
                rows = before_in[kind, pl.ds(pair * 16, 16), :].astype(f32)
                proj[kind, pl.ds((2 * pair + 1) * wide, 8), :] = rows[:8]
                if pair < 3:
                    proj[kind, pl.ds((2 * pair + 2) * wide, 8), :] = rows[8:]

        def short(lag, kind, cols):
            return short_taps[lag, pl.ds(kind, 1), cols]

        def inner(lag, cols):
            return inner_taps[pl.ds(lag, 1), cols]

        def behind(value, count):
            return pltpu.roll(value, count, 0)

        def ahead(value, count):
            return pltpu.roll(value, wide - count, 0)

        def forward(index, carry):
            begin = pl.multiple_of((index // steps) * span, span)
            first = pl.multiple_of((index // steps) * wide, 8)
            cols = tile(index % steps, 128)
            feats = []
            for kind in range(3):
                held = proj[kind, pl.ds(first, wide), cols]
                total = short(0, kind, cols) * held
                for lag in (1, 2):
                    total = total + short(lag, kind, cols) * behind(held, lag)
                feats.append(total)
            product = feats[1] * feats[2]
            total = inner(0, cols) * product
            for lag in range(1, 7):
                total = total + inner(lag, cols) * behind(product, lag)
            rows = pl.ds(begin, span)
            query[rows, cols] = feats[0][8:]
            grads[3, pl.ds(first, span), cols] = feats[1][8:]
            grads[2, pl.ds(first, span), cols] = feats[2][8:]
            gates[rows, cols] = total[8:]
            prods[rows, cols] = product[8:]
            acts[rows, tile(3 * steps + index % steps, 128)] = (feats[0][8:] * total[8:]).astype(bf16)
            return carry

        lax.fori_loop(0, bands * steps, forward, 0)
        edge_rows(heads, (2, 3), grads, 0)
        go(("edge", 3), lambda: last_copy(1))

        @pl.when(here.core == 1)
        def _():
            after_copy(1).start()

        lags[...] = jnp.zeros_like(lags)

        def turn(index, carry):
            turned[tile(index, 128), :] = acts[:, tile(index, 128)].T
            return carry

        lax.fori_loop(3 * steps, 4 * steps, turn, 0)
        out_load.wait()

        def branch_product(index, carry):
            cols = tile(index, chans)
            value = jnp.dot(acts[:, pl.ds(3 * chans, chans)], out_w[:, cols], preferred_element_type=f32)
            part[:, cols] = value.astype(bf16)
            return carry

        lax.fori_loop(0, width // chans, branch_product, 0)

        for slot in (3, 4, 7, 8, 9):
            arrived(1, slot)
        tp_begin(0)
        for_sibling(0, sib, 0)
        for_sibling(0, sib, 1)
        for_sibling(0, sib, 2)
        for_self(0, sib, 0)
        y_go(0, 0, 0)
        y_go(0, 0, 1)
        for_sibling(0, sib, 3)
        for_self(0, sib, 1)
        y_go(0, 0, 2)
        for_self(0, sib, 2)
        y_go(0, 0, 3)
        value = lax.dot_general(both[1], out_w[...], (((1,), (1,)), ((), ())), preferred_element_type=f32)
        for index in range(8):
            rows = pl.ds(index * span, span)
            grads[0, pl.ds(index * wide, span), :] = value[index * span : (index + 1) * span] * query[rows, :]
            grads[1, pl.ds(index * wide, span), :] = value[index * span : (index + 1) * span] * gates[rows, :]
        edge_rows(heads, (0, 1), grads, 0)
        go(("edge", 2), lambda: last_copy(0))

        @pl.when(here.core == 1)
        def _():
            after_copy(0).start()

        y_pass(0, 0)
        for index in range(4, 8):
            for_sibling(0, sib, index)
            for_self(0, sib, index - 1)
            if index == 5:
                y_go(0, 1, 0)
                y_go(0, 1, 1)
            if index == 6:
                y_go(0, 1, 2)
            if index == 7:
                y_go(0, 1, 3)
        for_self(0, sib, 7)
        for which in range(2):
            last_copy(which).wait_recv()
            share(after_in, ((0, 1), (2, 3))[which], lambda which=which: after_copy(which), heads)
        ended = (here.core == 1) & (here.y == 3) & (here.last_block() == 1)
        for kind in range(4):
            kept = jnp.where(ended, 0.0, 1.0).astype(f32) if kind < 2 else 1.0
            grads[kind, pl.ds(7 * wide + span, 8), :] = last_in[kind] * kept
            for pair in range(4):
                rows = after_in[kind, pl.ds(pair * 16, 16), :].astype(f32)
                if pair > 0:
                    grads[kind, pl.ds((2 * pair - 1) * wide + span, 8), :] = rows[:8]
                grads[kind, pl.ds(2 * pair * wide + span, 8), :] = rows[8:]

        def turn_tile(index):
            rows = tile(index // steps, 128)
            for kind in range(3):
                cols = tile(kind * steps + index % steps, 128)
                turned[cols, rows] = acts[rows, cols].T

        def backward(index, carry):
            turn_tile(jnp.maximum(index - 1, 0))
            for part_of in range(2):
                backward_band((index // steps) * 2 + part_of, index % steps)
            return carry

        def backward_band(band, column):
            begin = pl.multiple_of(band * span, span)
            first = pl.multiple_of(band * wide, 8)
            cols = tile(column, 128)
            rows = pl.ds(first, wide)
            here_rows = pl.ds(begin, span)

            def add_lag(row, value):
                lags[row, :, cols] += jnp.sum(value.reshape(span // 8, 8, 128), axis=0)

            gated = grads[0, rows, cols]
            product = prods[here_rows, cols]
            total = inner(0, cols) * gated
            add_lag(9, gated[:span] * product)
            for lag in range(1, 7):
                moved = ahead(gated, lag)
                total = total + inner(lag, cols) * moved
                add_lag(9 + lag, moved[:span] * product)
            feats = (grads[1, rows, cols], total * grads[2, rows, cols], total * grads[3, rows, cols])
            for kind in range(3):
                feat = feats[kind]
                held = proj[kind, pl.ds(pl.multiple_of(first + 8, 8), span), cols]
                summed = short(0, kind, cols) * feat[:span]
                add_lag(kind, feat[:span] * held)
                for lag in (1, 2):
                    moved = ahead(feat, lag)[:span]
                    summed = summed + short(lag, kind, cols) * moved
                    add_lag(lag * 3 + kind, moved * held)
                acts[here_rows, tile(kind * steps + column, 128)] = summed.astype(bf16)

        tiles = (bands // 2) * steps
        lax.fori_loop(0, tiles - steps, backward, 0)
        y_pass(0, 1)
        tp_halves(0)
        tp_last(0)
        lax.fori_loop(tiles - steps, tiles, backward, 0)
        turn_tile(tiles - 1)
        lag_sum[0] = jnp.sum(lags[...], axis=1) * scale
        go(("lag", 0), lambda: lag_copy(0))
        x_begin(0)
        for index in (0, 2, 3):
            drained(("edge", index))

        @pl.when(here.core == 1)
        def _():
            before_copy().wait_send()
            after_copy(0).wait_send()
            after_copy(1).wait_send()

        for index in range(4, 8):
            drained(("sib", 0, index))

    def reduce_phase(in_w, sib):
        def in_loads(step, slot):
            return [
                pltpu.make_async_copy(
                    in_w_hbm.at[kind, tile(step, step_in), :], in_w.at[slot, :, pl.ds(kind * chans, chans)],
                    in_w_sem.at[slot, kind])
                for kind in range(3)
            ]

        for step in range(2):
            for copy in in_loads(step, step):
                copy.start()

        def gnorm_product(first, count):
            def loop(step, carry):
                slot = step % 2
                for copy in in_loads(step, slot):
                    copy.wait()
                value = lax.dot_general(
                    acts[:, pl.ds(0, 3 * chans)], in_w[slot], (((1,), (1,)), ((), ())), preferred_element_type=f32)
                out_w[:, tile(step, step_in)] = value.astype(bf16)

                @pl.when(step + 2 < width // step_in)
                def _():
                    for copy in in_loads(step + 2, slot):
                        copy.start()

                return carry

            lax.fori_loop(first, first + count, loop, 0)

        for_sibling(1, sib, 0)
        for_sibling(1, sib, 1)
        for_self(1, sib, 0)
        y_go(1, 0, 0)
        y_go(1, 0, 1)
        tp_direct(0)
        for_sibling(1, sib, 2)
        for_self(1, sib, 1)
        y_go(1, 0, 2)
        for_sibling(1, sib, 3)
        for_self(1, sib, 2)
        y_go(1, 0, 3)
        lag_step(0)
        x_on(0)
        in_steps = width // step_in
        gnorm_product(0, in_steps // 2)
        y_pass(1, 0)
        gnorm_product(in_steps // 2, in_steps // 2)
        tp_begin(1)
        for_sibling(1, sib, 4)
        for_sibling(1, sib, 5)
        for_self(1, sib, 4)
        y_go(1, 1, 0)
        y_go(1, 1, 1)
        lag_step(1)
        for_sibling(1, sib, 6)
        for_self(1, sib, 5)
        y_go(1, 1, 2)
        for_sibling(1, sib, 7)
        for_self(1, sib, 6)
        y_go(1, 1, 3)
        for_self(1, sib, 3)
        for_self(1, sib, 7)
        tp_halves(1)
        tp_last(1)
        lag_step(2)
        x_begin(1)
        for slot in (5, 6, 7):
            tp_copy(0, slot).wait_recv()

        def layer_finish(index, carry):
            at, total = tp_total(0, index)
            layer_ref[at, :] = (hidden[at, :].astype(f32) + total).astype(bf16)
            return carry

        lax.fori_loop(0, block // 16, layer_finish, 0)
        result(0).start()
        tp_direct(1)
        for side in range(2):
            x_forward(0, side).wait_recv()
        y_done(0, 1)
        last(0, 0)
        last(0, 1)
        result(3).start()
        lag_step(3)
        result(4).start()
        y_pass(1, 1)
        x_on(1)
        for slot in (5, 6, 7):
            tp_copy(1, slot).wait_recv()

        def input_finish(index, carry):
            at, total = tp_total(1, index)
            floats = hidden[at, :].astype(f32)
            factor = lax.rsqrt(jnp.mean(floats * floats, axis=-1, keepdims=True) + 1e-05)
            gained = total * gain[...]
            inner = jnp.mean(floats * gained, axis=-1, keepdims=True) * factor * factor * factor
            input_ref[at, :] = (cot[at, :].astype(f32) + gained * factor - floats * inner).astype(bf16)
            return carry

        lax.fori_loop(0, block // 16, input_finish, 0)
        result(1).start()
        for side in range(2):
            x_forward(1, side).wait_recv()
        y_done(1, 1)
        last(1, 0)
        last(1, 1)
        result(2).start()
        for name in list(sends):
            drained(name)
        for index in range(5):
            result(index).wait()

    pl.run_scoped(gather_phase, pltpu.VMEM((3, width, chans), bf16))
    pl.run_scoped(
        filter_phase,
        pltpu.VMEM((tokens, chans), f32),
        pltpu.VMEM((tokens, chans), f32),
        pltpu.VMEM((tokens, chans), f32),
        pltpu.VMEM((4, bands * wide, chans), f32),
        pltpu.VMEM((3, bands * 8, chans), bf16),
        pltpu.VMEM((4, bands * 8, chans), bf16),
        pltpu.VMEM((4, chans, cut), bf16),
    )
    pl.run_scoped(
        reduce_phase, pltpu.VMEM((2, step_in, 3 * chans), bf16), pltpu.VMEM((4, 3 * chans, cut), bf16)
    )


def layer_results(hidden, cot, gain, short_taps, inner_taps, in_weight, out_weight, tokens, scale):
    block, width = hidden.shape
    chans = out_weight.shape[0]
    cut = width // 16
    any_space = pl.BlockSpec(memory_space=pl.ANY)
    bf16, f32 = jnp.bfloat16, jnp.float32
    dma = pltpu.SemaphoreType.DMA
    body = lambda *refs: layer_kernel(scale, tokens, *refs)
    return pl.pallas_call(
        body,
        out_shape=(
            jax.ShapeDtypeStruct((block, width), bf16),
            jax.ShapeDtypeStruct((block, width), bf16),
            jax.ShapeDtypeStruct((3, cut, chans), bf16),
            jax.ShapeDtypeStruct((chans, cut), bf16),
            jax.ShapeDtypeStruct((16, chans), f32),
        ),
        in_specs=[any_space] * 7,
        out_specs=(any_space,) * 5,
        scratch_shapes=[
            pltpu.VMEM(hidden.shape, bf16),
            pltpu.VMEM(cot.shape, bf16),
            pltpu.VMEM(gain.shape, f32),
            pltpu.VMEM(short_taps.shape, f32),
            pltpu.VMEM(inner_taps.shape, f32),
            pltpu.VMEM((block, width), bf16),
            pltpu.VMEM((block, width), bf16),
            pltpu.VMEM((3, cut, chans), bf16),
            pltpu.VMEM((chans, cut), bf16),
            pltpu.VMEM((16, chans), f32),
            pltpu.VMEM((2, tokens, width), bf16),
            pltpu.VMEM(out_weight.shape, bf16),
            pltpu.VMEM((3, tokens + 64, chans), f32),
            pltpu.VMEM((3, 8, chans), f32),
            pltpu.VMEM((3, 64, chans), bf16),
            pltpu.VMEM((4, 8, chans), f32),
            pltpu.VMEM((4, 64, chans), bf16),
            pltpu.VMEM((16, 8, chans), f32),
            pltpu.VMEM((tokens, 4 * chans), bf16),
            pltpu.VMEM((4 * chans, tokens), bf16),
            pltpu.VMEM((tokens, width), bf16),
            pltpu.VMEM((8, chans, cut), bf16),
            pltpu.VMEM((8, 3 * chans, cut), bf16),
            pltpu.VMEM((2, 6, chans // 2, cut), bf16),
            pltpu.VMEM((2, 6, 3 * chans // 2, cut), bf16),
            pltpu.VMEM((2, chans // 2, cut), bf16),
            pltpu.VMEM((2, 3 * chans // 2, cut), bf16),
            pltpu.VMEM((2, chans // 2, cut), bf16),
            pltpu.VMEM((2, 3 * chans // 2, cut), bf16),
            pltpu.VMEM((2, 7, block, width), bf16),
            pltpu.VMEM((4, 16, chans), f32),
            pltpu.VMEM((4, 16, chans), f32),
            dma((4,)), dma((5,)), dma((5,)), dma((2, 3)), dma((2, 10)), dma((2, 10)), dma((6,)), dma((6,)),
            dma((2, 8)), dma((2, 8)), dma((2, 2, 6)), dma((2, 2, 6)), dma((2, 4)), dma((2, 4)),
            dma((2, 8)), dma((2, 8)), dma((4,)), dma((4,)),
        ],
        compiler_params=pltpu.CompilerParams(
            collective_id=0, has_side_effects=True, vmem_limit_bytes=63 * 2**20
        ),
        name="whole_layer",
    )(hidden, cot, gain, short_taps, inner_taps, in_weight, out_weight)


def place_kernel(
    layer, grad, kinds, outer, lags, layer_to, grad_to, kinds_to, outer_to, short_to, inner_to,
    layer_at, grad_at, kinds_at, outer_at, lags_at, short_at, inner_at, read_sems, write_sems,
):
    ends = (
        (lags, lags_at, None), (kinds, kinds_at, kinds_to), (layer, layer_at, layer_to), (grad, grad_at, grad_to),
        (outer, outer_at, outer_to), (None, short_at, short_to), (None, inner_at, inner_to),
    )
    reads = [pltpu.make_async_copy(ends[index][0], ends[index][1], read_sems.at[index]) for index in range(5)]
    writes = [pltpu.make_async_copy(ends[index][1], ends[index][2], write_sems.at[index - 1]) for index in range(1, 7)]
    for copy in reads:
        copy.start()
    reads[0].wait()
    for lag in range(3):
        short_at[lag] = lags_at[pl.ds(3 * lag, 3), :]
    inner_at[...] = lags_at[pl.ds(9, 7), :]
    writes[4].start()
    writes[5].start()
    for index in range(4):
        reads[index + 1].wait()
        writes[index].start()
    for copy in writes:
        copy.wait()


def placed_results(layer, grad, kinds, outer, lags):
    chans = lags.shape[1]
    any_space = pl.BlockSpec(memory_space=pl.ANY)
    arrays = (layer, grad, kinds, outer)
    ends = ((3, 3, chans), (7, chans))
    return pl.pallas_call(
        place_kernel,
        out_shape=tuple(jax.ShapeDtypeStruct(array.shape, array.dtype) for array in arrays)
        + tuple(jax.ShapeDtypeStruct(shape, jnp.float32) for shape in ends),
        in_specs=[any_space] * 5,
        out_specs=(any_space,) * 6,
        scratch_shapes=[pltpu.VMEM(array.shape, array.dtype) for array in (*arrays, lags)]
        + [pltpu.VMEM(shape, jnp.float32) for shape in ends]
        + [pltpu.SemaphoreType.DMA((5,)), pltpu.SemaphoreType.DMA((6,))],
        compiler_params=pltpu.CompilerParams(vmem_limit_bytes=60 * 2**20),
        name="place_results",
    )(layer, grad, kinds, outer, lags)


def local(hidden_in, cotangent, norm_gain, in_weight, filter_taps, inner_taps, out_weight):
    tokens = hidden_in.shape[0] * lax.axis_size("tp")
    scale = (tokens * lax.axis_size("ctx")) ** (-0.5)
    gain = norm_gain.reshape(1, -1)
    kinds = jnp.transpose(in_weight, (1, 0, 2))
    layer_out, grad_input, grad_kinds, grad_out_weight, grad_filter, grad_inner = placed_results(
        *layer_results(hidden_in, cotangent, gain, filter_taps, inner_taps, kinds, out_weight, tokens, scale)
    )
    return (layer_out, grad_input, jnp.transpose(grad_kinds, (1, 0, 2)), grad_out_weight, grad_filter, grad_inner)


def solution(mesh):
    placed = (
        P(("ctx", "tp"), None),
        P(("ctx", "tp"), None),
        P(),
        P(None, None, "tp"),
        P(None, None, "tp"),
        P(None, "tp"),
        P("tp", None),
    )
    return jax.shard_map(
        local,
        mesh=mesh,
        in_specs=placed,
        out_specs=(
            P(("ctx", "tp"), None),
            P(("ctx", "tp"), None),
            P("ctx", None, "tp"),
            P("tp", "ctx"),
            P(None, None, "tp"),
            P(None, "tp"),
        ),
        check_vma=False,
    )
```

```python
import jax
import jax.numpy as jnp
from jax import lax
from jax.experimental import pallas as pl
from jax.experimental.pallas import tpu as pltpu
from jax.sharding import PartitionSpec as P

MESH = pl.DeviceIdType.MESH
DELTAS = (2, 1, 3, 0)


class Place:
    def __init__(self):
        ctx, tp = lax.axis_index("ctx"), lax.axis_index("tp")
        self.y, self.x_hi, self.core = ctx // 4, (ctx // 2) % 2, ctx % 2
        self.z, self.x_lo = tp // 2, tp % 2
        self.ctx, self.tp = ctx, tp

    def sibling(self):
        return (self.y * 4 + self.x_hi * 2 + 1 - self.core, self.tp)

    def along_y(self, step):
        return (((self.y + step) % 4) * 4 + self.x_hi * 2 + self.core, self.tp)

    def along_z(self, step):
        return (self.ctx, ((self.z + step) % 4) * 2 + self.x_lo)

    def along_x(self, step):
        x = (self.x_hi * 2 + self.x_lo + step) % 4
        return (self.y * 4 + (x // 2) * 2 + self.core, self.z * 2 + x % 2)

    def at(self, y, x, core):
        return (y * 4 + (x // 2) * 2 + core, self.z * 2 + x % 2)

    def partner(self):
        return self.along_x((1 - 2 * self.core) * (1 - 2 * self.x_lo))

    def last_block(self):
        x_hi, x_lo = self.x_hi, self.x_lo
        return jnp.where(self.core == 1, x_hi * x_lo + (1 - x_hi) * (1 - x_lo), x_hi)

    def following(self):
        x_hi, x_lo, core = self.x_hi, self.x_lo, self.core
        held = x_hi * x_lo + (1 - x_hi) * (1 - x_lo)
        x = (1 - core) * ((2 * x_hi + 3 * x_lo) % 4) + core * ((1 - held) * 2 + x_lo)
        return self.at((self.y + core * held) % 4, x, 1 - core)

    def preceding(self):
        x_hi, x_lo, core = self.x_hi, self.x_lo, self.core
        held = x_hi * (1 - x_lo) + (1 - x_hi) * x_lo
        x = core * (held * 2 + x_lo) + (1 - core) * (((1 - x_hi) * 2 + 2 - x_lo) % 4)
        return self.at((self.y - (1 - core) * (1 - x_hi)) % 4, x, 1 - core)

    def block(self, step, same):
        x_lo = self.x_lo if same else 1 - self.x_lo
        return ((self.z + step) % 4) * 2 + x_lo


def remote(source, target, send, recv, device):
    return pltpu.make_async_remote_copy(
        src_ref=source, dst_ref=target, send_sem=send, recv_sem=recv, device_id=device, device_id_type=MESH
    )


def tile(index, size):
    return pl.ds(pl.multiple_of(index * size, size), size)


def layer_kernel(
    scale, tokens,
    hidden_hbm, cot_hbm, gain_hbm, short_hbm, inner_hbm, in_w_hbm, out_w_hbm,
    layer_hbm, input_hbm, in_grad_hbm, out_grad_hbm, lag_hbm,
    hidden, cot, gain, short_taps, inner_taps, layer_ref, input_ref, in_grad_ref, out_grad_ref, lag_ref,
    both, out_w, proj, first_in, before_in, last_in, after_in, lags, acts, turned, part,
    sums_out, sums_in, y_out, y_in, pass_out, pass_in, x_out, x_in, tp_in, lag_sum, lag_got,
    load_sem, row_sem, result_sem, in_w_sem, send_sem, recv_sem, edge_send, edge_recv,
    sib_send, sib_recv, y_send, y_recv, x_send, x_recv, tp_send, tp_recv, lag_send, lag_recv,
):
    here = Place()
    block, width = hidden.shape
    chans = out_w_hbm.shape[0]
    cut = width // 16
    half = block // 2
    group = 2 * block
    wide, span = 72, 64
    steps = chans // 128
    bands = tokens // span
    step_in = 512
    x_cols = ((width // 128 * 15 // 16) * 128, (width // 128 // 2) * 128)
    bf16, f32 = jnp.bfloat16, jnp.float32

    out_load = pltpu.make_async_copy(out_w_hbm, out_w, load_sem.at[3])
    barrier = pltpu.get_barrier_semaphore()
    devices = [
        here.sibling(), here.along_y(1), here.along_y(-1), here.along_y(2), here.along_z(1), here.along_z(-1),
        here.along_x(1), here.along_x(-1), here.along_x(2), here.following(), here.preceding(),
    ]
    for device in devices:
        pl.semaphore_signal(barrier, inc=1, device_id=device, device_id_type=MESH)
    row_loads = [
        pltpu.make_async_copy(source, target, row_sem.at[index])
        for index, (source, target) in enumerate(
            ((hidden_hbm, hidden), (cot_hbm, cot), (gain_hbm, gain), (short_hbm, short_taps), (inner_hbm, inner_taps)))
    ]
    for copy in row_loads:
        copy.start()

    def result(index):
        source, target = (
            (layer_ref, layer_hbm), (input_ref, input_hbm), (in_grad_ref, in_grad_hbm),
            (out_grad_ref, out_grad_hbm), (lag_ref, lag_hbm),
        )[index]
        return pltpu.make_async_copy(source, target, result_sem.at[index])

    sends = {}

    def go(name, build):
        build().start()
        sends[name] = build

    def drained(name):
        sends.pop(name)().wait_send()


    def rows_of(step, same, begin=0, size=block):
        return pl.ds(pl.multiple_of(here.block(step, same) * block + begin, size), size)

    every = pl.ds(0, width)

    def slot_cols(which, slot):
        by_x = pl.ds(0, x_cols[which])
        by_z = pl.ds(x_cols[which], width - x_cols[which])
        return (every, every, every, by_z, by_z, every, every, every, by_x, by_x)[slot]

    def gather_copy(which, slot):
        rows, device = (
            lambda: (rows_of(0, True), here.partner()),
            lambda: (rows_of(0, True), here.along_z(1)),
            lambda: (rows_of(0, True), here.along_z(-1)),
            lambda: (rows_of(0, False), here.along_z(1)),
            lambda: (rows_of(0, False), here.along_z(-1)),
            lambda: (rows_of(-1, True, 0, half), here.along_z(1)),
            lambda: (rows_of(1, True, half, half), here.along_z(-1)),
            lambda: (rows_of(2, True), here.partner()),
            lambda: (rows_of(-1, True), here.partner()),
            lambda: (rows_of(1, True), here.partner()),
        )[slot]()
        held = both.at[which, rows, slot_cols(which, slot)]
        return remote(held, held, send_sem.at[which, slot], recv_sem.at[which, slot], device)

    def gather(which, slot):
        go(("gather", which, slot), lambda: gather_copy(which, slot))

    def arrived(which, slot):
        rows = (
            lambda: rows_of(0, False),
            lambda: rows_of(-1, True),
            lambda: rows_of(1, True),
            lambda: rows_of(-1, False),
            lambda: rows_of(1, False),
            lambda: rows_of(2, True, 0, half),
            lambda: rows_of(2, True, half, half),
            lambda: rows_of(2, False),
            lambda: rows_of(-1, False),
            lambda: rows_of(1, False),
        )[slot]()
        held = both.at[which, rows, slot_cols(which, slot)]
        remote(held, held, send_sem.at[which, slot], recv_sem.at[which, slot], here.partner()).wait_recv()


    parts = (part, out_w)

    def tp_copy(which, slot):
        source, held = parts[which], tp_in.at[which]
        first = pl.ds(0, half)
        second = pl.ds(half, half)
        rows, place, device = (
            lambda: (rows_of(2, False), held.at[0], here.partner()),
            lambda: (rows_of(1, False), held.at[1], here.along_z(1)),
            lambda: (rows_of(-1, False), held.at[2], here.along_z(-1)),
            lambda: (rows_of(2, True, 0, half), held.at[3, first], here.along_z(1)),
            lambda: (rows_of(2, True, half, half), held.at[3, second], here.along_z(-1)),
            lambda: (rows_of(1, True), held.at[4], here.along_z(1)),
            lambda: (rows_of(-1, True), held.at[5], here.along_z(-1)),
            lambda: (rows_of(0, False), held.at[6], here.partner()),
        )[slot]()
        return remote(source.at[rows], place, tp_send.at[which, slot], tp_recv.at[which, slot], device)

    def tp_go(which, slot):
        go(("tp", which, slot), lambda: tp_copy(which, slot))

    def add_rows(ref, base, length, others, size=128):
        def loop(index, carry):
            at = tile(index, size)
            rows = pl.ds(pl.multiple_of(base + index * size, size), size)
            total = ref[rows, :].astype(f32)
            for other in others:
                total = total + other[at, :].astype(f32)
            ref[rows, :] = total.astype(bf16)
            return carry

        lax.fori_loop(0, length // size, loop, 0)

    def tp_begin(which):
        for slot in range(3):
            tp_go(which, slot)

    def tp_halves(which):
        tp_copy(which, 0).wait_recv()
        add_rows(parts[which], here.block(2, True) * block, block, [tp_in.at[which, 0]], 16)
        tp_go(which, 3)
        tp_go(which, 4)

    def tp_direct(which):
        tp_copy(which, 3).wait_recv()
        add_rows(parts[which], here.block(1, True) * block, half, [tp_in.at[which, 3, pl.ds(0, half)]], 16)
        tp_go(which, 5)
        tp_copy(which, 4).wait_recv()
        add_rows(
            parts[which], here.block(-1, True) * block + half, half, [tp_in.at[which, 3, pl.ds(half, half)]], 16)
        tp_go(which, 6)

    def tp_last(which):
        tp_copy(which, 1).wait_recv()
        tp_copy(which, 2).wait_recv()
        add_rows(parts[which], here.block(0, False) * block, block, [tp_in.at[which, 1], tp_in.at[which, 2]], 16)
        tp_go(which, 7)

    def tp_total(which, index):
        at = tile(index, 16)
        rows = pl.ds(pl.multiple_of(here.tp * block + index * 16, 16), 16)
        total = parts[which][rows, :].astype(f32)
        for slot in (4, 5, 6):
            total = total + tp_in[which, slot, at, :].astype(f32)
        return at, total


    sums = (sums_out, sums_in)
    arriving = (y_out, y_in)
    passing = (pass_out, pass_in)
    crossing = (x_out, x_in)

    def halves(kind):
        size = sums[kind].shape[1] // 2
        return pl.ds(0, size), pl.ds(size, size), size

    def target(index, core):
        y = (here.y + DELTAS[index % 4]) % 4
        x_hi = 1 - here.x_hi if index < 4 else here.x_hi
        return y * 4 + x_hi * 2 + core

    def product(kind, index, core, write):
        cols = tile(target(index, core), cut)

        def one(step, carry):
            rows = tile(step, chans)
            first = 3 * chans if kind == 0 else 0
            left = turned[pl.ds(pl.multiple_of(first + step * chans, chans), chans), :]
            value = jnp.dot(left, both[1 - kind, :, cols], preferred_element_type=f32)
            write(rows, value * scale)
            return carry

        lax.fori_loop(0, (1, 3)[kind], one, 0)

    def sib_copy(kind, sib, index):
        return remote(
            sib.at[index % 4], sums[kind].at[index], sib_send.at[kind, index], sib_recv.at[kind, index],
            here.sibling())

    def for_sibling(kind, sib, index):
        if index >= 4:
            drained(("sib", kind, index - 4))

        def write(rows, value):
            sib[index % 4, rows, :] = value.astype(bf16)

        product(kind, index, 1 - here.core, write)
        go(("sib", kind, index), lambda: sib_copy(kind, sib, index))

    def for_self(kind, sib, index):
        sib_copy(kind, sib, index).wait_recv()

        def write(rows, value):
            held = sums[kind][index, rows, :].astype(f32)
            sums[kind][index, rows, :] = (held + value).astype(bf16)

        product(kind, index, here.core, write)

    def y_copy(kind, far, slot):
        upper, lower, _ = halves(kind)
        index, rows, step = (
            (0, upper, 1), (0, lower, -1), (1, lower, 1), (2, upper, -1), (1, upper, 1), (2, lower, -1)
        )[slot]
        return remote(
            sums[kind].at[far * 4 + index, rows], arriving[kind].at[far, slot],
            y_send.at[kind, far, slot], y_recv.at[kind, far, slot], here.along_y(step),
        )

    def y_go(kind, far, slot):
        go(("y", kind, far, slot), lambda: y_copy(kind, far, slot))

    def y_pass(kind, far):
        size = halves(kind)[2]
        y_copy(kind, far, 0).wait_recv()
        add_rows(sums[kind].at[far * 4 + 1], 0, size, [arriving[kind].at[far, 0]])
        y_go(kind, far, 4)
        y_copy(kind, far, 1).wait_recv()
        add_rows(sums[kind].at[far * 4 + 2], size, size, [arriving[kind].at[far, 1]])
        y_go(kind, far, 5)

    def y_done(kind, far):
        for slot in (3, 4, 2, 5):
            y_copy(kind, far, slot).wait_recv()

    def x_copy(kind, side):
        rows = halves(kind)[side]
        return remote(
            sums[kind].at[3, rows], passing[kind].at[side], x_send.at[kind, side], x_recv.at[kind, side],
            here.along_x((1, -1)[side]))

    def x_forward(kind, side):
        return remote(
            passing[kind].at[side], crossing[kind].at[side], x_send.at[kind, 2 + side], x_recv.at[kind, 2 + side],
            here.along_x((1, -1)[side]))

    def x_begin(kind):
        size = halves(kind)[2]
        y_done(kind, 0)
        add_rows(sums[kind].at[3], 0, size, [arriving[kind].at[0, 3], arriving[kind].at[0, 4]])
        go(("x", kind, 0), lambda: x_copy(kind, 0))
        add_rows(sums[kind].at[3], size, size, [arriving[kind].at[0, 2], arriving[kind].at[0, 5]])
        go(("x", kind, 1), lambda: x_copy(kind, 1))

    def x_go(kind, side):
        go(("x", kind, 2 + side), lambda: x_forward(kind, side))

    def x_on(kind):
        for side in range(2):
            x_copy(kind, side).wait_recv()
            x_go(kind, side)

    def last(kind, side):
        size = halves(kind)[2]
        begin = side * size
        others = [arriving[kind].at[1, slot] for slot in ((3, 4), (2, 5))[side]] + [crossing[kind].at[side]]
        for index in range(size // 128):
            row = begin + index * 128
            total = sums[kind][7, pl.ds(row, 128), :].astype(f32)
            for other in others:
                total = total + other[pl.ds(index * 128, 128), :].astype(f32)
            if kind == 1:
                in_grad_ref[row // chans, :, pl.ds(row % chans, 128)] = total.T.astype(bf16)
            else:
                out_grad_ref[pl.ds(row, 128), :] = total.astype(bf16)

    def lag_copy(step):
        device = (
            lambda: here.sibling(),
            lambda: here.along_x(2),
            lambda: here.along_y(1 - 2 * (here.y % 2)),
            lambda: here.along_y(2),
        )[step]()
        return remote(lag_sum.at[step], lag_got.at[step], lag_send.at[step], lag_recv.at[step], device)

    def lag_step(step):
        lag_copy(step).wait_recv()
        total = lag_sum[step] + lag_got[step]
        if step < 3:
            lag_sum[step + 1] = total
            go(("lag", step + 1), lambda: lag_copy(step + 1))
        else:
            lag_ref[...] = total

    def gather_phase(in_w):
        loads = [pltpu.make_async_copy(in_w_hbm.at[kind], in_w.at[kind], load_sem.at[kind]) for kind in range(3)]
        for copy in loads:
            copy.start()
        out_load.start()
        for copy in row_loads:
            copy.wait()

        def normalise(index, carry):
            at = tile(index, 16)
            rows = pl.ds(pl.multiple_of(here.tp * block + index * 16, 16), 16)
            floats = hidden[at, :].astype(f32)
            factor = lax.rsqrt(jnp.mean(floats * floats, axis=-1, keepdims=True) + 1e-05)
            both[0, rows, :] = (floats * factor * gain[...]).astype(bf16)
            both[1, rows, :] = cot[at, :]
            return carry

        lax.fori_loop(0, block // 16, normalise, 0)
        pl.semaphore_wait(barrier, len(devices))

        def project(step):
            begin = ((here.z + step) % 4) * group

            def loop(kind, carry):
                value = jnp.dot(
                    both[0, pl.ds(pl.multiple_of(begin, group), group), :], in_w[kind], preferred_element_type=f32
                )
                value = value.astype(bf16).astype(f32)
                for index in range(2):
                    first = (begin // block + index) * wide + 8
                    proj[kind, pl.ds(pl.multiple_of(first, 8), block), :] = value[index * block : (index + 1) * block]
                return carry

            lax.fori_loop(0, 3, loop, 0)

        for slot in range(3):
            gather(0, slot)
        gather(1, 0)
        arrived(0, 1)
        gather(0, 5)
        gather(0, 8)
        arrived(0, 2)
        gather(0, 6)
        gather(0, 9)
        arrived(0, 0)
        gather(0, 3)
        gather(0, 4)
        for copy in loads:
            copy.wait()
        project(0)
        arrived(0, 5)
        arrived(0, 6)
        gather(0, 7)
        gather(1, 1)
        gather(1, 2)
        arrived(0, 3)
        arrived(0, 8)
        project(-1)
        arrived(0, 4)
        arrived(0, 9)
        project(1)
        arrived(0, 7)
        project(2)

    def filter_phase(query, gates, prods, grads, ends, heads, sib):
        def first_copy():
            return remote(
                proj.at[:, pl.ds(7 * wide + span, 8), :], first_in, edge_send.at[0], edge_recv.at[0], here.following())

        def before_copy():
            return remote(ends, before_in, edge_send.at[1], edge_recv.at[1], here.along_x(2))

        def last_copy(which):
            kinds = pl.ds((0, 2)[which], 2)
            return remote(
                grads.at[kinds, pl.ds(0, 8), :], last_in.at[kinds], edge_send.at[2 + which], edge_recv.at[2 + which],
                here.preceding())

        def after_copy(which):
            kinds = pl.ds((0, 2)[which], 2)
            return remote(
                heads.at[kinds], after_in.at[kinds], edge_send.at[4 + which], edge_recv.at[4 + which],
                here.along_x(2))

        def edge_rows(target, kinds, source, offset):
            for kind in kinds:
                for pair in range(4):
                    rows = [source[kind, pl.ds((2 * pair + index) * wide + offset, 8), :] for index in range(2)]
                    target[kind, pl.ds(pair * 16, 16), :] = jnp.concatenate(rows).astype(bf16)

        def share(target, kinds, copy, source):
            @pl.when(here.core == 1)
            def _():
                copy().wait_recv()

            @pl.when(here.core == 0)
            def _():
                for kind in kinds:
                    target[kind] = source[kind]

        edge_rows(ends, range(3), proj, span)
        go(("edge", 0), first_copy)

        @pl.when(here.core == 1)
        def _():
            before_copy().start()

        arrived(1, 1)
        gather(1, 5)
        gather(1, 8)
        arrived(1, 2)
        gather(1, 6)
        gather(1, 9)
        arrived(1, 0)
        arrived(1, 5)
        arrived(1, 6)
        gather(1, 7)
        gather(1, 3)
        gather(1, 4)
        first_copy().wait_recv()
        share(before_in, range(3), before_copy, ends)
        for kind in range(3):
            proj[kind, pl.ds(0, 8), :] = first_in[kind] * jnp.where(here.ctx == 0, 0.0, 1.0).astype(f32)
            for pair in range(4):
                rows = before_in[kind, pl.ds(pair * 16, 16), :].astype(f32)
                proj[kind, pl.ds((2 * pair + 1) * wide, 8), :] = rows[:8]
                if pair < 3:
                    proj[kind, pl.ds((2 * pair + 2) * wide, 8), :] = rows[8:]

        def short(lag, kind, cols):
            return short_taps[lag, pl.ds(kind, 1), cols]

        def inner(lag, cols):
            return inner_taps[pl.ds(lag, 1), cols]

        def behind(value, count):
            return pltpu.roll(value, count, 0)

        def ahead(value, count):
            return pltpu.roll(value, wide - count, 0)

        def forward(index, carry):
            begin = pl.multiple_of((index // steps) * span, span)
            first = pl.multiple_of((index // steps) * wide, 8)
            cols = tile(index % steps, 128)
            feats = []
            for kind in range(3):
                held = proj[kind, pl.ds(first, wide), cols]
                total = short(0, kind, cols) * held
                for lag in (1, 2):
                    total = total + short(lag, kind, cols) * behind(held, lag)
                feats.append(total)
            product = feats[1] * feats[2]
            total = inner(0, cols) * product
            for lag in range(1, 7):
                total = total + inner(lag, cols) * behind(product, lag)
            rows = pl.ds(begin, span)
            query[rows, cols] = feats[0][8:]
            grads[3, pl.ds(first, span), cols] = feats[1][8:]
            grads[2, pl.ds(first, span), cols] = feats[2][8:]
            gates[rows, cols] = total[8:]
            prods[rows, cols] = product[8:]
            acts[rows, tile(3 * steps + index % steps, 128)] = (feats[0][8:] * total[8:]).astype(bf16)
            return carry

        lax.fori_loop(0, bands * steps, forward, 0)
        edge_rows(heads, (2, 3), grads, 0)
        go(("edge", 3), lambda: last_copy(1))

        @pl.when(here.core == 1)
        def _():
            after_copy(1).start()

        lags[...] = jnp.zeros_like(lags)

        def turn(index, carry):
            turned[tile(index, 128), :] = acts[:, tile(index, 128)].T
            return carry

        lax.fori_loop(3 * steps, 4 * steps, turn, 0)
        out_load.wait()

        def branch_product(index, carry):
            cols = tile(index, chans)
            value = jnp.dot(acts[:, pl.ds(3 * chans, chans)], out_w[:, cols], preferred_element_type=f32)
            part[:, cols] = value.astype(bf16)
            return carry

        for slot in (3, 4, 7, 8, 9):
            arrived(1, slot)
        for_sibling(0, sib, 0)
        for_sibling(0, sib, 1)
        for_sibling(0, sib, 2)
        for_self(0, sib, 0)
        y_go(0, 0, 0)
        y_go(0, 0, 1)
        for_sibling(0, sib, 3)
        for_self(0, sib, 1)
        y_go(0, 0, 2)
        for_self(0, sib, 2)
        y_go(0, 0, 3)
        lax.fori_loop(0, width // chans, branch_product, 0)
        tp_begin(0)
        value = lax.dot_general(both[1], out_w[...], (((1,), (1,)), ((), ())), preferred_element_type=f32)
        for index in range(8):
            rows = pl.ds(index * span, span)
            grads[0, pl.ds(index * wide, span), :] = value[index * span : (index + 1) * span] * query[rows, :]
            grads[1, pl.ds(index * wide, span), :] = value[index * span : (index + 1) * span] * gates[rows, :]
        edge_rows(heads, (0, 1), grads, 0)
        go(("edge", 2), lambda: last_copy(0))

        @pl.when(here.core == 1)
        def _():
            after_copy(0).start()

        y_pass(0, 0)
        for index in range(4, 8):
            for_sibling(0, sib, index)
            for_self(0, sib, index - 1)
            if index == 5:
                y_go(0, 1, 0)
                y_go(0, 1, 1)
            if index == 6:
                y_go(0, 1, 2)
            if index == 7:
                y_go(0, 1, 3)
        for_self(0, sib, 7)
        for which in range(2):
            last_copy(which).wait_recv()
            share(after_in, ((0, 1), (2, 3))[which], lambda which=which: after_copy(which), heads)
        ended = (here.core == 1) & (here.y == 3) & (here.last_block() == 1)
        for kind in range(4):
            kept = jnp.where(ended, 0.0, 1.0).astype(f32) if kind < 2 else 1.0
            grads[kind, pl.ds(7 * wide + span, 8), :] = last_in[kind] * kept
            for pair in range(4):
                rows = after_in[kind, pl.ds(pair * 16, 16), :].astype(f32)
                if pair > 0:
                    grads[kind, pl.ds((2 * pair - 1) * wide + span, 8), :] = rows[:8]
                grads[kind, pl.ds(2 * pair * wide + span, 8), :] = rows[8:]

        def turn_tile(index):
            rows = tile(index // steps, 128)
            for kind in range(3):
                cols = tile(kind * steps + index % steps, 128)
                turned[cols, rows] = acts[rows, cols].T

        def backward(index, carry):
            turn_tile(jnp.maximum(index - 1, 0))
            for part_of in range(2):
                backward_band((index // steps) * 2 + part_of, index % steps)
            return carry

        def backward_band(band, column):
            begin = pl.multiple_of(band * span, span)
            first = pl.multiple_of(band * wide, 8)
            cols = tile(column, 128)
            rows = pl.ds(first, wide)
            here_rows = pl.ds(begin, span)

            def add_lag(row, value):
                lags[row, :, cols] += jnp.sum(value.reshape(span // 8, 8, 128), axis=0)

            gated = grads[0, rows, cols]
            product = prods[here_rows, cols]
            total = inner(0, cols) * gated
            add_lag(9, gated[:span] * product)
            for lag in range(1, 7):
                moved = ahead(gated, lag)
                total = total + inner(lag, cols) * moved
                add_lag(9 + lag, moved[:span] * product)
            feats = (grads[1, rows, cols], total * grads[2, rows, cols], total * grads[3, rows, cols])
            for kind in range(3):
                feat = feats[kind]
                held = proj[kind, pl.ds(pl.multiple_of(first + 8, 8), span), cols]
                summed = short(0, kind, cols) * feat[:span]
                add_lag(kind, feat[:span] * held)
                for lag in (1, 2):
                    moved = ahead(feat, lag)[:span]
                    summed = summed + short(lag, kind, cols) * moved
                    add_lag(lag * 3 + kind, moved * held)
                acts[here_rows, tile(kind * steps + column, 128)] = summed.astype(bf16)

        tiles = (bands // 2) * steps
        lax.fori_loop(0, tiles - steps, backward, 0)
        y_pass(0, 1)
        lax.fori_loop(tiles - steps, tiles, backward, 0)
        turn_tile(tiles - 1)
        lag_sum[0] = jnp.sum(lags[...], axis=1) * scale
        go(("lag", 0), lambda: lag_copy(0))
        x_begin(0)
        for index in (0, 2, 3):
            drained(("edge", index))

        @pl.when(here.core == 1)
        def _():
            before_copy().wait_send()
            after_copy(0).wait_send()
            after_copy(1).wait_send()

        for index in range(4, 8):
            drained(("sib", 0, index))

    def reduce_phase(in_w, sib):
        def in_loads(step, slot):
            return [
                pltpu.make_async_copy(
                    in_w_hbm.at[kind, tile(step, step_in), :], in_w.at[slot, :, pl.ds(kind * chans, chans)],
                    in_w_sem.at[slot, kind])
                for kind in range(3)
            ]

        for step in range(2):
            for copy in in_loads(step, step):
                copy.start()

        def gnorm_product(first, count):
            def loop(step, carry):
                slot = step % 2
                for copy in in_loads(step, slot):
                    copy.wait()
                value = lax.dot_general(
                    acts[:, pl.ds(0, 3 * chans)], in_w[slot], (((1,), (1,)), ((), ())), preferred_element_type=f32)
                out_w[:, tile(step, step_in)] = value.astype(bf16)

                @pl.when(step + 2 < width // step_in)
                def _():
                    for copy in in_loads(step + 2, slot):
                        copy.start()

                return carry

            lax.fori_loop(first, first + count, loop, 0)

        for_sibling(1, sib, 0)
        for_sibling(1, sib, 1)
        for_self(1, sib, 0)
        y_go(1, 0, 0)
        y_go(1, 0, 1)
        tp_halves(0)
        tp_last(0)
        for_sibling(1, sib, 2)
        for_self(1, sib, 1)
        y_go(1, 0, 2)
        for_sibling(1, sib, 3)
        for_self(1, sib, 2)
        y_go(1, 0, 3)
        lag_step(0)
        x_on(0)
        tp_direct(0)
        in_steps = width // step_in
        gnorm_product(0, in_steps // 2)
        y_pass(1, 0)
        gnorm_product(in_steps // 2, in_steps // 2)
        tp_begin(1)
        for_sibling(1, sib, 4)
        for_sibling(1, sib, 5)
        for_self(1, sib, 4)
        y_go(1, 1, 0)
        y_go(1, 1, 1)
        lag_step(1)
        for_sibling(1, sib, 6)
        for_self(1, sib, 5)
        y_go(1, 1, 2)
        for_sibling(1, sib, 7)
        for_self(1, sib, 6)
        y_go(1, 1, 3)
        for_self(1, sib, 3)
        for_self(1, sib, 7)
        tp_halves(1)
        tp_last(1)
        lag_step(2)
        x_begin(1)
        for slot in (5, 6, 7):
            tp_copy(0, slot).wait_recv()

        def layer_finish(index, carry):
            at, total = tp_total(0, index)
            layer_ref[at, :] = (hidden[at, :].astype(f32) + total).astype(bf16)
            return carry

        lax.fori_loop(0, block // 16, layer_finish, 0)
        result(0).start()
        tp_direct(1)
        for side in range(2):
            x_forward(0, side).wait_recv()
        y_done(0, 1)
        last(0, 0)
        last(0, 1)
        result(3).start()
        lag_step(3)
        result(4).start()
        y_pass(1, 1)
        x_on(1)
        for slot in (5, 6, 7):
            tp_copy(1, slot).wait_recv()

        def input_finish(index, carry):
            at, total = tp_total(1, index)
            floats = hidden[at, :].astype(f32)
            factor = lax.rsqrt(jnp.mean(floats * floats, axis=-1, keepdims=True) + 1e-05)
            gained = total * gain[...]
            inner = jnp.mean(floats * gained, axis=-1, keepdims=True) * factor * factor * factor
            input_ref[at, :] = (cot[at, :].astype(f32) + gained * factor - floats * inner).astype(bf16)
            return carry

        lax.fori_loop(0, block // 16, input_finish, 0)
        result(1).start()
        for side in range(2):
            x_forward(1, side).wait_recv()
        y_done(1, 1)
        last(1, 0)
        last(1, 1)
        result(2).start()
        for name in list(sends):
            drained(name)
        for index in range(5):
            result(index).wait()

    pl.run_scoped(gather_phase, pltpu.VMEM((3, width, chans), bf16))
    pl.run_scoped(
        filter_phase,
        pltpu.VMEM((tokens, chans), f32),
        pltpu.VMEM((tokens, chans), f32),
        pltpu.VMEM((tokens, chans), f32),
        pltpu.VMEM((4, bands * wide, chans), f32),
        pltpu.VMEM((3, bands * 8, chans), bf16),
        pltpu.VMEM((4, bands * 8, chans), bf16),
        pltpu.VMEM((4, chans, cut), bf16),
    )
    pl.run_scoped(
        reduce_phase, pltpu.VMEM((2, step_in, 3 * chans), bf16), pltpu.VMEM((4, 3 * chans, cut), bf16)
    )


def layer_results(hidden, cot, gain, short_taps, inner_taps, in_weight, out_weight, tokens, scale):
    block, width = hidden.shape
    chans = out_weight.shape[0]
    cut = width // 16
    any_space = pl.BlockSpec(memory_space=pl.ANY)
    bf16, f32 = jnp.bfloat16, jnp.float32
    dma = pltpu.SemaphoreType.DMA
    body = lambda *refs: layer_kernel(scale, tokens, *refs)
    return pl.pallas_call(
        body,
        out_shape=(
            jax.ShapeDtypeStruct((block, width), bf16),
            jax.ShapeDtypeStruct((block, width), bf16),
            jax.ShapeDtypeStruct((3, cut, chans), bf16),
            jax.ShapeDtypeStruct((chans, cut), bf16),
            jax.ShapeDtypeStruct((16, chans), f32),
        ),
        in_specs=[any_space] * 7,
        out_specs=(any_space,) * 5,
        scratch_shapes=[
            pltpu.VMEM(hidden.shape, bf16),
            pltpu.VMEM(cot.shape, bf16),
            pltpu.VMEM(gain.shape, f32),
            pltpu.VMEM(short_taps.shape, f32),
            pltpu.VMEM(inner_taps.shape, f32),
            pltpu.VMEM((block, width), bf16),
            pltpu.VMEM((block, width), bf16),
            pltpu.VMEM((3, cut, chans), bf16),
            pltpu.VMEM((chans, cut), bf16),
            pltpu.VMEM((16, chans), f32),
            pltpu.VMEM((2, tokens, width), bf16),
            pltpu.VMEM(out_weight.shape, bf16),
            pltpu.VMEM((3, tokens + 64, chans), f32),
            pltpu.VMEM((3, 8, chans), f32),
            pltpu.VMEM((3, 64, chans), bf16),
            pltpu.VMEM((4, 8, chans), f32),
            pltpu.VMEM((4, 64, chans), bf16),
            pltpu.VMEM((16, 8, chans), f32),
            pltpu.VMEM((tokens, 4 * chans), bf16),
            pltpu.VMEM((4 * chans, tokens), bf16),
            pltpu.VMEM((tokens, width), bf16),
            pltpu.VMEM((8, chans, cut), bf16),
            pltpu.VMEM((8, 3 * chans, cut), bf16),
            pltpu.VMEM((2, 6, chans // 2, cut), bf16),
            pltpu.VMEM((2, 6, 3 * chans // 2, cut), bf16),
            pltpu.VMEM((2, chans // 2, cut), bf16),
            pltpu.VMEM((2, 3 * chans // 2, cut), bf16),
            pltpu.VMEM((2, chans // 2, cut), bf16),
            pltpu.VMEM((2, 3 * chans // 2, cut), bf16),
            pltpu.VMEM((2, 7, block, width), bf16),
            pltpu.VMEM((4, 16, chans), f32),
            pltpu.VMEM((4, 16, chans), f32),
            dma((4,)), dma((5,)), dma((5,)), dma((2, 3)), dma((2, 10)), dma((2, 10)), dma((6,)), dma((6,)),
            dma((2, 8)), dma((2, 8)), dma((2, 2, 6)), dma((2, 2, 6)), dma((2, 4)), dma((2, 4)),
            dma((2, 8)), dma((2, 8)), dma((4,)), dma((4,)),
        ],
        compiler_params=pltpu.CompilerParams(
            collective_id=0, has_side_effects=True, vmem_limit_bytes=63 * 2**20
        ),
        name="whole_layer",
    )(hidden, cot, gain, short_taps, inner_taps, in_weight, out_weight)


def place_kernel(
    layer, grad, kinds, outer, lags, layer_to, grad_to, kinds_to, outer_to, short_to, inner_to,
    layer_at, grad_at, kinds_at, outer_at, lags_at, short_at, inner_at, read_sems, write_sems,
):
    ends = (
        (lags, lags_at, None), (kinds, kinds_at, kinds_to), (layer, layer_at, layer_to), (grad, grad_at, grad_to),
        (outer, outer_at, outer_to), (None, short_at, short_to), (None, inner_at, inner_to),
    )
    reads = [pltpu.make_async_copy(ends[index][0], ends[index][1], read_sems.at[index]) for index in range(5)]
    writes = [pltpu.make_async_copy(ends[index][1], ends[index][2], write_sems.at[index - 1]) for index in range(1, 7)]
    for copy in reads:
        copy.start()
    reads[0].wait()
    for lag in range(3):
        short_at[lag] = lags_at[pl.ds(3 * lag, 3), :]
    inner_at[...] = lags_at[pl.ds(9, 7), :]
    writes[4].start()
    writes[5].start()
    for index in range(4):
        reads[index + 1].wait()
        writes[index].start()
    for copy in writes:
        copy.wait()


def placed_results(layer, grad, kinds, outer, lags):
    chans = lags.shape[1]
    any_space = pl.BlockSpec(memory_space=pl.ANY)
    arrays = (layer, grad, kinds, outer)
    ends = ((3, 3, chans), (7, chans))
    return pl.pallas_call(
        place_kernel,
        out_shape=tuple(jax.ShapeDtypeStruct(array.shape, array.dtype) for array in arrays)
        + tuple(jax.ShapeDtypeStruct(shape, jnp.float32) for shape in ends),
        in_specs=[any_space] * 5,
        out_specs=(any_space,) * 6,
        scratch_shapes=[pltpu.VMEM(array.shape, array.dtype) for array in (*arrays, lags)]
        + [pltpu.VMEM(shape, jnp.float32) for shape in ends]
        + [pltpu.SemaphoreType.DMA((5,)), pltpu.SemaphoreType.DMA((6,))],
        compiler_params=pltpu.CompilerParams(vmem_limit_bytes=60 * 2**20),
        name="place_results",
    )(layer, grad, kinds, outer, lags)


def local(hidden_in, cotangent, norm_gain, in_weight, filter_taps, inner_taps, out_weight):
    tokens = hidden_in.shape[0] * lax.axis_size("tp")
    scale = (tokens * lax.axis_size("ctx")) ** (-0.5)
    gain = norm_gain.reshape(1, -1)
    kinds = jnp.transpose(in_weight, (1, 0, 2))
    layer_out, grad_input, grad_kinds, grad_out_weight, grad_filter, grad_inner = placed_results(
        *layer_results(hidden_in, cotangent, gain, filter_taps, inner_taps, kinds, out_weight, tokens, scale)
    )
    return (layer_out, grad_input, jnp.transpose(grad_kinds, (1, 0, 2)), grad_out_weight, grad_filter, grad_inner)


def solution(mesh):
    placed = (
        P(("ctx", "tp"), None),
        P(("ctx", "tp"), None),
        P(),
        P(None, None, "tp"),
        P(None, None, "tp"),
        P(None, "tp"),
        P("tp", None),
    )
    return jax.shard_map(
        local,
        mesh=mesh,
        in_specs=placed,
        out_specs=(
            P(("ctx", "tp"), None),
            P(("ctx", "tp"), None),
            P("ctx", None, "tp"),
            P("tp", "ctx"),
            P(None, None, "tp"),
            P(None, "tp"),
        ),
        check_vma=False,
    )
```
